512 devices in a mesh: gy: 32 (over z_lo, y), gx: 4 (over x), gz: 4 (over z_hi, core).
Axes of the slice: x: 4, y: 4, z: 16 (z_hi: 2, z_lo: 8; z = z_hi * 8 + z_lo), core: 2. Of those that a mesh axis runs over, the one named last changes fastest.
Arguments:
- wall: bfloat16 [3, 1024, 768], P(None, ('gy', 'gx'), 'gz'), may hold values from -6 to 6
- kernel: bfloat16 [2, 3, 3, 32, 768, 1024], P(None, None, None, 'gy', 'gz', 'gx'), may hold values from -3 to 3
Outputs:
- estimate: bfloat16 [3, 32, 768, 1024], P(None, 'gy', 'gz', 'gx')
The draws below stay inside these ranges and needn't reach their ends.
All inputs are finite; a program needn't handle non-finite values.
Results may differ from the reference program's by a relative error of at most 0.025.
Values may be sent and summed in bfloat16 or wider, within the bound.
No kernel may reach another device: no remote copies, remote signals or barrier semaphores. Data moves between devices by JAX's collectives and lax.ppermute only.
A program may use at most 64 MiB of HBM per device.

```python
import math
import jax
import jax.numpy as jnp
from jax import lax

NX = 1024
NZ = 768
LEVELS = 32


def levels(rng, shape, shards, least, top_value):
    factor_of = 1.0
    for position, blocks in shards:
        draws = jax.random.uniform(jax.random.fold_in(jax.random.fold_in(rng, 6), position), (blocks,), jnp.float32, least / len(shards), top_value / len(shards))
        factor_of = factor_of * jnp.repeat(jnp.exp(draws), shape[position] // blocks).reshape((-1,) + (1,) * (len(shape) - 1 - position))
    return factor_of


def normal_values(own_key, dims, scale, reach, pieces=(), kind=jnp.bfloat16):
    loudness = levels(own_key, dims, pieces, -0.22, 0.18) if pieces else 1.0
    entries = jax.random.normal(own_key, dims, jnp.float32) * scale * loudness
    return jnp.minimum(jnp.maximum(entries, -reach), reach).astype(kind)


def setup_inputs(seed: int = 0) -> dict:
    key_of = jax.random.split(jax.random.key(seed), 3)
    wall = normal_values(key_of[0], (3, NX, NZ), 1.0, 6.0, ((1, 128), (2, 4)))
    kernel = normal_values(key_of[1], (2, 3, 3, LEVELS, NZ, NX), 0.5, 3.0, ((3, 32), (4, 4), (5, 4)))
    return {"wall": wall, "kernel": kernel}


def rounded(values):
    return lax.optimization_barrier(values.astype(jnp.bfloat16)).astype(jnp.float32)

def reference(wall, kernel):
    wall_values = wall.astype(jnp.float32)
    along_z = jnp.fft.fft(wall_values, axis=2) / math.sqrt(NZ)
    z_real = rounded(jnp.real(along_z))
    z_imag = rounded(jnp.imag(along_z))
    along_x = jnp.fft.fft(lax.complex(z_real, z_imag), axis=1) / math.sqrt(NX)
    spec_real = rounded(jnp.real(along_x))
    spec_imag = rounded(jnp.imag(along_x))

    def one_level(level):
        slab = lax.dynamic_index_in_dim(kernel, level, axis=3, keepdims=False).astype(jnp.float32)
        slab = jnp.swapaxes(slab, -1, -2)
        mode_real = rounded(lax.optimization_barrier(jnp.sum(slab[0] * spec_real[None] - slab[1] * spec_imag[None], axis=1)))
        mode_imag = rounded(lax.optimization_barrier(jnp.sum(slab[0] * spec_imag[None] + slab[1] * spec_real[None], axis=1)))
        inner = jnp.fft.ifft(lax.complex(mode_real, mode_imag), axis=2) * math.sqrt(NZ)
        column_real = rounded(jnp.real(inner))
        column_imag = rounded(jnp.imag(inner))
        outer = jnp.fft.ifft(lax.complex(column_real, column_imag), axis=1) * math.sqrt(NX)
        return jnp.swapaxes(jnp.real(outer), -1, -2).astype(jnp.bfloat16)
    stacked = lax.map(one_level, jnp.arange(LEVELS, dtype=jnp.int32))
    return jnp.transpose(stacked, (1, 0, 2, 3))
```

```python
import functools
import math

import jax
import jax.numpy as jnp
import numpy as np
from jax import lax
from jax.experimental import pallas as pl
from jax.experimental.pallas import tpu as pltpu
from jax.sharding import Mesh, PartitionSpec as P

NX = 1024
NZ = 768
NQ = 192
NP = 256
VMEM = 40 * 1024 * 1024


def angle(left, right, length):
    phase = (left[:, None].astype(np.int64) * right[None, :].astype(np.int64)) % length
    return phase * (2.0 * math.pi / length)


def forward_z_table():
    q = np.arange(NQ)
    theta = angle(q, q, NZ)
    both = np.stack([np.cos(theta), np.sin(theta)])
    main, tail = both[..., :128], both[..., 128:]
    zero = np.zeros_like(tail)
    return np.concatenate([tail, zero, main, zero, tail], axis=-1).astype(jnp.bfloat16)


def forward_x_table():
    y, source, low, r = np.meshgrid(
        np.arange(4), np.arange(4), np.arange(8), np.arange(8), indexing="ij"
    )
    x = (8 * (4 * (low * 4 + y) + source) + r).reshape(-1)
    theta = angle(x, np.arange(NP), NX).reshape(16, 64, NP)
    cos, sin = np.cos(theta), np.sin(theta)
    from_real = np.concatenate([cos, -sin], axis=2)
    from_imag = np.concatenate([sin, cos], axis=2)
    both = np.concatenate([from_real, from_imag], axis=1)
    return both.reshape(8, 256, 512).astype(jnp.bfloat16)


def inverse_x_table():
    theta = angle(np.arange(NX), np.arange(NX), NX).reshape(NX, 8, 128)
    both = np.concatenate([np.cos(theta), np.sin(theta)], axis=2)
    return np.transpose(both, (1, 0, 2)).astype(jnp.bfloat16)


def inverse_z_table():
    q = (
        48 * np.arange(4)[:, None, None]
        + 192 * np.arange(2)[None, :, None]
        + np.arange(48)[None, None, :]
    ).reshape(-1)
    theta = angle(np.arange(NZ), q, NZ).reshape(NZ, 8, 48)
    both = np.stack([np.cos(theta), -np.sin(theta)], axis=2)
    return both.reshape(4, NQ, NZ).astype(jnp.bfloat16)


def pack_body(wall_ref, table_ref, out_ref, kept_ref):
    kept_ref[...] = table_ref[...]
    rows = [wall_ref[c].astype(jnp.float32) for c in range(3)]
    tails = [row[:, 128:] for row in rows] + [jnp.zeros((8, 64), jnp.float32)]
    pieces = [row[:, :128] for row in rows]
    for c in range(0, 4, 2):
        pieces.append(jnp.concatenate(tails[c : c + 2], axis=1))
    packed = jnp.concatenate(pieces, axis=0).astype(jnp.bfloat16)
    for k in range(16):
        out_ref[k] = packed


def pack_call(wall, table):
    return pl.pallas_call(
        pack_body,
        out_shape=[
            jax.ShapeDtypeStruct((16, 40, 128), jnp.bfloat16),
            jax.ShapeDtypeStruct((2, NQ, 384), jnp.bfloat16),
        ],
        compiler_params=pltpu.CompilerParams(vmem_limit_bytes=VMEM),
        cost_estimate=pl.CostEstimate(flops=10000, bytes_accessed=180000, transcendentals=0),
        name="pack",
    )(wall, table)


def turned_lanes(values, turn):
    lane = lax.broadcasted_iota(jnp.int32, values.shape, 1)
    keep = jnp.where(turn == 0, 1.0, jnp.where(turn == 2, -1.0, 0.0))
    swap = jnp.where(turn == 1, 1.0, jnp.where(turn == 3, -1.0, 0.0))
    swap = jnp.where(lane < 64, swap, -swap)
    return values * keep + pltpu.roll(values, 64, axis=1) * swap


def partial_z(me, rows_ref, table_ref, step, c):
    turn = (me * lax.broadcasted_iota(jnp.int32, (64, 256), 1)) % 4
    to_real = jnp.where(turn == 0, 1.0, jnp.where(turn == 2, -1.0, 0.0))
    to_imag = jnp.where(turn == 3, 1.0, jnp.where(turn == 1, -1.0, 0.0))
    row = lax.broadcasted_iota(jnp.int32, (NQ, 128), 0)
    core = me % 2
    result = None
    for high in range(2):
        position = high * 2 + (core if step == 0 else 1 - core)
        blocks = [rows_ref[low * 2 + high].astype(jnp.float32) for low in range(8)]
        main = jnp.concatenate([block[c * 8 : c * 8 + 8] for block in blocks], axis=0)
        start = 24 + (c // 2) * 8
        tail = jnp.concatenate([block[start : start + 8] for block in blocks], axis=0)
        both = [main, tail] if c == 1 else [tail, main]
        rows = jnp.concatenate(both, axis=1)
        real = rows * to_real
        imag = rows * to_imag
        by_cos = jnp.concatenate([real, imag], axis=0).astype(jnp.bfloat16)
        by_sin = jnp.concatenate([imag, -real], axis=0).astype(jnp.bfloat16)
        lanes = slice(128, 384) if c == 1 else slice(0, 256)
        total = jnp.zeros((NQ, 128), jnp.float32)
        for part, values in enumerate((by_cos, by_sin)):
            total = total + lax.dot_general(
                table_ref[part, :, lanes],
                values,
                (((1,), (1,)), ((), ())),
                preferred_element_type=jnp.float32,
            )
        total = turned_lanes(total, (position * row) % 4)
        result = total if result is None else result + total
    return result


def forward_z_own_body(me_ref, rows_ref, table_ref, out_ref):
    for c in range(3):
        out_ref[c] = partial_z(me_ref[0], rows_ref, table_ref, 0, c)


def forward_z_body(me_ref, rows_ref, table_ref, own_ref, out_ref):
    lane = lax.broadcasted_iota(jnp.int32, (NQ, 128), 1)
    for c in range(3):
        total = own_ref[c] + partial_z(me_ref[0], rows_ref, table_ref, 1, c)
        total = total * (1.0 / math.sqrt(NZ))
        for x in range(4):
            turned = turned_lanes(total, (x * lane) % 4).astype(jnp.bfloat16)
            for y in range(4):
                out_ref[y * 4 + x, c * 48 : c * 48 + 48, :] = turned[y * 48 : y * 48 + 48]


def forward_z_call(me, rows, table, own):
    rows_spec = pl.BlockSpec((16, 40, 128), lambda j, s: (0, 0, 0))
    table_spec = pl.BlockSpec((2, NQ, 384), lambda j, s: (0, 0, 0))
    own_spec = pl.BlockSpec((3, NQ, 128), lambda j, s: (0, 0, 0))
    out_spec = pl.BlockSpec((16, 144, 128), lambda j, s: (0, 0, 0))
    first = own is None
    return pl.pallas_call(
        forward_z_own_body if first else forward_z_body,
        grid_spec=pltpu.PrefetchScalarGridSpec(
            num_scalar_prefetch=1,
            grid=(1,),
            in_specs=[rows_spec, table_spec] + ([] if first else [own_spec]),
            out_specs=own_spec if first else out_spec,
        ),
        out_shape=jax.ShapeDtypeStruct((3, NQ, 128), jnp.float32)
        if first
        else jax.ShapeDtypeStruct((16, 144, 128), jnp.bfloat16),
        compiler_params=pltpu.CompilerParams(vmem_limit_bytes=VMEM),
        cost_estimate=pl.CostEstimate(flops=151000000, bytes_accessed=1700000, transcendentals=0),
        name="forward_z_own" if first else "forward_z",
    )(me, rows, table, *([] if first else [own]))


def forward_x_body(values_ref, table_ref, out_ref):
    total = jnp.zeros((144, 512), jnp.float32)
    for k in range(8):
        pair = jnp.concatenate([values_ref[2 * k], values_ref[2 * k + 1]], axis=1)
        total = total + jnp.dot(pair, table_ref[k], preferred_element_type=jnp.float32)
    total = (total * (1.0 / 32.0)).astype(jnp.bfloat16)
    for y in range(4):
        out_ref[y] = total


def forward_x_call(values, table):
    return pl.pallas_call(
        forward_x_body,
        out_shape=jax.ShapeDtypeStruct((4, 144, 512), jnp.bfloat16),
        compiler_params=pltpu.CompilerParams(vmem_limit_bytes=VMEM),
        cost_estimate=pl.CostEstimate(flops=302000000, bytes_accessed=3300000, transcendentals=0),
        name="forward_x",
    )(values, table)


def modes_body(kernel_ref, spec_ref, out_ref):
    spec = [spec_ref[0, c * 48 : c * 48 + 48, :].astype(jnp.float32) for c in range(3)]
    for o in range(3):
        real = None
        imag = None
        for c in range(3):
            kr = kernel_ref[0, o, c, 0].astype(jnp.float32)
            ki = kernel_ref[1, o, c, 0].astype(jnp.float32)
            sr = spec[c][:, :NP]
            si = spec[c][:, NP:]
            r = kr * sr - ki * si
            i = kr * si + ki * sr
            real = r if real is None else real + r
            imag = i if imag is None else imag + i
        out_ref[0, o * 48 : o * 48 + 48, :] = real.astype(jnp.bfloat16)
        out_ref[0, 144 + o * 48 : 192 + o * 48, :] = imag.astype(jnp.bfloat16)


def modes_call(kernel, spec):
    return pl.pallas_call(
        modes_body,
        grid=(4,),
        in_specs=[
            pl.BlockSpec((2, 3, 3, 1, 48, NP), lambda j: (0, 0, 0, 0, j, 0)),
            pl.BlockSpec((1, 144, 512), lambda j: (j, 0, 0)),
        ],
        out_specs=pl.BlockSpec((1, 288, NP), lambda j: (j, 0, 0)),
        out_shape=jax.ShapeDtypeStruct((4, 288, NP), jnp.bfloat16),
        compiler_params=pltpu.CompilerParams(vmem_limit_bytes=VMEM),
        cost_estimate=pl.CostEstimate(flops=3600000, bytes_accessed=2950000, transcendentals=0),
        name="modes",
    )(kernel, spec)


def inverse_x_body(values_ref, table_ref, out_ref):
    values = jnp.concatenate([values_ref[s] for s in range(4)], axis=1)

    def block(j, carry):
        total = jnp.dot(values, table_ref[j], preferred_element_type=jnp.float32)
        total = total * (1.0 / 32.0)
        real = (total[:144, :128] - total[144:, 128:]).astype(jnp.bfloat16)
        imag = (total[:144, 128:] + total[144:, :128]).astype(jnp.bfloat16)
        for o in range(3):
            out_ref[j, 0:48, o * 128 : (o + 1) * 128] = real[o * 48 : (o + 1) * 48]
            out_ref[j, 48:96, o * 128 : (o + 1) * 128] = imag[o * 48 : (o + 1) * 48]
        return carry

    lax.fori_loop(0, 8, block, 0, unroll=True)


def inverse_x_call(values, table):
    return pl.pallas_call(
        inverse_x_body,
        out_shape=jax.ShapeDtypeStruct((8, 96, 384), jnp.bfloat16),
        compiler_params=pltpu.CompilerParams(vmem_limit_bytes=VMEM),
        cost_estimate=pl.CostEstimate(flops=1208000000, bytes_accessed=5400000, transcendentals=0),
        name="inverse_x",
    )(values, table)


def inverse_z_body(steps, me_ref, values_ref, table_ref, *out_refs):
    me = me_ref[0]
    values = values_ref[...]
    odd = (lax.broadcasted_iota(jnp.int32, (NQ, 384), 0) * (me // 2)) % 2
    scale = jnp.where(odd == 1, -1.0, 1.0) * (1.0 / math.sqrt(NZ))
    for k, out_ref in zip(steps, out_refs):
        total = jnp.dot(table_ref[me ^ k], values, preferred_element_type=jnp.float32)
        out_ref[...] = (total * scale).astype(out_ref.dtype)


def inverse_z_call(me, values, table, steps):
    block = pl.BlockSpec((NQ, 384), lambda j, s: (0, 0))
    return pl.pallas_call(
        functools.partial(inverse_z_body, steps),
        grid_spec=pltpu.PrefetchScalarGridSpec(
            num_scalar_prefetch=1,
            grid=(1,),
            in_specs=[
                pl.BlockSpec((NZ, 384), lambda j, s: (0, 0)),
                pl.BlockSpec((4, NQ, NZ), lambda j, s: (0, 0, 0)),
            ],
            out_specs=[block] * 2,
        ),
        out_shape=[jax.ShapeDtypeStruct((NQ, 384), jnp.bfloat16) for _ in range(2)],
        compiler_params=pltpu.CompilerParams(vmem_limit_bytes=VMEM),
        cost_estimate=pl.CostEstimate(flops=227000000, bytes_accessed=2000000, transcendentals=0),
        name="inverse_z_far" if steps[0] else "inverse_z_near",
    )(me, values, table)


def finish_body(core_ref, own_ref, far_own_ref, near_ref, far_near_ref, out_ref):
    own = own_ref[...].astype(jnp.float32) + far_own_ref[...].astype(jnp.float32)
    near = near_ref[...].astype(jnp.float32) + far_near_ref[...].astype(jnp.float32)
    first = core_ref[0] == 0
    left = jnp.where(first, own, near).astype(jnp.bfloat16)
    right = jnp.where(first, near, own).astype(jnp.bfloat16)
    for o in range(3):
        out_ref[o, 0, :, 0:128] = left[:, o * 128 : (o + 1) * 128]
        out_ref[o, 0, :, 128:256] = right[:, o * 128 : (o + 1) * 128]


def finish_call(core, own, far_own, near, far_near):
    block = pl.BlockSpec((NQ, 384), lambda j, s: (0, 0))
    return pl.pallas_call(
        finish_body,
        grid_spec=pltpu.PrefetchScalarGridSpec(
            num_scalar_prefetch=1,
            grid=(1,),
            in_specs=[block] * 4,
            out_specs=pl.BlockSpec((3, 1, NQ, NP), lambda j, s: (0, 0, 0, 0)),
        ),
        out_shape=jax.ShapeDtypeStruct((3, 1, NQ, NP), jnp.bfloat16),
        compiler_params=pltpu.CompilerParams(vmem_limit_bytes=VMEM),
        cost_estimate=pl.CostEstimate(flops=150000, bytes_accessed=900000, transcendentals=0),
        name="finish",
    )(core, own, far_own, near, far_near)


def exchange(values, axis):
    return lax.all_to_all(values, axis, split_axis=0, concat_axis=0, tiled=True)


def swap_cores(values):
    return lax.ppermute(values, "core", [(0, 1), (1, 0)])


def move_z(values, step, flip):
    def position(z, core):
        return (z % 8) * 4 + (z // 8) * 2 + core

    perm = []
    for z in range(16):
        for core in range(2):
            target = (z + (step if core == 0 else -step)) % 16
            perm.append((position(z, core), position(target, core ^ flip)))
    return lax.ppermute(values, ("z_lo", "z_hi", "core"), perm)


def per_device(wall, kernel):
    core = lax.axis_index("core")
    gz = (lax.axis_index("z_hi") * 2 + core).reshape(1).astype(jnp.int32)

    rows, z_table = pack_call(wall, jnp.asarray(forward_z_table()))
    rows = exchange(rows, ("z_lo", "z_hi"))
    other = swap_cores(rows)
    z_spectra = forward_z_call(gz, other, z_table, forward_z_call(gz, rows, z_table, None))
    z_spectra = exchange(z_spectra, ("y", "gx"))
    spec = exchange(forward_x_call(z_spectra, jnp.asarray(forward_x_table())), "y")

    modes = exchange(modes_call(kernel, spec), "gx")
    planes = exchange(inverse_x_call(modes, jnp.asarray(inverse_x_table())), ("gx", "core"))
    planes = planes.reshape(NZ, 384)
    z_table = jnp.asarray(inverse_z_table())
    to_far, to_far_near = inverse_z_call(gz, planes, z_table, (2, 3))
    own, to_near = inverse_z_call(gz, planes, z_table, (0, 1))
    far_own = move_z(move_z(to_far, 4, 0), 4, 0)
    far_near = move_z(move_z(to_far_near, 4, 0), 4, 1)
    near = swap_cores(to_near)
    return finish_call(core.reshape(1).astype(jnp.int32), own, far_own, near, far_near)


def solution(mesh):
    fine = Mesh(mesh.devices.reshape(8, 4, 4, 2, 2), ("z_lo", "y", "gx", "z_hi", "core"))
    return jax.shard_map(
        per_device,
        mesh=fine,
        in_specs=(
            P(None, ("z_lo", "y", "gx"), ("z_hi", "core")),
            P(None, None, None, ("z_lo", "y"), ("z_hi", "core"), "gx"),
        ),
        out_specs=P(None, ("z_lo", "y"), ("z_hi", "core"), "gx"),
        check_vma=False,
    )
```

```python
import functools
import math

import jax
import jax.numpy as jnp
import numpy as np
from jax import lax
from jax.experimental import pallas as pl
from jax.experimental.pallas import tpu as pltpu
from jax.sharding import Mesh, PartitionSpec as P

NX = 1024
NZ = 768
NQ = 192
NP = 256
VMEM = 40 * 1024 * 1024


def angle(left, right, length):
    phase = (left[:, None].astype(np.int64) * right[None, :].astype(np.int64)) % length
    return phase * (2.0 * math.pi / length)


def forward_z_table():
    q = np.arange(NQ)
    theta = angle(q, q, NZ)
    both = np.stack([np.cos(theta), np.sin(theta)])
    main, tail = both[..., :128], both[..., 128:]
    zero = np.zeros_like(tail)
    return np.concatenate([tail, zero, main, zero, tail], axis=-1).astype(jnp.bfloat16)


def forward_x_table():
    y, source, low, r = np.meshgrid(
        np.arange(4), np.arange(4), np.arange(8), np.arange(8), indexing="ij"
    )
    x = (8 * (4 * (low * 4 + y) + source) + r).reshape(-1)
    theta = angle(x, np.arange(NP), NX).reshape(16, 64, NP)
    cos, sin = np.cos(theta), np.sin(theta)
    from_real = np.concatenate([cos, -sin], axis=2)
    from_imag = np.concatenate([sin, cos], axis=2)
    both = np.concatenate([from_real, from_imag], axis=1)
    return both.reshape(8, 256, 512).astype(jnp.bfloat16)


def inverse_x_table():
    theta = angle(np.arange(NX), np.arange(NX), NX).reshape(NX, 8, 128)
    both = np.concatenate([np.cos(theta), np.sin(theta)], axis=2)
    return np.transpose(both, (1, 0, 2)).astype(jnp.bfloat16)


def inverse_z_table():
    q = (
        48 * np.arange(4)[:, None, None]
        + 192 * np.arange(2)[None, :, None]
        + np.arange(48)[None, None, :]
    ).reshape(-1)
    theta = angle(np.arange(NZ), q, NZ).reshape(NZ, 8, 48)
    both = np.stack([np.cos(theta), -np.sin(theta)], axis=2)
    return both.reshape(4, NQ, NZ).astype(jnp.bfloat16)


def pack_body(wall_hbm, table_hbm, out_ref, kept_ref, wall_ref, sems):
    wall_copy = pltpu.make_async_copy(wall_hbm, wall_ref, sems.at[0])
    table_copy = pltpu.make_async_copy(table_hbm, kept_ref, sems.at[1])
    wall_copy.start()
    table_copy.start()
    wall_copy.wait()
    rows = [wall_ref[c].astype(jnp.float32) for c in range(3)]
    tails = [row[:, 128:] for row in rows] + [jnp.zeros((8, 64), jnp.float32)]
    pieces = [row[:, :128] for row in rows]
    for c in range(0, 4, 2):
        pieces.append(jnp.concatenate(tails[c : c + 2], axis=1))
    packed = jnp.concatenate(pieces, axis=0).astype(jnp.bfloat16)
    for k in range(16):
        out_ref[k] = packed
    table_copy.wait()


def pack_call(wall, table):
    return pl.pallas_call(
        pack_body,
        in_specs=[pl.BlockSpec(memory_space=pltpu.HBM)] * 2,
        scratch_shapes=[pltpu.VMEM((3, 8, NQ), jnp.bfloat16), pltpu.SemaphoreType.DMA((2,))],
        out_shape=[
            jax.ShapeDtypeStruct((16, 40, 128), jnp.bfloat16),
            jax.ShapeDtypeStruct((2, NQ, 384), jnp.bfloat16),
        ],
        compiler_params=pltpu.CompilerParams(vmem_limit_bytes=VMEM),
        cost_estimate=pl.CostEstimate(flops=10000, bytes_accessed=180000, transcendentals=0),
        name="pack",
    )(
        pltpu.with_memory_space_constraint(wall, pltpu.HBM),
        pltpu.with_memory_space_constraint(table, pltpu.HBM),
    )


def turned_lanes(values, turn):
    lane = lax.broadcasted_iota(jnp.int32, values.shape, 1)
    keep = jnp.where(turn == 0, 1.0, jnp.where(turn == 2, -1.0, 0.0))
    swap = jnp.where(turn == 1, 1.0, jnp.where(turn == 3, -1.0, 0.0))
    swap = jnp.where(lane < 64, swap, -swap)
    return values * keep + pltpu.roll(values, 64, axis=1) * swap


def partial_z(me, rows_ref, table_ref, step, c):
    turn = (me * lax.broadcasted_iota(jnp.int32, (64, 256), 1)) % 4
    to_real = jnp.where(turn == 0, 1.0, jnp.where(turn == 2, -1.0, 0.0))
    to_imag = jnp.where(turn == 3, 1.0, jnp.where(turn == 1, -1.0, 0.0))
    row = lax.broadcasted_iota(jnp.int32, (NQ, 128), 0)
    core = me % 2
    result = None
    for high in range(2):
        position = high * 2 + (core if step == 0 else 1 - core)
        blocks = [rows_ref[low * 2 + high].astype(jnp.float32) for low in range(8)]
        main = jnp.concatenate([block[c * 8 : c * 8 + 8] for block in blocks], axis=0)
        start = 24 + (c // 2) * 8
        tail = jnp.concatenate([block[start : start + 8] for block in blocks], axis=0)
        both = [main, tail] if c == 1 else [tail, main]
        rows = jnp.concatenate(both, axis=1)
        real = rows * to_real
        imag = rows * to_imag
        by_cos = jnp.concatenate([real, imag], axis=0).astype(jnp.bfloat16)
        by_sin = jnp.concatenate([imag, -real], axis=0).astype(jnp.bfloat16)
        lanes = slice(128, 384) if c == 1 else slice(0, 256)
        total = jnp.zeros((NQ, 128), jnp.float32)
        for part, values in enumerate((by_cos, by_sin)):
            total = total + lax.dot_general(
                table_ref[part, :, lanes],
                values,
                (((1,), (1,)), ((), ())),
                preferred_element_type=jnp.float32,
            )
        total = turned_lanes(total, (position * row) % 4)
        result = total if result is None else result + total
    return result


def forward_z_own_body(me_ref, rows_ref, table_ref, out_ref):
    for c in range(3):
        out_ref[c] = partial_z(me_ref[0], rows_ref, table_ref, 0, c)


def forward_z_body(me_ref, rows_ref, table_ref, own_ref, out_ref):
    lane = lax.broadcasted_iota(jnp.int32, (NQ, 128), 1)
    totals = []
    for c in range(3):
        total = own_ref[c] + partial_z(me_ref[0], rows_ref, table_ref, 1, c)
        totals.append(total * (1.0 / math.sqrt(NZ)))
    for pair in range(2):
        if pair:
            totals = [jnp.where(lane % 2 == 1, -total, total) for total in totals]
        for y in range(4):
            for half in range(2):
                start = y * 48 + half * 24
                pieces = [total[start : start + 24] for total in totals]
                block = jnp.concatenate(pieces, axis=0).astype(jnp.bfloat16)
                out_ref[y * 4 + pair * 2 + half] = block


def forward_z_call(me, rows, table, own):
    rows_spec = pl.BlockSpec((16, 40, 128), lambda j, s: (0, 0, 0))
    table_spec = pl.BlockSpec((2, NQ, 384), lambda j, s: (0, 0, 0))
    own_spec = pl.BlockSpec((3, NQ, 128), lambda j, s: (0, 0, 0))
    out_spec = pl.BlockSpec((16, 72, 128), lambda j, s: (0, 0, 0))
    first = own is None
    return pl.pallas_call(
        forward_z_own_body if first else forward_z_body,
        grid_spec=pltpu.PrefetchScalarGridSpec(
            num_scalar_prefetch=1,
            grid=(1,),
            in_specs=[rows_spec, table_spec] + ([] if first else [own_spec]),
            out_specs=own_spec if first else out_spec,
        ),
        out_shape=jax.ShapeDtypeStruct((3, NQ, 128), jnp.float32)
        if first
        else jax.ShapeDtypeStruct((16, 72, 128), jnp.bfloat16),
        compiler_params=pltpu.CompilerParams(vmem_limit_bytes=VMEM),
        cost_estimate=pl.CostEstimate(flops=151000000, bytes_accessed=1700000, transcendentals=0),
        name="forward_z_own" if first else "forward_z",
    )(me, rows, table, *([] if first else [own]))


def forward_x_body(values_ref, table_ref, out_ref):
    turn = lax.broadcasted_iota(jnp.int32, (72, 128), 1) % 4
    total = jnp.zeros((144, 512), jnp.float32)
    for k in range(8):
        first = [values_ref[2 * k + i].astype(jnp.float32) for i in range(2)]
        second = [turned_lanes(value, turn) for value in first]
        both = [jnp.concatenate(pieces, axis=1) for pieces in (first, second)]
        both = jnp.concatenate(both, axis=0).astype(jnp.bfloat16)
        total = total + jnp.dot(both, table_ref[k], preferred_element_type=jnp.float32)
    total = total * (1.0 / 32.0)
    for half in range(2):
        block = total[half * 72 : half * 72 + 72].astype(jnp.bfloat16)
        for y in range(4):
            out_ref[y * 2 + half] = block


def forward_x_call(values, table):
    return pl.pallas_call(
        forward_x_body,
        out_shape=jax.ShapeDtypeStruct((8, 72, 512), jnp.bfloat16),
        compiler_params=pltpu.CompilerParams(vmem_limit_bytes=VMEM),
        cost_estimate=pl.CostEstimate(flops=302000000, bytes_accessed=3000000, transcendentals=0),
        name="forward_x",
    )(values, table)


def modes_body(kernel_ref, spec_ref, out_ref):
    halves = [spec_ref[half].astype(jnp.float32) for half in range(2)]
    spec = []
    for c in range(3):
        pieces = [half[c * 24 : c * 24 + 24] for half in halves]
        spec.append(jnp.concatenate(pieces, axis=0))
    for o in range(3):
        real = None
        imag = None
        for c in range(3):
            kr = kernel_ref[0, o, c, 0].astype(jnp.float32)
            ki = kernel_ref[1, o, c, 0].astype(jnp.float32)
            sr = spec[c][:, :NP]
            si = spec[c][:, NP:]
            r = kr * sr - ki * si
            i = kr * si + ki * sr
            real = r if real is None else real + r
            imag = i if imag is None else imag + i
        out_ref[0, o * 48 : o * 48 + 48, :] = real.astype(jnp.bfloat16)
        out_ref[0, 144 + o * 48 : 192 + o * 48, :] = imag.astype(jnp.bfloat16)


def modes_call(kernel, spec):
    return pl.pallas_call(
        modes_body,
        grid=(4,),
        in_specs=[
            pl.BlockSpec((2, 3, 3, 1, 48, NP), lambda j: (0, 0, 0, 0, j, 0)),
            pl.BlockSpec((2, 72, 512), lambda j: (j, 0, 0)),
        ],
        out_specs=pl.BlockSpec((1, 288, NP), lambda j: (j, 0, 0)),
        out_shape=jax.ShapeDtypeStruct((4, 288, NP), jnp.bfloat16),
        compiler_params=pltpu.CompilerParams(vmem_limit_bytes=VMEM),
        cost_estimate=pl.CostEstimate(flops=3600000, bytes_accessed=2950000, transcendentals=0),
        name="modes",
    )(kernel, spec)


def inverse_x_body(values_ref, table_ref, out_ref):
    values = jnp.concatenate([values_ref[s] for s in range(4)], axis=1)

    def block(j, carry):
        total = jnp.dot(values, table_ref[j], preferred_element_type=jnp.float32)
        total = total * (1.0 / 32.0)
        real = (total[:144, :128] - total[144:, 128:]).astype(jnp.bfloat16)
        imag = (total[:144, 128:] + total[144:, :128]).astype(jnp.bfloat16)
        for o in range(3):
            out_ref[j, 0:48, o * 128 : (o + 1) * 128] = real[o * 48 : (o + 1) * 48]
            out_ref[j, 48:96, o * 128 : (o + 1) * 128] = imag[o * 48 : (o + 1) * 48]
        return carry

    lax.fori_loop(0, 8, block, 0, unroll=True)


def inverse_x_call(values, table):
    return pl.pallas_call(
        inverse_x_body,
        out_shape=jax.ShapeDtypeStruct((8, 96, 384), jnp.bfloat16),
        compiler_params=pltpu.CompilerParams(vmem_limit_bytes=VMEM),
        cost_estimate=pl.CostEstimate(flops=1208000000, bytes_accessed=5400000, transcendentals=0),
        name="inverse_x",
    )(values, table)


def inverse_z_body(steps, me_ref, values_ref, table_ref, *out_refs):
    me = me_ref[0]
    values = values_ref[...]
    odd = (lax.broadcasted_iota(jnp.int32, (NQ, 384), 0) * (me // 2)) % 2
    scale = jnp.where(odd == 1, -1.0, 1.0) * (1.0 / math.sqrt(NZ))
    for k, out_ref in zip(steps, out_refs):
        total = jnp.dot(table_ref[me ^ k], values, preferred_element_type=jnp.float32)
        out_ref[...] = (total * scale).astype(out_ref.dtype)


def inverse_z_call(me, values, table, steps):
    block = pl.BlockSpec((NQ, 384), lambda j, s: (0, 0))
    return pl.pallas_call(
        functools.partial(inverse_z_body, steps),
        grid_spec=pltpu.PrefetchScalarGridSpec(
            num_scalar_prefetch=1,
            grid=(1,),
            in_specs=[
                pl.BlockSpec((NZ, 384), lambda j, s: (0, 0)),
                pl.BlockSpec((4, NQ, NZ), lambda j, s: (0, 0, 0)),
            ],
            out_specs=[block] * 2,
        ),
        out_shape=[jax.ShapeDtypeStruct((NQ, 384), jnp.bfloat16) for _ in range(2)],
        compiler_params=pltpu.CompilerParams(vmem_limit_bytes=VMEM),
        cost_estimate=pl.CostEstimate(flops=227000000, bytes_accessed=2000000, transcendentals=0),
        name="inverse_z_far" if steps[0] else "inverse_z_near",
    )(me, values, table)


def finish_body(core_ref, own_ref, far_own_ref, near_ref, far_near_ref, out_ref):
    own = own_ref[...].astype(jnp.float32) + far_own_ref[...].astype(jnp.float32)
    near = near_ref[...].astype(jnp.float32) + far_near_ref[...].astype(jnp.float32)
    first = core_ref[0] == 0
    left = jnp.where(first, own, near).astype(jnp.bfloat16)
    right = jnp.where(first, near, own).astype(jnp.bfloat16)
    for o in range(3):
        out_ref[o, 0, :, 0:128] = left[:, o * 128 : (o + 1) * 128]
        out_ref[o, 0, :, 128:256] = right[:, o * 128 : (o + 1) * 128]


def finish_call(core, own, far_own, near, far_near):
    block = pl.BlockSpec((NQ, 384), lambda j, s: (0, 0))
    return pl.pallas_call(
        finish_body,
        grid_spec=pltpu.PrefetchScalarGridSpec(
            num_scalar_prefetch=1,
            grid=(1,),
            in_specs=[block] * 4,
            out_specs=pl.BlockSpec((3, 1, NQ, NP), lambda j, s: (0, 0, 0, 0)),
        ),
        out_shape=jax.ShapeDtypeStruct((3, 1, NQ, NP), jnp.bfloat16),
        compiler_params=pltpu.CompilerParams(vmem_limit_bytes=VMEM),
        cost_estimate=pl.CostEstimate(flops=150000, bytes_accessed=900000, transcendentals=0),
        name="finish",
    )(core, own, far_own, near, far_near)


def exchange(values, axis):
    return lax.all_to_all(values, axis, split_axis=0, concat_axis=0, tiled=True)


def swap_cores(values):
    return lax.ppermute(values, "core", [(0, 1), (1, 0)])


def move_z(values, step, flip):
    def position(z, core):
        return (z % 8) * 4 + (z // 8) * 2 + core

    perm = []
    for z in range(16):
        for core in range(2):
            target = (z + (step if core == 0 else -step)) % 16
            perm.append((position(z, core), position(target, core ^ flip)))
    return lax.ppermute(values, ("z_lo", "z_hi", "core"), perm)


def per_device(wall, kernel):
    core = lax.axis_index("core")
    gz = (lax.axis_index("z_hi") * 2 + core).reshape(1).astype(jnp.int32)

    rows, z_table = pack_call(wall, jnp.asarray(forward_z_table()))
    rows = exchange(rows, ("z_lo", "z_hi"))
    other = swap_cores(rows)
    z_spectra = forward_z_call(gz, other, z_table, forward_z_call(gz, rows, z_table, None))
    z_spectra = exchange(z_spectra, ("y", "gx_pair", "gx_in"))
    spec = exchange(forward_x_call(z_spectra, jnp.asarray(forward_x_table())), ("y", "gx_in"))

    modes = exchange(modes_call(kernel, spec), ("gx_pair", "gx_in"))
    planes = exchange(inverse_x_call(modes, jnp.asarray(inverse_x_table())), ("gx_pair", "gx_in", "core"))
    planes = planes.reshape(NZ, 384)
    z_table = jnp.asarray(inverse_z_table())
    to_far, to_far_near = inverse_z_call(gz, planes, z_table, (2, 3))
    own, to_near = inverse_z_call(gz, planes, z_table, (0, 1))
    far_own = move_z(move_z(to_far, 4, 0), 4, 0)
    far_near = move_z(move_z(to_far_near, 4, 0), 4, 1)
    near = swap_cores(to_near)
    return finish_call(core.reshape(1).astype(jnp.int32), own, far_own, near, far_near)


def solution(mesh):
    fine = Mesh(
        mesh.devices.reshape(8, 4, 2, 2, 2, 2),
        ("z_lo", "y", "gx_pair", "gx_in", "z_hi", "core"),
    )
    gx, gz = ("gx_pair", "gx_in"), ("z_hi", "core")
    return jax.shard_map(
        per_device,
        mesh=fine,
        in_specs=(
            P(None, ("z_lo", "y") + gx, gz),
            P(None, None, None, ("z_lo", "y"), gz, gx),
        ),
        out_specs=P(None, ("z_lo", "y"), gz, gx),
        check_vma=False,
    )
```

```python
import functools
import math

import jax
import jax.numpy as jnp
import numpy as np
from jax import lax
from jax.experimental import pallas as pl
from jax.experimental.pallas import tpu as pltpu
from jax.sharding import Mesh, PartitionSpec as P

NX = 1024
NZ = 768
NQ = 192
NP = 256
VMEM = 40 * 1024 * 1024


def angle(left, right, length):
    phase = (left[:, None].astype(np.int64) * right[None, :].astype(np.int64)) % length
    return phase * (2.0 * math.pi / length)


def forward_z_table():
    q = np.arange(NQ)
    theta = angle(q, q, NZ)
    both = np.stack([np.cos(theta), np.sin(theta)])
    main, tail = both[..., :128], both[..., 128:]
    zero = np.zeros_like(tail)
    return np.concatenate([tail, zero, main, zero, tail], axis=-1).astype(jnp.bfloat16)


def forward_x_table():
    y, source, low, r = np.meshgrid(
        np.arange(4), np.arange(4), np.arange(8), np.arange(8), indexing="ij"
    )
    x = (8 * (4 * (low * 4 + y) + source) + r).reshape(-1)
    theta = angle(x, np.arange(NP), NX).reshape(16, 64, NP)
    cos, sin = np.cos(theta), np.sin(theta)
    from_real = np.concatenate([cos, -sin], axis=2)
    from_imag = np.concatenate([sin, cos], axis=2)
    both = np.concatenate([from_real, from_imag], axis=1)
    return both.reshape(8, 256, 512).astype(jnp.bfloat16)


def inverse_x_table():
    theta = angle(np.arange(NX), np.arange(NX), NX).reshape(NX, 8, 128)
    both = np.concatenate([np.cos(theta), np.sin(theta)], axis=2)
    return np.transpose(both, (1, 0, 2)).astype(jnp.bfloat16)


def inverse_z_table():
    q = (
        48 * np.arange(4)[:, None, None]
        + 192 * np.arange(2)[None, :, None]
        + np.arange(48)[None, None, :]
    ).reshape(-1)
    theta = angle(np.arange(NZ), q, NZ).reshape(NZ, 8, 48)
    both = np.stack([np.cos(theta), -np.sin(theta)], axis=2)
    return both.reshape(4, NQ, NZ).astype(jnp.bfloat16)


def pack_body(wall_hbm, table_hbm, out_ref, kept_ref, wall_ref, sems):
    wall_copy = pltpu.make_async_copy(wall_hbm, wall_ref, sems.at[0])
    table_copy = pltpu.make_async_copy(table_hbm, kept_ref, sems.at[1])
    wall_copy.start()
    table_copy.start()
    wall_copy.wait()
    rows = [wall_ref[c].astype(jnp.float32) for c in range(3)]
    tails = [row[:, 128:] for row in rows] + [jnp.zeros((8, 64), jnp.float32)]
    pieces = [row[:, :128] for row in rows]
    for c in range(0, 4, 2):
        pieces.append(jnp.concatenate(tails[c : c + 2], axis=1))
    packed = jnp.concatenate(pieces, axis=0).astype(jnp.bfloat16)
    for k in range(16):
        out_ref[k] = packed
    table_copy.wait()


def pack_call(wall, table):
    return pl.pallas_call(
        pack_body,
        in_specs=[pl.BlockSpec(memory_space=pltpu.HBM)] * 2,
        scratch_shapes=[pltpu.VMEM((3, 8, NQ), jnp.bfloat16), pltpu.SemaphoreType.DMA((2,))],
        out_shape=[
            jax.ShapeDtypeStruct((16, 40, 128), jnp.bfloat16),
            jax.ShapeDtypeStruct((2, NQ, 384), jnp.bfloat16),
        ],
        compiler_params=pltpu.CompilerParams(vmem_limit_bytes=VMEM),
        cost_estimate=pl.CostEstimate(flops=10000, bytes_accessed=180000, transcendentals=0),
        name="pack",
    )(
        pltpu.with_memory_space_constraint(wall, pltpu.HBM),
        pltpu.with_memory_space_constraint(table, pltpu.HBM),
    )


def turned_lanes(values, turn):
    lane = lax.broadcasted_iota(jnp.int32, values.shape, 1)
    keep = jnp.where(turn == 0, 1.0, jnp.where(turn == 2, -1.0, 0.0))
    swap = jnp.where(turn == 1, 1.0, jnp.where(turn == 3, -1.0, 0.0))
    swap = jnp.where(lane < 64, swap, -swap)
    return values * keep + pltpu.roll(values, 64, axis=1) * swap


def partial_z(me, rows_ref, table_ref, step, c):
    turn = (me * lax.broadcasted_iota(jnp.int32, (64, 256), 1)) % 4
    to_real = jnp.where(turn == 0, 1.0, jnp.where(turn == 2, -1.0, 0.0))
    to_imag = jnp.where(turn == 3, 1.0, jnp.where(turn == 1, -1.0, 0.0))
    row = lax.broadcasted_iota(jnp.int32, (NQ, 128), 0)
    core = me % 2
    result = None
    for high in range(2):
        position = high * 2 + (core if step == 0 else 1 - core)
        blocks = [rows_ref[low * 2 + high].astype(jnp.float32) for low in range(8)]
        main = jnp.concatenate([block[c * 8 : c * 8 + 8] for block in blocks], axis=0)
        start = 24 + (c // 2) * 8
        tail = jnp.concatenate([block[start : start + 8] for block in blocks], axis=0)
        both = [main, tail] if c == 1 else [tail, main]
        rows = jnp.concatenate(both, axis=1)
        real = rows * to_real
        imag = rows * to_imag
        by_cos = jnp.concatenate([real, imag], axis=0).astype(jnp.bfloat16)
        by_sin = jnp.concatenate([imag, -real], axis=0).astype(jnp.bfloat16)
        lanes = slice(128, 384) if c == 1 else slice(0, 256)
        total = jnp.zeros((NQ, 128), jnp.float32)
        for part, values in enumerate((by_cos, by_sin)):
            total = total + lax.dot_general(
                table_ref[part, :, lanes],
                values,
                (((1,), (1,)), ((), ())),
                preferred_element_type=jnp.float32,
            )
        total = turned_lanes(total, (position * row) % 4)
        result = total if result is None else result + total
    return result


def forward_z_own_body(me_ref, rows_ref, table_ref, out_ref):
    for c in range(3):
        out_ref[c] = partial_z(me_ref[0], rows_ref, table_ref, 0, c)


def forward_z_body(me_ref, rows_ref, table_ref, own_ref, out_ref):
    lane = lax.broadcasted_iota(jnp.int32, (NQ, 128), 1)
    totals = []
    for c in range(3):
        total = own_ref[c] + partial_z(me_ref[0], rows_ref, table_ref, 1, c)
        totals.append(total * (1.0 / math.sqrt(NZ)))
    for pair in range(2):
        if pair:
            totals = [jnp.where(lane % 2 == 1, -total, total) for total in totals]
        for y in range(4):
            for half in range(2):
                start = y * 48 + half * 24
                pieces = [total[start : start + 24] for total in totals]
                block = jnp.concatenate(pieces, axis=0).astype(jnp.bfloat16)
                out_ref[y * 4 + pair * 2 + half] = block


def forward_z_call(me, rows, table, own):
    rows_spec = pl.BlockSpec((16, 40, 128), lambda j, s: (0, 0, 0))
    table_spec = pl.BlockSpec((2, NQ, 384), lambda j, s: (0, 0, 0))
    own_spec = pl.BlockSpec((3, NQ, 128), lambda j, s: (0, 0, 0))
    out_spec = pl.BlockSpec((16, 72, 128), lambda j, s: (0, 0, 0))
    first = own is None
    return pl.pallas_call(
        forward_z_own_body if first else forward_z_body,
        grid_spec=pltpu.PrefetchScalarGridSpec(
            num_scalar_prefetch=1,
            grid=(1,),
            in_specs=[rows_spec, table_spec] + ([] if first else [own_spec]),
            out_specs=own_spec if first else out_spec,
        ),
        out_shape=jax.ShapeDtypeStruct((3, NQ, 128), jnp.float32)
        if first
        else jax.ShapeDtypeStruct((16, 72, 128), jnp.bfloat16),
        compiler_params=pltpu.CompilerParams(vmem_limit_bytes=VMEM),
        cost_estimate=pl.CostEstimate(flops=151000000, bytes_accessed=1700000, transcendentals=0),
        name="forward_z_own" if first else "forward_z",
    )(me, rows, table, *([] if first else [own]))


def forward_x_body(values_ref, table_ref, out_ref):
    turn = lax.broadcasted_iota(jnp.int32, (72, 128), 1) % 4
    total = jnp.zeros((144, 512), jnp.float32)
    for k in range(8):
        first = [values_ref[2 * k + i].astype(jnp.float32) for i in range(2)]
        second = [turned_lanes(value, turn) for value in first]
        both = [jnp.concatenate(pieces, axis=1) for pieces in (first, second)]
        both = jnp.concatenate(both, axis=0).astype(jnp.bfloat16)
        total = total + jnp.dot(both, table_ref[k], preferred_element_type=jnp.float32)
    total = total * (1.0 / 32.0)
    for half in range(2):
        block = total[half * 72 : half * 72 + 72].astype(jnp.bfloat16)
        for y in range(4):
            out_ref[y * 2 + half] = block


def forward_x_call(values, table):
    return pl.pallas_call(
        forward_x_body,
        out_shape=jax.ShapeDtypeStruct((8, 72, 512), jnp.bfloat16),
        compiler_params=pltpu.CompilerParams(vmem_limit_bytes=VMEM),
        cost_estimate=pl.CostEstimate(flops=302000000, bytes_accessed=3000000, transcendentals=0),
        name="forward_x",
    )(values, table)


def modes_body(kernel_ref, spec_ref, out_ref):
    halves = [spec_ref[half].astype(jnp.float32) for half in range(2)]
    spec = []
    for c in range(3):
        pieces = [half[c * 24 : c * 24 + 24] for half in halves]
        spec.append(jnp.concatenate(pieces, axis=0))
    for o in range(3):
        real = None
        imag = None
        for c in range(3):
            kr = kernel_ref[0, o, c, 0].astype(jnp.float32)
            ki = kernel_ref[1, o, c, 0].astype(jnp.float32)
            sr = spec[c][:, :NP]
            si = spec[c][:, NP:]
            r = kr * sr - ki * si
            i = kr * si + ki * sr
            real = r if real is None else real + r
            imag = i if imag is None else imag + i
        out_ref[0, o * 48 : o * 48 + 48, :] = real.astype(jnp.bfloat16)
        out_ref[0, 144 + o * 48 : 192 + o * 48, :] = imag.astype(jnp.bfloat16)


def modes_call(kernel, spec):
    return pl.pallas_call(
        modes_body,
        grid=(4,),
        in_specs=[
            pl.BlockSpec((2, 3, 3, 1, 48, NP), lambda j: (0, 0, 0, 0, j, 0)),
            pl.BlockSpec((2, 72, 512), lambda j: (j, 0, 0)),
        ],
        out_specs=pl.BlockSpec((1, 288, NP), lambda j: (j, 0, 0)),
        out_shape=jax.ShapeDtypeStruct((4, 288, NP), jnp.bfloat16),
        compiler_params=pltpu.CompilerParams(vmem_limit_bytes=VMEM),
        cost_estimate=pl.CostEstimate(flops=3600000, bytes_accessed=2950000, transcendentals=0),
        name="modes",
    )(kernel, spec)


def inverse_x_body(values_ref, table_ref, out_ref):
    values = jnp.concatenate([values_ref[s] for s in range(4)], axis=1)

    def block(j, carry):
        total = jnp.dot(values, table_ref[j], preferred_element_type=jnp.float32)
        total = total * (1.0 / 32.0)
        real = (total[:144, :128] - total[144:, 128:]).astype(jnp.bfloat16)
        imag = (total[:144, 128:] + total[144:, :128]).astype(jnp.bfloat16)
        for o in range(3):
            out_ref[j, 0:48, o * 128 : (o + 1) * 128] = real[o * 48 : (o + 1) * 48]
            out_ref[j, 48:96, o * 128 : (o + 1) * 128] = imag[o * 48 : (o + 1) * 48]
        return carry

    lax.fori_loop(0, 8, block, 0, unroll=True)


def inverse_x_call(values, table):
    return pl.pallas_call(
        inverse_x_body,
        out_shape=jax.ShapeDtypeStruct((8, 96, 384), jnp.bfloat16),
        compiler_params=pltpu.CompilerParams(vmem_limit_bytes=VMEM),
        cost_estimate=pl.CostEstimate(flops=1208000000, bytes_accessed=5400000, transcendentals=0),
        name="inverse_x",
    )(values, table)


def inverse_z_body(steps, me_ref, values_ref, table_ref, *out_refs):
    me = me_ref[0]
    values = values_ref[...]
    odd = (lax.broadcasted_iota(jnp.int32, (NQ, 384), 0) * (me // 2)) % 2
    scale = jnp.where(odd == 1, -1.0, 1.0) * (1.0 / math.sqrt(NZ))
    for k, out_ref in zip(steps, out_refs):
        total = jnp.dot(table_ref[me ^ k], values, preferred_element_type=jnp.float32)
        out_ref[...] = (total * scale).astype(out_ref.dtype)


def inverse_z_call(me, values, table, steps):
    block = pl.BlockSpec((NQ, 384), lambda j, s: (0, 0))
    return pl.pallas_call(
        functools.partial(inverse_z_body, steps),
        grid_spec=pltpu.PrefetchScalarGridSpec(
            num_scalar_prefetch=1,
            grid=(1,),
            in_specs=[
                pl.BlockSpec((NZ, 384), lambda j, s: (0, 0)),
                pl.BlockSpec((4, NQ, NZ), lambda j, s: (0, 0, 0)),
            ],
            out_specs=[block] * 2,
        ),
        out_shape=[jax.ShapeDtypeStruct((NQ, 384), jnp.bfloat16) for _ in range(2)],
        compiler_params=pltpu.CompilerParams(vmem_limit_bytes=VMEM),
        cost_estimate=pl.CostEstimate(flops=227000000, bytes_accessed=2000000, transcendentals=0),
        name="inverse_z_far" if steps[0] else "inverse_z_near",
    )(me, values, table)


def finish_body(core_ref, own_ref, far_own_ref, near_ref, far_near_ref, out_ref):
    own = own_ref[...].astype(jnp.float32) + far_own_ref[...].astype(jnp.float32)
    near = near_ref[...].astype(jnp.float32) + far_near_ref[...].astype(jnp.float32)
    first = core_ref[0] == 0
    left = jnp.where(first, own, near).astype(jnp.bfloat16)
    right = jnp.where(first, near, own).astype(jnp.bfloat16)
    for o in range(3):
        out_ref[o, 0, :, 0:128] = left[:, o * 128 : (o + 1) * 128]
        out_ref[o, 0, :, 128:256] = right[:, o * 128 : (o + 1) * 128]


def finish_call(core, own, far_own, near, far_near):
    block = pl.BlockSpec((NQ, 384), lambda j, s: (0, 0))
    return pl.pallas_call(
        finish_body,
        grid_spec=pltpu.PrefetchScalarGridSpec(
            num_scalar_prefetch=1,
            grid=(1,),
            in_specs=[block] * 4,
            out_specs=pl.BlockSpec((3, 1, NQ, NP), lambda j, s: (0, 0, 0, 0)),
        ),
        out_shape=jax.ShapeDtypeStruct((3, 1, NQ, NP), jnp.bfloat16),
        compiler_params=pltpu.CompilerParams(vmem_limit_bytes=VMEM),
        cost_estimate=pl.CostEstimate(flops=150000, bytes_accessed=900000, transcendentals=0),
        name="finish",
    )(core, own, far_own, near, far_near)


def exchange(values, axis):
    return lax.all_to_all(values, axis, split_axis=0, concat_axis=0, tiled=True)


def swap_cores(values):
    return lax.ppermute(values, "core", [(0, 1), (1, 0)])


def move_z(values, step, flip):
    def position(z, core):
        return (z % 8) * 4 + (z // 8) * 2 + core

    perm = []
    for z in range(16):
        for core in range(2):
            target = (z + (step if core == 0 else -step)) % 16
            perm.append((position(z, core), position(target, core ^ flip)))
    return lax.ppermute(values, ("z_lo", "z_hi", "core"), perm)


def per_device(wall, kernel):
    core = lax.axis_index("core")
    gz = (lax.axis_index("z_hi") * 2 + core).reshape(1).astype(jnp.int32)

    rows, z_table = pack_call(wall, jnp.asarray(forward_z_table()))
    rows = exchange(rows, ("z_lo", "z_hi"))
    other = swap_cores(rows)
    z_spectra = forward_z_call(gz, other, z_table, forward_z_call(gz, rows, z_table, None))
    z_spectra = exchange(z_spectra, ("y", "gx_pair", "gx_in"))
    spec = exchange(forward_x_call(z_spectra, jnp.asarray(forward_x_table())), ("y", "gx_in"))

    modes = exchange(modes_call(kernel, spec), ("gx_pair", "gx_in"))
    planes = exchange(inverse_x_call(modes, jnp.asarray(inverse_x_table())), ("gx_pair", "gx_in", "core"))
    planes = planes.reshape(NZ, 384)
    z_table = jnp.asarray(inverse_z_table())
    to_far, to_far_near = inverse_z_call(gz, planes, z_table, (2, 3))
    own, to_near = inverse_z_call(gz, planes, z_table, (0, 1))
    half_own = move_z(to_far, 4, 0)
    half_near = move_z(to_far_near, 4, 0)
    half_own, to_near = lax.optimization_barrier((half_own, to_near))
    far_own = move_z(half_own, 4, 0)
    far_near = move_z(half_near, 4, 1)
    near = swap_cores(to_near)
    return finish_call(core.reshape(1).astype(jnp.int32), own, far_own, near, far_near)


def solution(mesh):
    fine = Mesh(
        mesh.devices.reshape(8, 4, 2, 2, 2, 2),
        ("z_lo", "y", "gx_pair", "gx_in", "z_hi", "core"),
    )
    gx, gz = ("gx_pair", "gx_in"), ("z_hi", "core")
    return jax.shard_map(
        per_device,
        mesh=fine,
        in_specs=(
            P(None, ("z_lo", "y") + gx, gz),
            P(None, None, None, ("z_lo", "y"), gz, gx),
        ),
        out_specs=P(None, ("z_lo", "y"), gz, gx),
        check_vma=False,
    )
```

```python
import functools
import math

import jax
import jax.numpy as jnp
import numpy as np
from jax import lax
from jax.experimental import pallas as pl
from jax.experimental.pallas import tpu as pltpu
from jax.sharding import Mesh, PartitionSpec as P

NX = 1024
NZ = 768
NQ = 192
NP = 256
VMEM = 40 * 1024 * 1024


def angle(left, right, length):
    phase = (left[:, None].astype(np.int64) * right[None, :].astype(np.int64)) % length
    return phase * (2.0 * math.pi / length)


def forward_z_table():
    q = np.arange(NQ)
    theta = angle(q, q, NZ)
    both = np.stack([np.cos(theta), np.sin(theta)])
    main, tail = both[..., :128], both[..., 128:]
    zero = np.zeros_like(tail)
    return np.concatenate([tail, zero, main, zero, tail], axis=-1).astype(jnp.bfloat16)


def forward_x_table():
    y, source, low, r = np.meshgrid(
        np.arange(4), np.arange(4), np.arange(8), np.arange(8), indexing="ij"
    )
    x = (8 * (4 * (low * 4 + y) + source) + r).reshape(-1)
    theta = angle(x, np.arange(NP), NX).reshape(16, 64, NP)
    cos, sin = np.cos(theta), np.sin(theta)
    from_real = np.concatenate([cos, -sin], axis=2)
    from_imag = np.concatenate([sin, cos], axis=2)
    both = np.concatenate([from_real, from_imag], axis=1)
    return both.reshape(8, 256, 512).astype(jnp.bfloat16)


def inverse_x_table():
    theta = angle(np.arange(NX), np.arange(NX), NX).reshape(NX, 8, 128)
    both = np.concatenate([np.cos(theta), np.sin(theta)], axis=2)
    return np.transpose(both, (1, 0, 2)).astype(jnp.bfloat16)


def inverse_z_table():
    q = (
        48 * np.arange(4)[:, None, None]
        + 192 * np.arange(2)[None, :, None]
        + np.arange(48)[None, None, :]
    ).reshape(-1)
    theta = angle(np.arange(NZ), q, NZ).reshape(NZ, 8, 48)
    both = np.stack([np.cos(theta), -np.sin(theta)], axis=2)
    return both.reshape(4, NQ, NZ).astype(jnp.bfloat16)


def pack_body(wall_hbm, table_hbm, out_ref, kept_ref, wall_ref, sems):
    wall_copy = pltpu.make_async_copy(wall_hbm, wall_ref, sems.at[0])
    table_copy = pltpu.make_async_copy(table_hbm, kept_ref, sems.at[1])
    wall_copy.start()
    table_copy.start()
    wall_copy.wait()
    rows = [wall_ref[c].astype(jnp.float32) for c in range(3)]
    tails = [row[:, 128:] for row in rows] + [jnp.zeros((8, 64), jnp.float32)]
    pieces = [row[:, :128] for row in rows]
    for c in range(0, 4, 2):
        pieces.append(jnp.concatenate(tails[c : c + 2], axis=1))
    packed = jnp.concatenate(pieces, axis=0).astype(jnp.bfloat16)
    for k in range(16):
        out_ref[k] = packed
    table_copy.wait()


def pack_call(wall, table):
    return pl.pallas_call(
        pack_body,
        in_specs=[pl.BlockSpec(memory_space=pltpu.HBM)] * 2,
        scratch_shapes=[pltpu.VMEM((3, 8, NQ), jnp.bfloat16), pltpu.SemaphoreType.DMA((2,))],
        out_shape=[
            jax.ShapeDtypeStruct((16, 40, 128), jnp.bfloat16),
            jax.ShapeDtypeStruct((2, NQ, 384), jnp.bfloat16),
        ],
        compiler_params=pltpu.CompilerParams(vmem_limit_bytes=VMEM),
        cost_estimate=pl.CostEstimate(flops=10000, bytes_accessed=180000, transcendentals=0),
        name="pack",
    )(
        pltpu.with_memory_space_constraint(wall, pltpu.HBM),
        pltpu.with_memory_space_constraint(table, pltpu.HBM),
    )


def turned_lanes(values, turn):
    lane = lax.broadcasted_iota(jnp.int32, values.shape, 1)
    keep = jnp.where(turn == 0, 1.0, jnp.where(turn == 2, -1.0, 0.0))
    swap = jnp.where(turn == 1, 1.0, jnp.where(turn == 3, -1.0, 0.0))
    swap = jnp.where(lane < 64, swap, -swap)
    return values * keep + pltpu.roll(values, 64, axis=1) * swap


def partial_z(me, rows_ref, table_ref, step, c):
    turn = (me * lax.broadcasted_iota(jnp.int32, (64, 256), 1)) % 4
    to_real = jnp.where(turn == 0, 1.0, jnp.where(turn == 2, -1.0, 0.0))
    to_imag = jnp.where(turn == 3, 1.0, jnp.where(turn == 1, -1.0, 0.0))
    row = lax.broadcasted_iota(jnp.int32, (NQ, 128), 0)
    core = me % 2
    result = None
    for high in range(2):
        position = high * 2 + (core if step == 0 else 1 - core)
        blocks = [rows_ref[low * 2 + high].astype(jnp.float32) for low in range(8)]
        main = jnp.concatenate([block[c * 8 : c * 8 + 8] for block in blocks], axis=0)
        start = 24 + (c // 2) * 8
        tail = jnp.concatenate([block[start : start + 8] for block in blocks], axis=0)
        both = [main, tail] if c == 1 else [tail, main]
        rows = jnp.concatenate(both, axis=1)
        real = rows * to_real
        imag = rows * to_imag
        by_cos = jnp.concatenate([real, imag], axis=0).astype(jnp.bfloat16)
        by_sin = jnp.concatenate([imag, -real], axis=0).astype(jnp.bfloat16)
        lanes = slice(128, 384) if c == 1 else slice(0, 256)
        total = jnp.zeros((NQ, 128), jnp.float32)
        for part, values in enumerate((by_cos, by_sin)):
            total = total + lax.dot_general(
                table_ref[part, :, lanes],
                values,
                (((1,), (1,)), ((), ())),
                preferred_element_type=jnp.float32,
            )
        total = turned_lanes(total, (position * row) % 4)
        result = total if result is None else result + total
    return result


def forward_z_own_body(me_ref, rows_ref, table_ref, out_ref):
    for c in range(3):
        out_ref[c] = partial_z(me_ref[0], rows_ref, table_ref, 0, c)


def forward_z_body(me_ref, rows_ref, table_ref, own_ref, out_ref):
    lane = lax.broadcasted_iota(jnp.int32, (NQ, 128), 1)
    totals = []
    for c in range(3):
        total = own_ref[c] + partial_z(me_ref[0], rows_ref, table_ref, 1, c)
        totals.append(total * (1.0 / math.sqrt(NZ)))
    for pair in range(2):
        if pair:
            totals = [jnp.where(lane % 2 == 1, -total, total) for total in totals]
        for y in range(4):
            for half in range(2):
                start = y * 48 + half * 24
                pieces = [total[start : start + 24] for total in totals]
                block = jnp.concatenate(pieces, axis=0).astype(jnp.bfloat16)
                out_ref[y * 4 + pair * 2 + half] = block


def forward_z_call(me, rows, table, own):
    rows_spec = pl.BlockSpec((16, 40, 128), lambda j, s: (0, 0, 0))
    table_spec = pl.BlockSpec((2, NQ, 384), lambda j, s: (0, 0, 0))
    own_spec = pl.BlockSpec((3, NQ, 128), lambda j, s: (0, 0, 0))
    out_spec = pl.BlockSpec((16, 72, 128), lambda j, s: (0, 0, 0))
    first = own is None
    return pl.pallas_call(
        forward_z_own_body if first else forward_z_body,
        grid_spec=pltpu.PrefetchScalarGridSpec(
            num_scalar_prefetch=1,
            grid=(1,),
            in_specs=[rows_spec, table_spec] + ([] if first else [own_spec]),
            out_specs=own_spec if first else out_spec,
        ),
        out_shape=jax.ShapeDtypeStruct((3, NQ, 128), jnp.float32)
        if first
        else jax.ShapeDtypeStruct((16, 72, 128), jnp.bfloat16),
        compiler_params=pltpu.CompilerParams(vmem_limit_bytes=VMEM),
        cost_estimate=pl.CostEstimate(flops=151000000, bytes_accessed=1700000, transcendentals=0),
        name="forward_z_own" if first else "forward_z",
    )(me, rows, table, *([] if first else [own]))


def forward_x_body(values_ref, table_ref, out_ref):
    turn = lax.broadcasted_iota(jnp.int32, (72, 128), 1) % 4
    total = jnp.zeros((144, 512), jnp.float32)
    for k in range(8):
        first = [values_ref[2 * k + i].astype(jnp.float32) for i in range(2)]
        second = [turned_lanes(value, turn) for value in first]
        both = [jnp.concatenate(pieces, axis=1) for pieces in (first, second)]
        both = jnp.concatenate(both, axis=0).astype(jnp.bfloat16)
        total = total + jnp.dot(both, table_ref[k], preferred_element_type=jnp.float32)
    total = total * (1.0 / 32.0)
    for half in range(2):
        block = total[half * 72 : half * 72 + 72].astype(jnp.bfloat16)
        for y in range(4):
            out_ref[y * 2 + half] = block


def forward_x_call(values, table):
    return pl.pallas_call(
        forward_x_body,
        out_shape=jax.ShapeDtypeStruct((8, 72, 512), jnp.bfloat16),
        compiler_params=pltpu.CompilerParams(vmem_limit_bytes=VMEM),
        cost_estimate=pl.CostEstimate(flops=302000000, bytes_accessed=3000000, transcendentals=0),
        name="forward_x",
    )(values, table)


def modes_body(kernel_ref, spec_ref, out_ref):
    halves = [spec_ref[half].astype(jnp.float32) for half in range(2)]
    spec = []
    for c in range(3):
        pieces = [half[c * 24 : c * 24 + 24] for half in halves]
        spec.append(jnp.concatenate(pieces, axis=0))
    for o in range(3):
        real = None
        imag = None
        for c in range(3):
            kr = kernel_ref[0, o, c, 0].astype(jnp.float32)
            ki = kernel_ref[1, o, c, 0].astype(jnp.float32)
            sr = spec[c][:, :NP]
            si = spec[c][:, NP:]
            r = kr * sr - ki * si
            i = kr * si + ki * sr
            real = r if real is None else real + r
            imag = i if imag is None else imag + i
        out_ref[0, o * 48 : o * 48 + 48, :] = real.astype(jnp.bfloat16)
        out_ref[0, 144 + o * 48 : 192 + o * 48, :] = imag.astype(jnp.bfloat16)


def modes_call(kernel, spec):
    return pl.pallas_call(
        modes_body,
        grid=(4,),
        in_specs=[
            pl.BlockSpec((2, 3, 3, 1, 48, NP), lambda j: (0, 0, 0, 0, j, 0)),
            pl.BlockSpec((2, 72, 512), lambda j: (j, 0, 0)),
        ],
        out_specs=pl.BlockSpec((1, 288, NP), lambda j: (j, 0, 0)),
        out_shape=jax.ShapeDtypeStruct((4, 288, NP), jnp.bfloat16),
        compiler_params=pltpu.CompilerParams(vmem_limit_bytes=VMEM),
        cost_estimate=pl.CostEstimate(flops=3600000, bytes_accessed=2950000, transcendentals=0),
        name="modes",
    )(kernel, spec)


def inverse_x_body(values_ref, table_ref, out_ref):
    values = jnp.concatenate([values_ref[s] for s in range(4)], axis=1)

    def block(j, carry):
        total = jnp.dot(values, table_ref[j], preferred_element_type=jnp.float32)
        total = total * (1.0 / 32.0)
        real = (total[:144, :128] - total[144:, 128:]).astype(jnp.bfloat16)
        imag = (total[:144, 128:] + total[144:, :128]).astype(jnp.bfloat16)
        for o in range(3):
            out_ref[j, 0:48, o * 128 : (o + 1) * 128] = real[o * 48 : (o + 1) * 48]
            out_ref[j, 48:96, o * 128 : (o + 1) * 128] = imag[o * 48 : (o + 1) * 48]
        return carry

    lax.fori_loop(0, 8, block, 0, unroll=True)


def inverse_x_call(values, table):
    return pl.pallas_call(
        inverse_x_body,
        out_shape=jax.ShapeDtypeStruct((8, 96, 384), jnp.bfloat16),
        compiler_params=pltpu.CompilerParams(vmem_limit_bytes=VMEM),
        cost_estimate=pl.CostEstimate(flops=1208000000, bytes_accessed=5400000, transcendentals=0),
        name="inverse_x",
    )(values, table)


def inverse_z_body(steps, me_ref, values_ref, table_ref, *out_refs):
    me = me_ref[0]
    values = values_ref[...]
    odd = (lax.broadcasted_iota(jnp.int32, (NQ, 384), 0) * (me // 2)) % 2
    scale = jnp.where(odd == 1, -1.0, 1.0) * (1.0 / math.sqrt(NZ))
    for k, out_ref in zip(steps, out_refs):
        total = jnp.dot(table_ref[me ^ k], values, preferred_element_type=jnp.float32)
        out_ref[...] = (total * scale).astype(out_ref.dtype)


def inverse_z_call(me, values, table, steps):
    block = pl.BlockSpec((NQ, 384), lambda j, s: (0, 0))
    return pl.pallas_call(
        functools.partial(inverse_z_body, steps),
        grid_spec=pltpu.PrefetchScalarGridSpec(
            num_scalar_prefetch=1,
            grid=(1,),
            in_specs=[
                pl.BlockSpec((NZ, 384), lambda j, s: (0, 0)),
                pl.BlockSpec((4, NQ, NZ), lambda j, s: (0, 0, 0)),
            ],
            out_specs=[block] * 2,
        ),
        out_shape=[jax.ShapeDtypeStruct((NQ, 384), jnp.bfloat16) for _ in range(2)],
        compiler_params=pltpu.CompilerParams(vmem_limit_bytes=VMEM),
        cost_estimate=pl.CostEstimate(flops=227000000, bytes_accessed=2000000, transcendentals=0),
        name="inverse_z_far" if steps[0] else "inverse_z_near",
    )(me, values, table)


def finish_body(core_ref, own_ref, far_own_ref, near_ref, far_near_ref, out_ref):
    own = own_ref[...].astype(jnp.float32) + far_own_ref[...].astype(jnp.float32)
    near = near_ref[...].astype(jnp.float32) + far_near_ref[...].astype(jnp.float32)
    first = core_ref[0] == 0
    left = jnp.where(first, own, near).astype(jnp.bfloat16)
    right = jnp.where(first, near, own).astype(jnp.bfloat16)
    for o in range(3):
        out_ref[o, 0, :, 0:128] = left[:, o * 128 : (o + 1) * 128]
        out_ref[o, 0, :, 128:256] = right[:, o * 128 : (o + 1) * 128]


def finish_call(core, own, far_own, near, far_near):
    block = pl.BlockSpec((NQ, 384), lambda j, s: (0, 0))
    return pl.pallas_call(
        finish_body,
        grid_spec=pltpu.PrefetchScalarGridSpec(
            num_scalar_prefetch=1,
            grid=(1,),
            in_specs=[block] * 4,
            out_specs=pl.BlockSpec((3, 1, NQ, NP), lambda j, s: (0, 0, 0, 0)),
        ),
        out_shape=jax.ShapeDtypeStruct((3, 1, NQ, NP), jnp.bfloat16),
        compiler_params=pltpu.CompilerParams(vmem_limit_bytes=VMEM),
        cost_estimate=pl.CostEstimate(flops=150000, bytes_accessed=900000, transcendentals=0),
        name="finish",
    )(core, own, far_own, near, far_near)


def exchange(values, axis):
    return lax.all_to_all(values, axis, split_axis=0, concat_axis=0, tiled=True)


def swap_cores(values):
    return lax.ppermute(values, "core", [(0, 1), (1, 0)])


def move_z(values, step, flip):
    def position(z, core):
        return (z % 8) * 4 + (z // 8) * 2 + core

    perm = []
    for z in range(16):
        for core in range(2):
            target = (z + (step if core == 0 else -step)) % 16
            perm.append((position(z, core), position(target, core ^ flip)))
    return lax.ppermute(values, ("z_lo", "z_hi", "core"), perm)


def per_device(wall, kernel):
    core = lax.axis_index("core")
    gz = (lax.axis_index("z_hi") * 2 + core).reshape(1).astype(jnp.int32)

    rows, z_table = pack_call(wall, jnp.asarray(forward_z_table()))
    rows = exchange(rows, ("z_lo", "z_hi"))
    other = swap_cores(rows)
    z_spectra = forward_z_call(gz, other, z_table, forward_z_call(gz, rows, z_table, None))
    z_spectra = exchange(z_spectra, ("y", "gx_pair", "gx_in"))
    spec = exchange(forward_x_call(z_spectra, jnp.asarray(forward_x_table())), ("y", "gx_in"))

    modes = exchange(modes_call(kernel, spec), ("gx_pair", "gx_in"))
    planes = exchange(inverse_x_call(modes, jnp.asarray(inverse_x_table())), ("gx_pair", "gx_in", "core"))
    planes = planes.reshape(NZ, 384)
    z_table = jnp.asarray(inverse_z_table())
    to_far, to_far_near = inverse_z_call(gz, planes, z_table, (2, 3))
    own, to_near = inverse_z_call(gz, planes, z_table, (0, 1))
    far_own = move_z(move_z(to_far, 4, 0), 4, 0)
    far_near = move_z(move_z(to_far_near, 4, 1), -4, 0)
    near = swap_cores(to_near)
    return finish_call(core.reshape(1).astype(jnp.int32), own, far_own, near, far_near)


def solution(mesh):
    fine = Mesh(
        mesh.devices.reshape(8, 4, 2, 2, 2, 2),
        ("z_lo", "y", "gx_pair", "gx_in", "z_hi", "core"),
    )
    gx, gz = ("gx_pair", "gx_in"), ("z_hi", "core")
    return jax.shard_map(
        per_device,
        mesh=fine,
        in_specs=(
            P(None, ("z_lo", "y") + gx, gz),
            P(None, None, None, ("z_lo", "y"), gz, gx),
        ),
        out_specs=P(None, ("z_lo", "y"), gz, gx),
        check_vma=False,
    )
```

```python
import functools
import math

import jax
import jax.numpy as jnp
import numpy as np
from jax import lax
from jax.experimental import pallas as pl
from jax.experimental.pallas import tpu as pltpu
from jax.sharding import Mesh, PartitionSpec as P

NX = 1024
NZ = 768
NQ = 192
NP = 256
VMEM = 40 * 1024 * 1024


def angle(left, right, length):
    phase = (left[:, None].astype(np.int64) * right[None, :].astype(np.int64)) % length
    return phase * (2.0 * math.pi / length)


def forward_z_table():
    q = np.arange(NQ)
    theta = angle(q, q, NZ)
    both = np.stack([np.cos(theta), np.sin(theta)])
    main, tail = both[..., :128], both[..., 128:]
    zero = np.zeros_like(tail)
    return np.concatenate([tail, zero, main, zero, tail], axis=-1).astype(jnp.bfloat16)


def forward_x_table():
    source, y, low, r = np.meshgrid(
        np.arange(4), np.arange(4), np.arange(8), np.arange(8), indexing="ij"
    )
    x = (8 * (4 * (low * 4 + y) + source) + r).reshape(-1)
    theta = angle(x, np.arange(NP), NX).reshape(16, 64, NP)
    cos, sin = np.cos(theta), np.sin(theta)
    from_real = np.concatenate([cos, -sin], axis=2)
    from_imag = np.concatenate([sin, cos], axis=2)
    both = np.concatenate([from_real, from_imag], axis=1)
    return both.reshape(8, 256, 512).astype(jnp.bfloat16)


def inverse_x_table():
    theta = angle(np.arange(NX), np.arange(NX), NX).reshape(NX, 8, 128)
    both = np.concatenate([np.cos(theta), np.sin(theta)], axis=2)
    return np.transpose(both, (1, 0, 2)).astype(jnp.bfloat16)


def inverse_z_table():
    q = (
        192 * np.arange(2)[:, None, None]
        + 48 * np.arange(4)[None, :, None]
        + np.arange(48)[None, None, :]
    ).reshape(-1)
    theta = angle(np.arange(NZ), q, NZ).reshape(NZ, 8, 48)
    both = np.stack([np.cos(theta), -np.sin(theta)], axis=2)
    return both.reshape(4, NQ, NZ).astype(jnp.bfloat16)


def pack_body(wall_hbm, table_hbm, out_ref, kept_ref, wall_ref, sems):
    wall_copy = pltpu.make_async_copy(wall_hbm, wall_ref, sems.at[0])
    table_copy = pltpu.make_async_copy(table_hbm, kept_ref, sems.at[1])
    wall_copy.start()
    table_copy.start()
    wall_copy.wait()
    rows = [wall_ref[c].astype(jnp.float32) for c in range(3)]
    tails = [row[:, 128:] for row in rows] + [jnp.zeros((8, 64), jnp.float32)]
    pieces = [row[:, :128] for row in rows]
    for c in range(0, 4, 2):
        pieces.append(jnp.concatenate(tails[c : c + 2], axis=1))
    packed = jnp.concatenate(pieces, axis=0).astype(jnp.bfloat16)
    for k in range(16):
        out_ref[k] = packed
    table_copy.wait()


def pack_call(wall, table):
    return pl.pallas_call(
        pack_body,
        in_specs=[pl.BlockSpec(memory_space=pltpu.HBM)] * 2,
        scratch_shapes=[pltpu.VMEM((3, 8, NQ), jnp.bfloat16), pltpu.SemaphoreType.DMA((2,))],
        out_shape=[
            jax.ShapeDtypeStruct((16, 40, 128), jnp.bfloat16),
            jax.ShapeDtypeStruct((2, NQ, 384), jnp.bfloat16),
        ],
        compiler_params=pltpu.CompilerParams(vmem_limit_bytes=VMEM),
        cost_estimate=pl.CostEstimate(flops=10000, bytes_accessed=180000, transcendentals=0),
        name="pack",
    )(
        pltpu.with_memory_space_constraint(wall, pltpu.HBM),
        pltpu.with_memory_space_constraint(table, pltpu.HBM),
    )


def turned_lanes(values, turn):
    lane = lax.broadcasted_iota(jnp.int32, values.shape, 1)
    keep = jnp.where(turn == 0, 1.0, jnp.where(turn == 2, -1.0, 0.0))
    swap = jnp.where(turn == 1, 1.0, jnp.where(turn == 3, -1.0, 0.0))
    swap = jnp.where(lane < 64, swap, -swap)
    return values * keep + pltpu.roll(values, 64, axis=1) * swap


def partial_z(me, rows_ref, table_ref, step, c):
    turn = (me * lax.broadcasted_iota(jnp.int32, (64, 256), 1)) % 4
    to_real = jnp.where(turn == 0, 1.0, jnp.where(turn == 2, -1.0, 0.0))
    to_imag = jnp.where(turn == 3, 1.0, jnp.where(turn == 1, -1.0, 0.0))
    row = lax.broadcasted_iota(jnp.int32, (NQ, 128), 0)
    core = me % 2
    result = None
    for high in range(2):
        position = high * 2 + (core if step == 0 else 1 - core)
        blocks = [rows_ref[high * 8 + low].astype(jnp.float32) for low in range(8)]
        main = jnp.concatenate([block[c * 8 : c * 8 + 8] for block in blocks], axis=0)
        start = 24 + (c // 2) * 8
        tail = jnp.concatenate([block[start : start + 8] for block in blocks], axis=0)
        both = [main, tail] if c == 1 else [tail, main]
        rows = jnp.concatenate(both, axis=1)
        real = rows * to_real
        imag = rows * to_imag
        by_cos = jnp.concatenate([real, imag], axis=0).astype(jnp.bfloat16)
        by_sin = jnp.concatenate([imag, -real], axis=0).astype(jnp.bfloat16)
        lanes = slice(128, 384) if c == 1 else slice(0, 256)
        total = jnp.zeros((NQ, 128), jnp.float32)
        for part, values in enumerate((by_cos, by_sin)):
            total = total + lax.dot_general(
                table_ref[part, :, lanes],
                values,
                (((1,), (1,)), ((), ())),
                preferred_element_type=jnp.float32,
            )
        total = turned_lanes(total, (position * row) % 4)
        result = total if result is None else result + total
    return result


def forward_z_own_body(me_ref, rows_ref, table_ref, out_ref):
    for c in range(3):
        out_ref[c] = partial_z(me_ref[0], rows_ref, table_ref, 0, c)


def forward_z_body(me_ref, rows_ref, table_ref, own_ref, out_ref):
    lane = lax.broadcasted_iota(jnp.int32, (NQ, 128), 1)
    totals = []
    for c in range(3):
        total = own_ref[c] + partial_z(me_ref[0], rows_ref, table_ref, 1, c)
        totals.append(total * (1.0 / math.sqrt(NZ)))
    for pair in range(2):
        if pair:
            totals = [jnp.where(lane % 2 == 1, -total, total) for total in totals]
        for y in range(4):
            for half in range(2):
                start = y * 48 + half * 24
                pieces = [total[start : start + 24] for total in totals]
                block = jnp.concatenate(pieces, axis=0).astype(jnp.bfloat16)
                out_ref[pair * 8 + half * 4 + y] = block


def forward_z_call(me, rows, table, own):
    rows_spec = pl.BlockSpec((16, 40, 128), lambda j, s: (0, 0, 0))
    table_spec = pl.BlockSpec((2, NQ, 384), lambda j, s: (0, 0, 0))
    own_spec = pl.BlockSpec((3, NQ, 128), lambda j, s: (0, 0, 0))
    out_spec = pl.BlockSpec((16, 72, 128), lambda j, s: (0, 0, 0))
    first = own is None
    return pl.pallas_call(
        forward_z_own_body if first else forward_z_body,
        grid_spec=pltpu.PrefetchScalarGridSpec(
            num_scalar_prefetch=1,
            grid=(1,),
            in_specs=[rows_spec, table_spec] + ([] if first else [own_spec]),
            out_specs=own_spec if first else out_spec,
        ),
        out_shape=jax.ShapeDtypeStruct((3, NQ, 128), jnp.float32)
        if first
        else jax.ShapeDtypeStruct((16, 72, 128), jnp.bfloat16),
        compiler_params=pltpu.CompilerParams(vmem_limit_bytes=VMEM),
        cost_estimate=pl.CostEstimate(flops=151000000, bytes_accessed=1700000, transcendentals=0),
        name="forward_z_own" if first else "forward_z",
    )(me, rows, table, *([] if first else [own]))


def forward_x_body(values_ref, table_ref, out_ref):
    turn = lax.broadcasted_iota(jnp.int32, (72, 128), 1) % 4
    total = jnp.zeros((144, 512), jnp.float32)
    for k in range(8):
        first = [values_ref[2 * k + i].astype(jnp.float32) for i in range(2)]
        second = [turned_lanes(value, turn) for value in first]
        both = [jnp.concatenate(pieces, axis=1) for pieces in (first, second)]
        both = jnp.concatenate(both, axis=0).astype(jnp.bfloat16)
        total = total + jnp.dot(both, table_ref[k], preferred_element_type=jnp.float32)
    total = total * (1.0 / 32.0)
    for half in range(2):
        block = total[half * 72 : half * 72 + 72].astype(jnp.bfloat16)
        for y in range(4):
            out_ref[half * 4 + y] = block


def forward_x_call(values, table):
    return pl.pallas_call(
        forward_x_body,
        out_shape=jax.ShapeDtypeStruct((8, 72, 512), jnp.bfloat16),
        compiler_params=pltpu.CompilerParams(vmem_limit_bytes=VMEM),
        cost_estimate=pl.CostEstimate(flops=302000000, bytes_accessed=3000000, transcendentals=0),
        name="forward_x",
    )(values, table)


def modes_body(kernel_ref, spec_ref, out_ref):
    halves = [spec_ref[half, 0].astype(jnp.float32) for half in range(2)]
    spec = []
    for c in range(3):
        pieces = [half[c * 24 : c * 24 + 24] for half in halves]
        spec.append(jnp.concatenate(pieces, axis=0))
    for o in range(3):
        real = None
        imag = None
        for c in range(3):
            kr = kernel_ref[0, o, c, 0].astype(jnp.float32)
            ki = kernel_ref[1, o, c, 0].astype(jnp.float32)
            sr = spec[c][:, :NP]
            si = spec[c][:, NP:]
            r = kr * sr - ki * si
            i = kr * si + ki * sr
            real = r if real is None else real + r
            imag = i if imag is None else imag + i
        out_ref[0, o * 48 : o * 48 + 48, :] = real.astype(jnp.bfloat16)
        out_ref[0, 144 + o * 48 : 192 + o * 48, :] = imag.astype(jnp.bfloat16)


def modes_call(kernel, spec):
    return pl.pallas_call(
        modes_body,
        grid=(4,),
        in_specs=[
            pl.BlockSpec((2, 3, 3, 1, 48, NP), lambda j: (0, 0, 0, 0, j, 0)),
            pl.BlockSpec((2, 1, 72, 512), lambda j: (0, j, 0, 0)),
        ],
        out_specs=pl.BlockSpec((1, 288, NP), lambda j: (j, 0, 0)),
        out_shape=jax.ShapeDtypeStruct((4, 288, NP), jnp.bfloat16),
        compiler_params=pltpu.CompilerParams(vmem_limit_bytes=VMEM),
        cost_estimate=pl.CostEstimate(flops=3600000, bytes_accessed=2950000, transcendentals=0),
        name="modes",
    )(kernel, spec)


def inverse_x_body(values_ref, table_ref, out_ref):
    values = jnp.concatenate([values_ref[s] for s in range(4)], axis=1)

    def block(j, carry):
        total = jnp.dot(values, table_ref[j], preferred_element_type=jnp.float32)
        total = total * (1.0 / 32.0)
        real = (total[:144, :128] - total[144:, 128:]).astype(jnp.bfloat16)
        imag = (total[:144, 128:] + total[144:, :128]).astype(jnp.bfloat16)
        for o in range(3):
            out_ref[(j % 2) * 4 + j // 2, 0:48, o * 128 : (o + 1) * 128] = real[o * 48 : (o + 1) * 48]
            out_ref[(j % 2) * 4 + j // 2, 48:96, o * 128 : (o + 1) * 128] = imag[o * 48 : (o + 1) * 48]
        return carry

    lax.fori_loop(0, 8, block, 0, unroll=True)


def inverse_x_call(values, table):
    return pl.pallas_call(
        inverse_x_body,
        out_shape=jax.ShapeDtypeStruct((8, 96, 384), jnp.bfloat16),
        compiler_params=pltpu.CompilerParams(vmem_limit_bytes=VMEM),
        cost_estimate=pl.CostEstimate(flops=1208000000, bytes_accessed=5400000, transcendentals=0),
        name="inverse_x",
    )(values, table)


def inverse_z_body(steps, me_ref, values_ref, table_ref, *out_refs):
    me = me_ref[0]
    values = values_ref[...]
    odd = (lax.broadcasted_iota(jnp.int32, (NQ, 384), 0) * (me // 2)) % 2
    scale = jnp.where(odd == 1, -1.0, 1.0) * (1.0 / math.sqrt(NZ))
    for k, out_ref in zip(steps, out_refs):
        total = jnp.dot(table_ref[me ^ k], values, preferred_element_type=jnp.float32)
        out_ref[...] = (total * scale).astype(out_ref.dtype)


def inverse_z_call(me, values, table, steps):
    block = pl.BlockSpec((NQ, 384), lambda j, s: (0, 0))
    return pl.pallas_call(
        functools.partial(inverse_z_body, steps),
        grid_spec=pltpu.PrefetchScalarGridSpec(
            num_scalar_prefetch=1,
            grid=(1,),
            in_specs=[
                pl.BlockSpec((NZ, 384), lambda j, s: (0, 0)),
                pl.BlockSpec((4, NQ, NZ), lambda j, s: (0, 0, 0)),
            ],
            out_specs=[block] * len(steps),
        ),
        out_shape=[jax.ShapeDtypeStruct((NQ, 384), jnp.bfloat16) for _ in steps],
        compiler_params=pltpu.CompilerParams(vmem_limit_bytes=VMEM),
        cost_estimate=pl.CostEstimate(flops=227000000, bytes_accessed=2000000, transcendentals=0),
        name="inverse_z_far" if steps[0] else "inverse_z_near",
    )(me, values, table)


def finish_body(core_ref, own_ref, far_own_ref, near_ref, far_near_ref, out_ref):
    own = own_ref[...].astype(jnp.float32) + far_own_ref[...].astype(jnp.float32)
    near = near_ref[...].astype(jnp.float32) + far_near_ref[...].astype(jnp.float32)
    first = core_ref[0] == 0
    left = jnp.where(first, own, near).astype(jnp.bfloat16)
    right = jnp.where(first, near, own).astype(jnp.bfloat16)
    for o in range(3):
        out_ref[o, 0, :, 0:128] = left[:, o * 128 : (o + 1) * 128]
        out_ref[o, 0, :, 128:256] = right[:, o * 128 : (o + 1) * 128]


def finish_call(core, own, far_own, near, far_near):
    block = pl.BlockSpec((NQ, 384), lambda j, s: (0, 0))
    return pl.pallas_call(
        finish_body,
        grid_spec=pltpu.PrefetchScalarGridSpec(
            num_scalar_prefetch=1,
            grid=(1,),
            in_specs=[block] * 4,
            out_specs=pl.BlockSpec((3, 1, NQ, NP), lambda j, s: (0, 0, 0, 0)),
        ),
        out_shape=jax.ShapeDtypeStruct((3, 1, NQ, NP), jnp.bfloat16),
        compiler_params=pltpu.CompilerParams(vmem_limit_bytes=VMEM),
        cost_estimate=pl.CostEstimate(flops=150000, bytes_accessed=900000, transcendentals=0),
        name="finish",
    )(core, own, far_own, near, far_near)


def exchange(values, axis):
    return lax.all_to_all(values, axis, split_axis=0, concat_axis=0, tiled=True)


def swap_cores(values):
    return lax.ppermute(values, "core", [(0, 1), (1, 0)])


def move_z(values, step, flip):
    def position(z, core):
        return (z % 8) * 4 + (z // 8) * 2 + core

    perm = []
    for z in range(16):
        for core in range(2):
            target = (z + (step if core == 0 else -step)) % 16
            perm.append((position(z, core), position(target, core ^ flip)))
    return lax.ppermute(values, ("z_lo", "z_hi", "core"), perm)


def per_device(wall, kernel):
    core = lax.axis_index("core")
    gz = (lax.axis_index("z_hi") * 2 + core).reshape(1).astype(jnp.int32)

    rows, z_table = pack_call(wall, jnp.asarray(forward_z_table()))
    rows = exchange(rows, ("z_hi", "z_lo"))
    other = swap_cores(rows)
    z_spectra = forward_z_call(gz, other, z_table, forward_z_call(gz, rows, z_table, None))
    z_spectra = exchange(z_spectra, ("gx_pair", "gx_in", "y"))
    spec = exchange(forward_x_call(z_spectra, jnp.asarray(forward_x_table())), ("gx_in", "y"))

    modes = exchange(modes_call(kernel, spec.reshape(2, 4, 72, 512)), ("gx_pair", "gx_in"))
    planes = exchange(inverse_x_call(modes, jnp.asarray(inverse_x_table())), ("core", "gx_pair", "gx_in"))
    planes = planes.reshape(NZ, 384)
    z_table = jnp.asarray(inverse_z_table())
    (to_far,) = inverse_z_call(gz, planes, z_table, (2,))
    (to_far_near,) = inverse_z_call(gz, planes, z_table, (3,))
    own, to_near = inverse_z_call(gz, planes, z_table, (0, 1))
    far_own = move_z(move_z(to_far, 4, 0), 4, 0)
    far_near = move_z(move_z(to_far_near, 4, 0), 4, 1)
    near = swap_cores(to_near)
    return finish_call(core.reshape(1).astype(jnp.int32), own, far_own, near, far_near)


def solution(mesh):
    fine = Mesh(
        mesh.devices.reshape(8, 4, 2, 2, 2, 2),
        ("z_lo", "y", "gx_pair", "gx_in", "z_hi", "core"),
    )
    gx, gz = ("gx_pair", "gx_in"), ("z_hi", "core")
    return jax.shard_map(
        per_device,
        mesh=fine,
        in_specs=(
            P(None, ("z_lo", "y") + gx, gz),
            P(None, None, None, ("z_lo", "y"), gz, gx),
        ),
        out_specs=P(None, ("z_lo", "y"), gz, gx),
        check_vma=False,
    )
```

```python
import functools
import math

import jax
import jax.numpy as jnp
import numpy as np
from jax import lax
from jax.experimental import pallas as pl
from jax.experimental.pallas import tpu as pltpu
from jax.sharding import Mesh, PartitionSpec as P

NX = 1024
NZ = 768
NQ = 192
NP = 256
VMEM = 40 * 1024 * 1024


def angle(left, right, length):
    phase = (left[:, None].astype(np.int64) * right[None, :].astype(np.int64)) % length
    return phase * (2.0 * math.pi / length)


def forward_z_table():
    q = np.arange(NQ)
    theta = angle(q, q, NZ)
    both = np.stack([np.cos(theta), np.sin(theta)])
    main, tail = both[..., :128], both[..., 128:]
    zero = np.zeros_like(tail)
    return np.concatenate([tail, zero, main, zero, tail], axis=-1).astype(jnp.bfloat16)


def forward_x_table():
    source, y, low, r = np.meshgrid(
        np.arange(4), np.arange(4), np.arange(8), np.arange(8), indexing="ij"
    )
    x = (8 * (4 * (low * 4 + y) + source) + r).reshape(-1)
    theta = angle(x, np.arange(NP), NX).reshape(16, 64, NP)
    cos, sin = np.cos(theta), np.sin(theta)
    from_real = np.concatenate([cos, -sin], axis=2)
    from_imag = np.concatenate([sin, cos], axis=2)
    both = np.concatenate([from_real, from_imag], axis=1)
    return both.reshape(8, 256, 512).astype(jnp.bfloat16)


def inverse_x_table():
    theta = angle(np.arange(NX), np.arange(NX), NX).reshape(NX, 8, 128)
    both = np.concatenate([np.cos(theta), np.sin(theta)], axis=2)
    return np.transpose(both, (1, 0, 2)).astype(jnp.bfloat16)


def inverse_z_table():
    q = (
        192 * np.arange(2)[:, None, None]
        + 48 * np.arange(4)[None, :, None]
        + np.arange(48)[None, None, :]
    ).reshape(-1)
    theta = angle(np.arange(NZ), q, NZ).reshape(NZ, 8, 48)
    both = np.stack([np.cos(theta), -np.sin(theta)], axis=2)
    return both.reshape(4, NQ, NZ).astype(jnp.bfloat16)


def pack_body(wall_hbm, table_hbm, out_ref, kept_ref, wall_ref, sems):
    wall_copy = pltpu.make_async_copy(wall_hbm, wall_ref, sems.at[0])
    table_copy = pltpu.make_async_copy(table_hbm, kept_ref, sems.at[1])
    wall_copy.start()
    table_copy.start()
    wall_copy.wait()
    rows = [wall_ref[c].astype(jnp.float32) for c in range(3)]
    tails = [row[:, 128:] for row in rows] + [jnp.zeros((8, 64), jnp.float32)]
    pieces = [row[:, :128] for row in rows]
    for c in range(0, 4, 2):
        pieces.append(jnp.concatenate(tails[c : c + 2], axis=1))
    packed = jnp.concatenate(pieces, axis=0).astype(jnp.bfloat16)
    for k in range(16):
        out_ref[k] = packed
    table_copy.wait()


def pack_call(wall, table):
    return pl.pallas_call(
        pack_body,
        in_specs=[pl.BlockSpec(memory_space=pltpu.HBM)] * 2,
        scratch_shapes=[pltpu.VMEM((3, 8, NQ), jnp.bfloat16), pltpu.SemaphoreType.DMA((2,))],
        out_shape=[
            jax.ShapeDtypeStruct((16, 40, 128), jnp.bfloat16),
            jax.ShapeDtypeStruct((2, NQ, 384), jnp.bfloat16),
        ],
        compiler_params=pltpu.CompilerParams(vmem_limit_bytes=VMEM),
        cost_estimate=pl.CostEstimate(flops=10000, bytes_accessed=180000, transcendentals=0),
        name="pack",
    )(
        pltpu.with_memory_space_constraint(wall, pltpu.HBM),
        pltpu.with_memory_space_constraint(table, pltpu.HBM),
    )


def turned_lanes(values, turn):
    lane = lax.broadcasted_iota(jnp.int32, values.shape, 1)
    keep = jnp.where(turn == 0, 1.0, jnp.where(turn == 2, -1.0, 0.0))
    swap = jnp.where(turn == 1, 1.0, jnp.where(turn == 3, -1.0, 0.0))
    swap = jnp.where(lane < 64, swap, -swap)
    return values * keep + pltpu.roll(values, 64, axis=1) * swap


def partial_z(me, rows_ref, table_ref, step, c):
    turn = (me * lax.broadcasted_iota(jnp.int32, (64, 256), 1)) % 4
    to_real = jnp.where(turn == 0, 1.0, jnp.where(turn == 2, -1.0, 0.0))
    to_imag = jnp.where(turn == 3, 1.0, jnp.where(turn == 1, -1.0, 0.0))
    row = lax.broadcasted_iota(jnp.int32, (NQ, 128), 0)
    core = me % 2
    result = None
    for high in range(2):
        position = high * 2 + (core if step == 0 else 1 - core)
        blocks = [rows_ref[low * 2 + high].astype(jnp.float32) for low in range(8)]
        main = jnp.concatenate([block[c * 8 : c * 8 + 8] for block in blocks], axis=0)
        start = 24 + (c // 2) * 8
        tail = jnp.concatenate([block[start : start + 8] for block in blocks], axis=0)
        both = [main, tail] if c == 1 else [tail, main]
        rows = jnp.concatenate(both, axis=1)
        real = rows * to_real
        imag = rows * to_imag
        by_cos = jnp.concatenate([real, imag], axis=0).astype(jnp.bfloat16)
        by_sin = jnp.concatenate([imag, -real], axis=0).astype(jnp.bfloat16)
        lanes = slice(128, 384) if c == 1 else slice(0, 256)
        total = jnp.zeros((NQ, 128), jnp.float32)
        for part, values in enumerate((by_cos, by_sin)):
            total = total + lax.dot_general(
                table_ref[part, :, lanes],
                values,
                (((1,), (1,)), ((), ())),
                preferred_element_type=jnp.float32,
            )
        total = turned_lanes(total, (position * row) % 4)
        result = total if result is None else result + total
    return result


def forward_z_own_body(me_ref, rows_ref, table_ref, out_ref):
    for c in range(3):
        out_ref[c] = partial_z(me_ref[0], rows_ref, table_ref, 0, c)


def forward_z_body(me_ref, rows_ref, table_ref, own_ref, out_ref):
    lane = lax.broadcasted_iota(jnp.int32, (NQ, 128), 1)
    totals = []
    for c in range(3):
        total = own_ref[c] + partial_z(me_ref[0], rows_ref, table_ref, 1, c)
        totals.append(total * (1.0 / math.sqrt(NZ)))
    for pair in range(2):
        if pair:
            totals = [jnp.where(lane % 2 == 1, -total, total) for total in totals]
        for y in range(4):
            for half in range(2):
                start = y * 48 + half * 24
                pieces = [total[start : start + 24] for total in totals]
                block = jnp.concatenate(pieces, axis=0).astype(jnp.bfloat16)
                out_ref[pair * 8 + half * 4 + y] = block


def forward_z_call(me, rows, table, own):
    rows_spec = pl.BlockSpec((16, 40, 128), lambda j, s: (0, 0, 0))
    table_spec = pl.BlockSpec((2, NQ, 384), lambda j, s: (0, 0, 0))
    own_spec = pl.BlockSpec((3, NQ, 128), lambda j, s: (0, 0, 0))
    out_spec = pl.BlockSpec((16, 72, 128), lambda j, s: (0, 0, 0))
    first = own is None
    return pl.pallas_call(
        forward_z_own_body if first else forward_z_body,
        grid_spec=pltpu.PrefetchScalarGridSpec(
            num_scalar_prefetch=1,
            grid=(1,),
            in_specs=[rows_spec, table_spec] + ([] if first else [own_spec]),
            out_specs=own_spec if first else out_spec,
        ),
        out_shape=jax.ShapeDtypeStruct((3, NQ, 128), jnp.float32)
        if first
        else jax.ShapeDtypeStruct((16, 72, 128), jnp.bfloat16),
        compiler_params=pltpu.CompilerParams(vmem_limit_bytes=VMEM),
        cost_estimate=pl.CostEstimate(flops=151000000, bytes_accessed=1700000, transcendentals=0),
        name="forward_z_own" if first else "forward_z",
    )(me, rows, table, *([] if first else [own]))


def forward_x_body(values_ref, table_ref, out_ref):
    turn = lax.broadcasted_iota(jnp.int32, (72, 128), 1) % 4
    total = jnp.zeros((144, 512), jnp.float32)
    for k in range(8):
        first = [values_ref[2 * k + i].astype(jnp.float32) for i in range(2)]
        second = [turned_lanes(value, turn) for value in first]
        both = [jnp.concatenate(pieces, axis=1) for pieces in (first, second)]
        both = jnp.concatenate(both, axis=0).astype(jnp.bfloat16)
        total = total + jnp.dot(both, table_ref[k], preferred_element_type=jnp.float32)
    total = total * (1.0 / 32.0)
    for half in range(2):
        block = total[half * 72 : half * 72 + 72].astype(jnp.bfloat16)
        for y in range(4):
            out_ref[half * 4 + y] = block


def forward_x_call(values, table):
    return pl.pallas_call(
        forward_x_body,
        out_shape=jax.ShapeDtypeStruct((8, 72, 512), jnp.bfloat16),
        compiler_params=pltpu.CompilerParams(vmem_limit_bytes=VMEM),
        cost_estimate=pl.CostEstimate(flops=302000000, bytes_accessed=3000000, transcendentals=0),
        name="forward_x",
    )(values, table)


def modes_body(kernel_ref, spec_ref, out_ref):
    halves = [spec_ref[half, 0].astype(jnp.float32) for half in range(2)]
    spec = []
    for c in range(3):
        pieces = [half[c * 24 : c * 24 + 24] for half in halves]
        spec.append(jnp.concatenate(pieces, axis=0))
    for o in range(3):
        real = None
        imag = None
        for c in range(3):
            kr = kernel_ref[0, o, c, 0].astype(jnp.float32)
            ki = kernel_ref[1, o, c, 0].astype(jnp.float32)
            sr = spec[c][:, :NP]
            si = spec[c][:, NP:]
            r = kr * sr - ki * si
            i = kr * si + ki * sr
            real = r if real is None else real + r
            imag = i if imag is None else imag + i
        out_ref[0, o * 48 : o * 48 + 48, :] = real.astype(jnp.bfloat16)
        out_ref[0, 144 + o * 48 : 192 + o * 48, :] = imag.astype(jnp.bfloat16)


def modes_call(kernel, spec):
    return pl.pallas_call(
        modes_body,
        grid=(4,),
        in_specs=[
            pl.BlockSpec((2, 3, 3, 1, 48, NP), lambda j: (0, 0, 0, 0, j, 0)),
            pl.BlockSpec((2, 1, 72, 512), lambda j: (0, j, 0, 0)),
        ],
        out_specs=pl.BlockSpec((1, 288, NP), lambda j: (j, 0, 0)),
        out_shape=jax.ShapeDtypeStruct((4, 288, NP), jnp.bfloat16),
        compiler_params=pltpu.CompilerParams(vmem_limit_bytes=VMEM),
        cost_estimate=pl.CostEstimate(flops=3600000, bytes_accessed=2950000, transcendentals=0),
        name="modes",
    )(kernel, spec)


def inverse_x_body(values_ref, table_ref, out_ref):
    values = jnp.concatenate([values_ref[s] for s in range(4)], axis=1)

    def block(j, carry):
        total = jnp.dot(values, table_ref[j], preferred_element_type=jnp.float32)
        total = total * (1.0 / 32.0)
        real = (total[:144, :128] - total[144:, 128:]).astype(jnp.bfloat16)
        imag = (total[:144, 128:] + total[144:, :128]).astype(jnp.bfloat16)
        for o in range(3):
            out_ref[(j % 2) * 4 + j // 2, 0:48, o * 128 : (o + 1) * 128] = real[o * 48 : (o + 1) * 48]
            out_ref[(j % 2) * 4 + j // 2, 48:96, o * 128 : (o + 1) * 128] = imag[o * 48 : (o + 1) * 48]
        return carry

    lax.fori_loop(0, 8, block, 0, unroll=True)


def inverse_x_call(values, table):
    return pl.pallas_call(
        inverse_x_body,
        out_shape=jax.ShapeDtypeStruct((8, 96, 384), jnp.bfloat16),
        compiler_params=pltpu.CompilerParams(vmem_limit_bytes=VMEM),
        cost_estimate=pl.CostEstimate(flops=1208000000, bytes_accessed=5400000, transcendentals=0),
        name="inverse_x",
    )(values, table)


def inverse_z_body(steps, me_ref, values_ref, table_ref, *out_refs):
    me = me_ref[0]
    values = values_ref[...]
    odd = (lax.broadcasted_iota(jnp.int32, (NQ, 384), 0) * (me // 2)) % 2
    scale = jnp.where(odd == 1, -1.0, 1.0) * (1.0 / math.sqrt(NZ))
    for k, out_ref in zip(steps, out_refs):
        total = jnp.dot(table_ref[me ^ k], values, preferred_element_type=jnp.float32)
        out_ref[...] = (total * scale).astype(out_ref.dtype)


def inverse_z_call(me, values, table, steps):
    block = pl.BlockSpec((NQ, 384), lambda j, s: (0, 0))
    return pl.pallas_call(
        functools.partial(inverse_z_body, steps),
        grid_spec=pltpu.PrefetchScalarGridSpec(
            num_scalar_prefetch=1,
            grid=(1,),
            in_specs=[
                pl.BlockSpec((NZ, 384), lambda j, s: (0, 0)),
                pl.BlockSpec((4, NQ, NZ), lambda j, s: (0, 0, 0)),
            ],
            out_specs=[block] * len(steps),
        ),
        out_shape=[jax.ShapeDtypeStruct((NQ, 384), jnp.bfloat16) for _ in steps],
        compiler_params=pltpu.CompilerParams(vmem_limit_bytes=VMEM),
        cost_estimate=pl.CostEstimate(flops=227000000, bytes_accessed=2000000, transcendentals=0),
        name="inverse_z_far" if steps[0] else "inverse_z_near",
    )(me, values, table)


def finish_body(core_ref, own_ref, far_own_ref, near_ref, far_near_ref, out_ref):
    own = own_ref[...].astype(jnp.float32) + far_own_ref[...].astype(jnp.float32)
    near = near_ref[...].astype(jnp.float32) + far_near_ref[...].astype(jnp.float32)
    first = core_ref[0] == 0
    left = jnp.where(first, own, near).astype(jnp.bfloat16)
    right = jnp.where(first, near, own).astype(jnp.bfloat16)
    for o in range(3):
        out_ref[o, 0, :, 0:128] = left[:, o * 128 : (o + 1) * 128]
        out_ref[o, 0, :, 128:256] = right[:, o * 128 : (o + 1) * 128]


def finish_call(core, own, far_own, near, far_near):
    block = pl.BlockSpec((NQ, 384), lambda j, s: (0, 0))
    return pl.pallas_call(
        finish_body,
        grid_spec=pltpu.PrefetchScalarGridSpec(
            num_scalar_prefetch=1,
            grid=(1,),
            in_specs=[block] * 4,
            out_specs=pl.BlockSpec((3, 1, NQ, NP), lambda j, s: (0, 0, 0, 0)),
        ),
        out_shape=jax.ShapeDtypeStruct((3, 1, NQ, NP), jnp.bfloat16),
        compiler_params=pltpu.CompilerParams(vmem_limit_bytes=VMEM),
        cost_estimate=pl.CostEstimate(flops=150000, bytes_accessed=900000, transcendentals=0),
        name="finish",
    )(core, own, far_own, near, far_near)


def exchange(values, axis):
    return lax.all_to_all(values, axis, split_axis=0, concat_axis=0, tiled=True)


def swap_cores(values):
    return lax.ppermute(values, "core", [(0, 1), (1, 0)])


def move_z(values, step, flip):
    def position(z, core):
        return (z % 8) * 4 + (z // 8) * 2 + core

    perm = []
    for z in range(16):
        for core in range(2):
            target = (z + (step if core == 0 else -step)) % 16
            perm.append((position(z, core), position(target, core ^ flip)))
    return lax.ppermute(values, ("z_lo", "z_hi", "core"), perm)


def per_device(wall, kernel):
    core = lax.axis_index("core")
    gz = (lax.axis_index("z_hi") * 2 + core).reshape(1).astype(jnp.int32)

    rows, z_table = pack_call(wall, jnp.asarray(forward_z_table()))
    rows = exchange(rows, ("z_lo", "z_hi"))
    other = swap_cores(rows)
    z_spectra = forward_z_call(gz, other, z_table, forward_z_call(gz, rows, z_table, None))
    z_spectra = exchange(z_spectra, ("gx_pair", "gx_in", "y"))
    spec = exchange(forward_x_call(z_spectra, jnp.asarray(forward_x_table())), ("gx_in", "y"))

    modes = exchange(modes_call(kernel, spec.reshape(2, 4, 72, 512)), ("gx_pair", "gx_in"))
    planes = exchange(inverse_x_call(modes, jnp.asarray(inverse_x_table())), ("core", "gx_pair", "gx_in"))
    planes = planes.reshape(NZ, 384)
    z_table = jnp.asarray(inverse_z_table())
    (to_far,) = inverse_z_call(gz, planes, z_table, (2,))
    (to_far_near,) = inverse_z_call(gz, planes, z_table, (3,))
    own, to_near = inverse_z_call(gz, planes, z_table, (0, 1))
    far_own = move_z(move_z(to_far, 4, 0), 4, 0)
    far_near = move_z(move_z(to_far_near, 4, 0), 4, 1)
    near = swap_cores(to_near)
    return finish_call(core.reshape(1).astype(jnp.int32), own, far_own, near, far_near)


def solution(mesh):
    fine = Mesh(
        mesh.devices.reshape(8, 4, 2, 2, 2, 2),
        ("z_lo", "y", "gx_pair", "gx_in", "z_hi", "core"),
    )
    gx, gz = ("gx_pair", "gx_in"), ("z_hi", "core")
    return jax.shard_map(
        per_device,
        mesh=fine,
        in_specs=(
            P(None, ("z_lo", "y") + gx, gz),
            P(None, None, None, ("z_lo", "y"), gz, gx),
        ),
        out_specs=P(None, ("z_lo", "y"), gz, gx),
        check_vma=False,
    )
```

```python
import functools
import math

import jax
import jax.numpy as jnp
import numpy as np
from jax import lax
from jax.experimental import pallas as pl
from jax.experimental.pallas import tpu as pltpu
from jax.sharding import Mesh, PartitionSpec as P

NX = 1024
NZ = 768
NQ = 192
NP = 256
VMEM = 40 * 1024 * 1024


def angle(left, right, length):
    phase = (left[:, None].astype(np.int64) * right[None, :].astype(np.int64)) % length
    return phase * (2.0 * math.pi / length)


def forward_z_table():
    q = np.arange(NQ)
    theta = angle(q, q, NZ)
    both = np.stack([np.cos(theta), np.sin(theta)])
    main, tail = both[..., :128], both[..., 128:]
    zero = np.zeros_like(tail)
    return np.concatenate([tail, zero, main, zero, tail], axis=-1).astype(jnp.bfloat16)


def forward_x_table():
    source, y, low, r = np.meshgrid(
        np.arange(4), np.arange(4), np.arange(8), np.arange(8), indexing="ij"
    )
    x = (8 * (4 * (low * 4 + y) + source) + r).reshape(-1)
    theta = angle(x, np.arange(NP), NX).reshape(16, 64, NP)
    cos, sin = np.cos(theta), np.sin(theta)
    from_real = np.concatenate([cos, -sin], axis=2)
    from_imag = np.concatenate([sin, cos], axis=2)
    both = np.concatenate([from_real, from_imag], axis=1)
    return both.reshape(8, 256, 512).astype(jnp.bfloat16)


def inverse_x_table():
    theta = angle(np.arange(NX), np.arange(NX), NX).reshape(NX, 8, 128)
    both = np.concatenate([np.cos(theta), np.sin(theta)], axis=2)
    return np.transpose(both, (1, 0, 2)).astype(jnp.bfloat16)


def inverse_z_table():
    q = (
        192 * np.arange(2)[:, None, None]
        + 48 * np.arange(4)[None, :, None]
        + np.arange(48)[None, None, :]
    ).reshape(-1)
    theta = angle(np.arange(NZ), q, NZ).reshape(NZ, 8, 48)
    both = np.stack([np.cos(theta), -np.sin(theta)], axis=2)
    return both.reshape(4, NQ, NZ).astype(jnp.bfloat16)


def pack_body(wall_hbm, table_hbm, out_ref, kept_ref, wall_ref, sems):
    wall_copy = pltpu.make_async_copy(wall_hbm, wall_ref, sems.at[0])
    table_copy = pltpu.make_async_copy(table_hbm, kept_ref, sems.at[1])
    wall_copy.start()
    table_copy.start()
    wall_copy.wait()
    rows = [wall_ref[c].astype(jnp.float32) for c in range(3)]
    tails = [row[:, 128:] for row in rows] + [jnp.zeros((8, 64), jnp.float32)]
    pieces = [row[:, :128] for row in rows]
    for c in range(0, 4, 2):
        pieces.append(jnp.concatenate(tails[c : c + 2], axis=1))
    packed = jnp.concatenate(pieces, axis=0).astype(jnp.bfloat16)
    for k in range(16):
        out_ref[k] = packed
    table_copy.wait()


def pack_call(wall, table):
    return pl.pallas_call(
        pack_body,
        in_specs=[pl.BlockSpec(memory_space=pltpu.HBM)] * 2,
        scratch_shapes=[pltpu.VMEM((3, 8, NQ), jnp.bfloat16), pltpu.SemaphoreType.DMA((2,))],
        out_shape=[
            jax.ShapeDtypeStruct((16, 40, 128), jnp.bfloat16),
            jax.ShapeDtypeStruct((2, NQ, 384), jnp.bfloat16),
        ],
        compiler_params=pltpu.CompilerParams(vmem_limit_bytes=VMEM),
        cost_estimate=pl.CostEstimate(flops=10000, bytes_accessed=180000, transcendentals=0),
        name="pack",
    )(
        pltpu.with_memory_space_constraint(wall, pltpu.HBM),
        pltpu.with_memory_space_constraint(table, pltpu.HBM),
    )


def turned_lanes(values, turn):
    lane = lax.broadcasted_iota(jnp.int32, values.shape, 1)
    keep = jnp.where(turn == 0, 1.0, jnp.where(turn == 2, -1.0, 0.0))
    swap = jnp.where(turn == 1, 1.0, jnp.where(turn == 3, -1.0, 0.0))
    swap = jnp.where(lane < 64, swap, -swap)
    return values * keep + pltpu.roll(values, 64, axis=1) * swap


def partial_z(me, rows_ref, table_ref, step, c):
    turn = (me * lax.broadcasted_iota(jnp.int32, (64, 256), 1)) % 4
    to_real = jnp.where(turn == 0, 1.0, jnp.where(turn == 2, -1.0, 0.0))
    to_imag = jnp.where(turn == 3, 1.0, jnp.where(turn == 1, -1.0, 0.0))
    row = lax.broadcasted_iota(jnp.int32, (NQ, 128), 0)
    core = me % 2
    result = None
    for high in range(2):
        position = high * 2 + (core if step == 0 else 1 - core)
        blocks = [rows_ref[low * 2 + high].astype(jnp.float32) for low in range(8)]
        main = jnp.concatenate([block[c * 8 : c * 8 + 8] for block in blocks], axis=0)
        start = 24 + (c // 2) * 8
        tail = jnp.concatenate([block[start : start + 8] for block in blocks], axis=0)
        both = [main, tail] if c == 1 else [tail, main]
        rows = jnp.concatenate(both, axis=1)
        real = rows * to_real
        imag = rows * to_imag
        by_cos = jnp.concatenate([real, imag], axis=0).astype(jnp.bfloat16)
        by_sin = jnp.concatenate([imag, -real], axis=0).astype(jnp.bfloat16)
        lanes = slice(128, 384) if c == 1 else slice(0, 256)
        total = jnp.zeros((NQ, 128), jnp.float32)
        for part, values in enumerate((by_cos, by_sin)):
            total = total + lax.dot_general(
                table_ref[part, :, lanes],
                values,
                (((1,), (1,)), ((), ())),
                preferred_element_type=jnp.float32,
            )
        total = turned_lanes(total, (position * row) % 4)
        result = total if result is None else result + total
    return result


def forward_z_own_body(me_ref, rows_ref, table_ref, out_ref):
    for c in range(3):
        out_ref[c] = partial_z(me_ref[0], rows_ref, table_ref, 0, c)


def forward_z_body(me_ref, rows_ref, table_ref, own_ref, out_ref):
    lane = lax.broadcasted_iota(jnp.int32, (NQ, 128), 1)
    totals = []
    for c in range(3):
        total = own_ref[c] + partial_z(me_ref[0], rows_ref, table_ref, 1, c)
        totals.append(total * (1.0 / math.sqrt(NZ)))
    for pair in range(2):
        if pair:
            totals = [jnp.where(lane % 2 == 1, -total, total) for total in totals]
        for y in range(4):
            for half in range(2):
                start = y * 48 + half * 24
                pieces = [total[start : start + 24] for total in totals]
                block = jnp.concatenate(pieces, axis=0).astype(jnp.bfloat16)
                out_ref[pair * 8 + half * 4 + y] = block


def forward_z_call(me, rows, table, own):
    rows_spec = pl.BlockSpec((16, 40, 128), lambda j, s: (0, 0, 0))
    table_spec = pl.BlockSpec((2, NQ, 384), lambda j, s: (0, 0, 0))
    own_spec = pl.BlockSpec((3, NQ, 128), lambda j, s: (0, 0, 0))
    out_spec = pl.BlockSpec((16, 72, 128), lambda j, s: (0, 0, 0))
    first = own is None
    return pl.pallas_call(
        forward_z_own_body if first else forward_z_body,
        grid_spec=pltpu.PrefetchScalarGridSpec(
            num_scalar_prefetch=1,
            grid=(1,),
            in_specs=[rows_spec, table_spec] + ([] if first else [own_spec]),
            out_specs=own_spec if first else out_spec,
        ),
        out_shape=jax.ShapeDtypeStruct((3, NQ, 128), jnp.float32)
        if first
        else jax.ShapeDtypeStruct((16, 72, 128), jnp.bfloat16),
        compiler_params=pltpu.CompilerParams(vmem_limit_bytes=VMEM),
        cost_estimate=pl.CostEstimate(flops=151000000, bytes_accessed=1700000, transcendentals=0),
        name="forward_z_own" if first else "forward_z",
    )(me, rows, table, *([] if first else [own]))


def forward_x_body(values_ref, table_ref, out_ref):
    turn = lax.broadcasted_iota(jnp.int32, (72, 128), 1) % 4
    total = jnp.zeros((144, 512), jnp.float32)
    for k in range(8):
        first = [values_ref[2 * k + i].astype(jnp.float32) for i in range(2)]
        second = [turned_lanes(value, turn) for value in first]
        both = [jnp.concatenate(pieces, axis=1) for pieces in (first, second)]
        both = jnp.concatenate(both, axis=0).astype(jnp.bfloat16)
        total = total + jnp.dot(both, table_ref[k], preferred_element_type=jnp.float32)
    total = total * (1.0 / 32.0)
    for half in range(2):
        block = total[half * 72 : half * 72 + 72].astype(jnp.bfloat16)
        for y in range(4):
            out_ref[half * 4 + y] = block


def forward_x_call(values, table):
    return pl.pallas_call(
        forward_x_body,
        out_shape=jax.ShapeDtypeStruct((8, 72, 512), jnp.bfloat16),
        compiler_params=pltpu.CompilerParams(vmem_limit_bytes=VMEM),
        cost_estimate=pl.CostEstimate(flops=302000000, bytes_accessed=3000000, transcendentals=0),
        name="forward_x",
    )(values, table)


def modes_body(kernel_ref, spec_ref, out_ref):
    halves = [spec_ref[half, 0].astype(jnp.float32) for half in range(2)]
    spec = []
    for c in range(3):
        pieces = [half[c * 24 : c * 24 + 24] for half in halves]
        spec.append(jnp.concatenate(pieces, axis=0))
    for o in range(3):
        real = None
        imag = None
        for c in range(3):
            kr = kernel_ref[0, o, c, 0].astype(jnp.float32)
            ki = kernel_ref[1, o, c, 0].astype(jnp.float32)
            sr = spec[c][:, :NP]
            si = spec[c][:, NP:]
            r = kr * sr - ki * si
            i = kr * si + ki * sr
            real = r if real is None else real + r
            imag = i if imag is None else imag + i
        out_ref[0, o * 48 : o * 48 + 48, :] = real.astype(jnp.bfloat16)
        out_ref[0, 144 + o * 48 : 192 + o * 48, :] = imag.astype(jnp.bfloat16)


def modes_call(kernel, spec):
    return pl.pallas_call(
        modes_body,
        grid=(4,),
        in_specs=[
            pl.BlockSpec((2, 3, 3, 1, 48, NP), lambda j: (0, 0, 0, 0, j, 0)),
            pl.BlockSpec((2, 1, 72, 512), lambda j: (0, j, 0, 0)),
        ],
        out_specs=pl.BlockSpec((1, 288, NP), lambda j: (j, 0, 0)),
        out_shape=jax.ShapeDtypeStruct((4, 288, NP), jnp.bfloat16),
        compiler_params=pltpu.CompilerParams(vmem_limit_bytes=VMEM),
        cost_estimate=pl.CostEstimate(flops=3600000, bytes_accessed=2950000, transcendentals=0),
        name="modes",
    )(kernel, spec)


def inverse_x_body(values_ref, table_ref, out_ref):
    values = jnp.concatenate([values_ref[s] for s in range(4)], axis=1)

    def block(j, carry):
        total = jnp.dot(values, table_ref[j], preferred_element_type=jnp.float32)
        total = total * (1.0 / 32.0)
        real = (total[:144, :128] - total[144:, 128:]).astype(jnp.bfloat16)
        imag = (total[:144, 128:] + total[144:, :128]).astype(jnp.bfloat16)
        for o in range(3):
            out_ref[(j % 2) * 4 + j // 2, 0:48, o * 128 : (o + 1) * 128] = real[o * 48 : (o + 1) * 48]
            out_ref[(j % 2) * 4 + j // 2, 48:96, o * 128 : (o + 1) * 128] = imag[o * 48 : (o + 1) * 48]
        return carry

    lax.fori_loop(0, 8, block, 0, unroll=True)


def inverse_x_call(values, table):
    return pl.pallas_call(
        inverse_x_body,
        out_shape=jax.ShapeDtypeStruct((8, 96, 384), jnp.bfloat16),
        compiler_params=pltpu.CompilerParams(vmem_limit_bytes=VMEM),
        cost_estimate=pl.CostEstimate(flops=1208000000, bytes_accessed=5400000, transcendentals=0),
        name="inverse_x",
    )(values, table)


def inverse_z_body(steps, me_ref, values_ref, table_ref, *out_refs):
    me = me_ref[0]
    values = values_ref[...]
    odd = (lax.broadcasted_iota(jnp.int32, (NQ, 384), 0) * (me // 2)) % 2
    scale = jnp.where(odd == 1, -1.0, 1.0) * (1.0 / math.sqrt(NZ))
    for k, out_ref in zip(steps, out_refs):
        total = jnp.dot(table_ref[me ^ k], values, preferred_element_type=jnp.float32)
        out_ref[...] = (total * scale).astype(out_ref.dtype)


def inverse_z_call(me, values, table, steps):
    block = pl.BlockSpec((NQ, 384), lambda j, s: (0, 0))
    return pl.pallas_call(
        functools.partial(inverse_z_body, steps),
        grid_spec=pltpu.PrefetchScalarGridSpec(
            num_scalar_prefetch=1,
            grid=(1,),
            in_specs=[
                pl.BlockSpec((NZ, 384), lambda j, s: (0, 0)),
                pl.BlockSpec((4, NQ, NZ), lambda j, s: (0, 0, 0)),
            ],
            out_specs=[block] * len(steps),
        ),
        out_shape=[jax.ShapeDtypeStruct((NQ, 384), jnp.bfloat16) for _ in steps],
        compiler_params=pltpu.CompilerParams(vmem_limit_bytes=VMEM),
        cost_estimate=pl.CostEstimate(flops=227000000, bytes_accessed=2000000, transcendentals=0),
        name="inverse_z_far" if steps[0] else "inverse_z_near",
    )(me, values, table)


def finish_body(core_ref, near_ref, far_near_ref, own_ref, far_own_ref, out_ref):
    own = own_ref[...].astype(jnp.float32) + far_own_ref[...].astype(jnp.float32)
    near = near_ref[...].astype(jnp.float32) + far_near_ref[...].astype(jnp.float32)
    first = core_ref[0] == 0
    left = jnp.where(first, own, near).astype(jnp.bfloat16)
    right = jnp.where(first, near, own).astype(jnp.bfloat16)
    for o in range(3):
        out_ref[o, 0, :, 0:128] = left[:, o * 128 : (o + 1) * 128]
        out_ref[o, 0, :, 128:256] = right[:, o * 128 : (o + 1) * 128]


def finish_call(core, near, far_near, own, far_own):
    block = pl.BlockSpec((NQ, 384), lambda j, s: (0, 0))
    return pl.pallas_call(
        finish_body,
        grid_spec=pltpu.PrefetchScalarGridSpec(
            num_scalar_prefetch=1,
            grid=(1,),
            in_specs=[block] * 4,
            out_specs=pl.BlockSpec((3, 1, NQ, NP), lambda j, s: (0, 0, 0, 0)),
        ),
        out_shape=jax.ShapeDtypeStruct((3, 1, NQ, NP), jnp.bfloat16),
        compiler_params=pltpu.CompilerParams(vmem_limit_bytes=VMEM),
        cost_estimate=pl.CostEstimate(flops=150000, bytes_accessed=900000, transcendentals=0),
        name="finish",
    )(core, near, far_near, own, far_own)


def exchange(values, axis):
    return lax.all_to_all(values, axis, split_axis=0, concat_axis=0, tiled=True)


def swap_cores(values):
    return lax.ppermute(values, "core", [(0, 1), (1, 0)])


def move_z(values, step, flip):
    def position(z, core):
        return (z % 8) * 4 + (z // 8) * 2 + core

    perm = []
    for z in range(16):
        for core in range(2):
            target = (z + (step if core == 0 else -step)) % 16
            perm.append((position(z, core), position(target, core ^ flip)))
    return lax.ppermute(values, ("z_lo", "z_hi", "core"), perm)


def per_device(wall, kernel):
    core = lax.axis_index("core")
    gz = (lax.axis_index("z_hi") * 2 + core).reshape(1).astype(jnp.int32)

    rows, z_table = pack_call(wall, jnp.asarray(forward_z_table()))
    rows = exchange(rows, ("z_lo", "z_hi"))
    other = swap_cores(rows)
    z_spectra = forward_z_call(gz, other, z_table, forward_z_call(gz, rows, z_table, None))
    z_spectra = exchange(z_spectra, ("gx_pair", "gx_in", "y"))
    spec = exchange(forward_x_call(z_spectra, jnp.asarray(forward_x_table())), ("gx_in", "y"))

    modes = exchange(modes_call(kernel, spec.reshape(2, 4, 72, 512)), ("gx_pair", "gx_in"))
    planes = exchange(inverse_x_call(modes, jnp.asarray(inverse_x_table())), ("core", "gx_pair", "gx_in"))
    planes = planes.reshape(NZ, 384)
    z_table = jnp.asarray(inverse_z_table())
    (to_far_near,) = inverse_z_call(gz, planes, z_table, (3,))
    (to_far,) = inverse_z_call(gz, planes, z_table, (2,))
    own, to_near = inverse_z_call(gz, planes, z_table, (0, 1))
    far_near = move_z(move_z(to_far_near, 4, 0), 4, 1)
    far_own = move_z(move_z(to_far, 4, 0), 4, 0)
    near = swap_cores(to_near)
    return finish_call(core.reshape(1).astype(jnp.int32), near, far_near, own, far_own)


def solution(mesh):
    fine = Mesh(
        mesh.devices.reshape(8, 4, 2, 2, 2, 2),
        ("z_lo", "y", "gx_pair", "gx_in", "z_hi", "core"),
    )
    gx, gz = ("gx_pair", "gx_in"), ("z_hi", "core")
    return jax.shard_map(
        per_device,
        mesh=fine,
        in_specs=(
            P(None, ("z_lo", "y") + gx, gz),
            P(None, None, None, ("z_lo", "y"), gz, gx),
        ),
        out_specs=P(None, ("z_lo", "y"), gz, gx),
        check_vma=False,
    )
```

```python
import functools
import math

import jax
import jax.numpy as jnp
import numpy as np
from jax import lax
from jax.experimental import pallas as pl
from jax.experimental.pallas import tpu as pltpu
from jax.sharding import Mesh, PartitionSpec as P

NX = 1024
NZ = 768
NQ = 192
NP = 256
VMEM = 40 * 1024 * 1024


def angle(left, right, length):
    phase = (left[:, None].astype(np.int64) * right[None, :].astype(np.int64)) % length
    return phase * (2.0 * math.pi / length)


def forward_z_table():
    q = np.arange(NQ)
    theta = angle(q, q, NZ)
    both = np.stack([np.cos(theta), np.sin(theta)])
    main, tail = both[..., :128], both[..., 128:]
    zero = np.zeros_like(tail)
    return np.concatenate([tail, zero, main, zero, tail], axis=-1).astype(jnp.bfloat16)


def forward_x_table():
    source, y, low, r = np.meshgrid(
        np.arange(4), np.arange(4), np.arange(8), np.arange(8), indexing="ij"
    )
    x = (8 * (4 * (low * 4 + y) + source) + r).reshape(-1)
    theta = angle(x, np.arange(NP), NX).reshape(16, 64, NP)
    cos, sin = np.cos(theta), np.sin(theta)
    from_real = np.concatenate([cos, -sin], axis=2)
    from_imag = np.concatenate([sin, cos], axis=2)
    both = np.concatenate([from_real, from_imag], axis=1)
    return both.reshape(8, 256, 512).astype(jnp.bfloat16)


def inverse_x_table():
    theta = angle(np.arange(NX), np.arange(NX), NX).reshape(NX, 8, 128)
    both = np.concatenate([np.cos(theta), np.sin(theta)], axis=2)
    return np.transpose(both, (1, 0, 2)).astype(jnp.bfloat16)


def inverse_z_table():
    q = (
        192 * np.arange(2)[:, None, None]
        + 48 * np.arange(4)[None, :, None]
        + np.arange(48)[None, None, :]
    ).reshape(-1)
    theta = angle(np.arange(NZ), q, NZ).reshape(NZ, 8, 48)
    both = np.stack([np.cos(theta), -np.sin(theta)], axis=2)
    return both.reshape(4, NQ, NZ).astype(jnp.bfloat16)


def pack_body(wall_hbm, table_hbm, out_ref, kept_ref, wall_ref, sems):
    wall_copy = pltpu.make_async_copy(wall_hbm, wall_ref, sems.at[0])
    table_copy = pltpu.make_async_copy(table_hbm, kept_ref, sems.at[1])
    wall_copy.start()
    table_copy.start()
    wall_copy.wait()
    rows = [wall_ref[c].astype(jnp.float32) for c in range(3)]
    tails = [row[:, 128:] for row in rows] + [jnp.zeros((8, 64), jnp.float32)]
    pieces = [row[:, :128] for row in rows]
    for c in range(0, 4, 2):
        pieces.append(jnp.concatenate(tails[c : c + 2], axis=1))
    packed = jnp.concatenate(pieces, axis=0).astype(jnp.bfloat16)
    for k in range(16):
        out_ref[k] = packed
    table_copy.wait()


def pack_call(wall, table):
    return pl.pallas_call(
        pack_body,
        in_specs=[pl.BlockSpec(memory_space=pltpu.HBM)] * 2,
        scratch_shapes=[pltpu.VMEM((3, 8, NQ), jnp.bfloat16), pltpu.SemaphoreType.DMA((2,))],
        out_shape=[
            jax.ShapeDtypeStruct((16, 40, 128), jnp.bfloat16),
            jax.ShapeDtypeStruct((2, NQ, 384), jnp.bfloat16),
        ],
        compiler_params=pltpu.CompilerParams(vmem_limit_bytes=VMEM),
        cost_estimate=pl.CostEstimate(flops=10000, bytes_accessed=180000, transcendentals=0),
        name="pack",
    )(
        pltpu.with_memory_space_constraint(wall, pltpu.HBM),
        pltpu.with_memory_space_constraint(table, pltpu.HBM),
    )


def turned_lanes(values, turn):
    lane = lax.broadcasted_iota(jnp.int32, values.shape, 1)
    keep = jnp.where(turn == 0, 1.0, jnp.where(turn == 2, -1.0, 0.0))
    swap = jnp.where(turn == 1, 1.0, jnp.where(turn == 3, -1.0, 0.0))
    swap = jnp.where(lane < 64, swap, -swap)
    return values * keep + pltpu.roll(values, 64, axis=1) * swap


def partial_z(me, rows_ref, table_ref, step, c):
    turn = (me * lax.broadcasted_iota(jnp.int32, (64, 256), 1)) % 4
    to_real = jnp.where(turn == 0, 1.0, jnp.where(turn == 2, -1.0, 0.0))
    to_imag = jnp.where(turn == 3, 1.0, jnp.where(turn == 1, -1.0, 0.0))
    row = lax.broadcasted_iota(jnp.int32, (NQ, 128), 0)
    core = me % 2
    result = None
    for high in range(2):
        position = high * 2 + (core if step == 0 else 1 - core)
        blocks = [rows_ref[low * 2 + high].astype(jnp.float32) for low in range(8)]
        main = jnp.concatenate([block[c * 8 : c * 8 + 8] for block in blocks], axis=0)
        start = 24 + (c // 2) * 8
        tail = jnp.concatenate([block[start : start + 8] for block in blocks], axis=0)
        both = [main, tail] if c == 1 else [tail, main]
        rows = jnp.concatenate(both, axis=1)
        real = rows * to_real
        imag = rows * to_imag
        by_cos = jnp.concatenate([real, imag], axis=0).astype(jnp.bfloat16)
        by_sin = jnp.concatenate([imag, -real], axis=0).astype(jnp.bfloat16)
        lanes = slice(128, 384) if c == 1 else slice(0, 256)
        total = jnp.zeros((NQ, 128), jnp.float32)
        for part, values in enumerate((by_cos, by_sin)):
            total = total + lax.dot_general(
                table_ref[part, :, lanes],
                values,
                (((1,), (1,)), ((), ())),
                preferred_element_type=jnp.float32,
            )
        total = turned_lanes(total, (position * row) % 4)
        result = total if result is None else result + total
    return result


def forward_z_own_body(me_ref, rows_ref, table_ref, out_ref):
    for c in range(3):
        out_ref[c] = partial_z(me_ref[0], rows_ref, table_ref, 0, c)


def forward_z_body(me_ref, rows_ref, table_ref, own_ref, out_ref):
    lane = lax.broadcasted_iota(jnp.int32, (NQ, 128), 1)
    totals = []
    for c in range(3):
        total = own_ref[c] + partial_z(me_ref[0], rows_ref, table_ref, 1, c)
        totals.append(total * (1.0 / math.sqrt(NZ)))
    for pair in range(2):
        if pair:
            totals = [jnp.where(lane % 2 == 1, -total, total) for total in totals]
        for y in range(4):
            for half in range(2):
                start = y * 48 + half * 24
                pieces = [total[start : start + 24] for total in totals]
                block = jnp.concatenate(pieces, axis=0).astype(jnp.bfloat16)
                out_ref[pair * 8 + half * 4 + y] = block


def forward_z_call(me, rows, table, own):
    rows_spec = pl.BlockSpec((16, 40, 128), lambda j, s: (0, 0, 0))
    table_spec = pl.BlockSpec((2, NQ, 384), lambda j, s: (0, 0, 0))
    own_spec = pl.BlockSpec((3, NQ, 128), lambda j, s: (0, 0, 0))
    out_spec = pl.BlockSpec((16, 72, 128), lambda j, s: (0, 0, 0))
    first = own is None
    return pl.pallas_call(
        forward_z_own_body if first else forward_z_body,
        grid_spec=pltpu.PrefetchScalarGridSpec(
            num_scalar_prefetch=1,
            grid=(1,),
            in_specs=[rows_spec, table_spec] + ([] if first else [own_spec]),
            out_specs=own_spec if first else out_spec,
        ),
        out_shape=jax.ShapeDtypeStruct((3, NQ, 128), jnp.float32)
        if first
        else jax.ShapeDtypeStruct((16, 72, 128), jnp.bfloat16),
        compiler_params=pltpu.CompilerParams(vmem_limit_bytes=VMEM),
        cost_estimate=pl.CostEstimate(flops=151000000, bytes_accessed=1700000, transcendentals=0),
        name="forward_z_own" if first else "forward_z",
    )(me, rows, table, *([] if first else [own]))


def forward_x_body(values_ref, table_ref, out_ref):
    turn = lax.broadcasted_iota(jnp.int32, (72, 128), 1) % 4
    total = jnp.zeros((144, 512), jnp.float32)
    for k in range(8):
        first = [values_ref[2 * k + i].astype(jnp.float32) for i in range(2)]
        second = [turned_lanes(value, turn) for value in first]
        both = [jnp.concatenate(pieces, axis=1) for pieces in (first, second)]
        both = jnp.concatenate(both, axis=0).astype(jnp.bfloat16)
        total = total + jnp.dot(both, table_ref[k], preferred_element_type=jnp.float32)
    total = total * (1.0 / 32.0)
    for half in range(2):
        block = total[half * 72 : half * 72 + 72].astype(jnp.bfloat16)
        for y in range(4):
            out_ref[half * 4 + y] = block


def forward_x_call(values, table):
    return pl.pallas_call(
        forward_x_body,
        out_shape=jax.ShapeDtypeStruct((8, 72, 512), jnp.bfloat16),
        compiler_params=pltpu.CompilerParams(vmem_limit_bytes=VMEM),
        cost_estimate=pl.CostEstimate(flops=302000000, bytes_accessed=3000000, transcendentals=0),
        name="forward_x",
    )(values, table)


def modes_body(kernel_ref, spec_ref, out_ref):
    halves = [spec_ref[half, 0].astype(jnp.float32) for half in range(2)]
    spec = []
    for c in range(3):
        pieces = [half[c * 24 : c * 24 + 24] for half in halves]
        spec.append(jnp.concatenate(pieces, axis=0))
    for o in range(3):
        real = None
        imag = None
        for c in range(3):
            kr = kernel_ref[0, o, c, 0].astype(jnp.float32)
            ki = kernel_ref[1, o, c, 0].astype(jnp.float32)
            sr = spec[c][:, :NP]
            si = spec[c][:, NP:]
            r = kr * sr - ki * si
            i = kr * si + ki * sr
            real = r if real is None else real + r
            imag = i if imag is None else imag + i
        out_ref[0, o * 48 : o * 48 + 48, :] = real.astype(jnp.bfloat16)
        out_ref[0, 144 + o * 48 : 192 + o * 48, :] = imag.astype(jnp.bfloat16)


def modes_call(kernel, spec):
    return pl.pallas_call(
        modes_body,
        grid=(4,),
        in_specs=[
            pl.BlockSpec((2, 3, 3, 1, 48, NP), lambda j: (0, 0, 0, 0, j, 0)),
            pl.BlockSpec((2, 1, 72, 512), lambda j: (0, j, 0, 0)),
        ],
        out_specs=pl.BlockSpec((1, 288, NP), lambda j: (j, 0, 0)),
        out_shape=jax.ShapeDtypeStruct((4, 288, NP), jnp.bfloat16),
        compiler_params=pltpu.CompilerParams(vmem_limit_bytes=VMEM),
        cost_estimate=pl.CostEstimate(flops=3600000, bytes_accessed=2950000, transcendentals=0),
        name="modes",
    )(kernel, spec)


def inverse_x_body(values_ref, table_ref, out_ref):
    values = jnp.concatenate([values_ref[s] for s in range(4)], axis=1)

    def block(j, carry):
        total = jnp.dot(values, table_ref[j], preferred_element_type=jnp.float32)
        total = total * (1.0 / 32.0)
        real = (total[:144, :128] - total[144:, 128:]).astype(jnp.bfloat16)
        imag = (total[:144, 128:] + total[144:, :128]).astype(jnp.bfloat16)
        for o in range(3):
            out_ref[(j % 2) * 4 + j // 2, 0:48, o * 128 : (o + 1) * 128] = real[o * 48 : (o + 1) * 48]
            out_ref[(j % 2) * 4 + j // 2, 48:96, o * 128 : (o + 1) * 128] = imag[o * 48 : (o + 1) * 48]
        return carry

    lax.fori_loop(0, 8, block, 0, unroll=True)


def inverse_x_call(values, table):
    return pl.pallas_call(
        inverse_x_body,
        out_shape=jax.ShapeDtypeStruct((8, 96, 384), jnp.bfloat16),
        compiler_params=pltpu.CompilerParams(vmem_limit_bytes=VMEM),
        cost_estimate=pl.CostEstimate(flops=1208000000, bytes_accessed=5400000, transcendentals=0),
        name="inverse_x",
    )(values, table)


def inverse_z_body(steps, me_ref, values_ref, table_ref, *out_refs):
    me = me_ref[0]
    values = values_ref[...]
    odd = (lax.broadcasted_iota(jnp.int32, (NQ, 384), 0) * (me // 2)) % 2
    scale = jnp.where(odd == 1, -1.0, 1.0) * (1.0 / math.sqrt(NZ))
    for i, k in enumerate(steps):
        total = jnp.dot(table_ref[me ^ k], values, preferred_element_type=jnp.float32)
        total = (total * scale).astype(jnp.bfloat16)
        if len(out_refs) == len(steps):
            out_refs[i][...] = total
        else:
            out_refs[0][i] = total


def inverse_z_call(me, values, table, steps, stacked=False):
    if stacked:
        shapes = [(len(steps), NQ, 384)]
    else:
        shapes = [(NQ, 384)] * len(steps)
    blocks = [pl.BlockSpec(shape, lambda j, s, n=len(shape): (0,) * n) for shape in shapes]
    return pl.pallas_call(
        functools.partial(inverse_z_body, steps),
        grid_spec=pltpu.PrefetchScalarGridSpec(
            num_scalar_prefetch=1,
            grid=(1,),
            in_specs=[
                pl.BlockSpec((NZ, 384), lambda j, s: (0, 0)),
                pl.BlockSpec((4, NQ, NZ), lambda j, s: (0, 0, 0)),
            ],
            out_specs=blocks,
        ),
        out_shape=[jax.ShapeDtypeStruct(shape, jnp.bfloat16) for shape in shapes],
        compiler_params=pltpu.CompilerParams(vmem_limit_bytes=VMEM),
        cost_estimate=pl.CostEstimate(flops=227000000, bytes_accessed=2000000, transcendentals=0),
        name="inverse_z_far" if steps[0] else "inverse_z_near",
    )(me, values, table)


def finish_body(core_ref, own_ref, far_own_ref, near_ref, far_near_ref, out_ref):
    own = own_ref[...].astype(jnp.float32) + far_own_ref[...].astype(jnp.float32)
    near = near_ref[...].astype(jnp.float32) + far_near_ref[...].astype(jnp.float32)
    first = core_ref[0] == 0
    left = jnp.where(first, own, near).astype(jnp.bfloat16)
    right = jnp.where(first, near, own).astype(jnp.bfloat16)
    for o in range(3):
        out_ref[o, 0, :, 0:128] = left[:, o * 128 : (o + 1) * 128]
        out_ref[o, 0, :, 128:256] = right[:, o * 128 : (o + 1) * 128]


def finish_call(core, own, far_own, near, far_near):
    block = pl.BlockSpec((NQ, 384), lambda j, s: (0, 0))
    return pl.pallas_call(
        finish_body,
        grid_spec=pltpu.PrefetchScalarGridSpec(
            num_scalar_prefetch=1,
            grid=(1,),
            in_specs=[block] * 4,
            out_specs=pl.BlockSpec((3, 1, NQ, NP), lambda j, s: (0, 0, 0, 0)),
        ),
        out_shape=jax.ShapeDtypeStruct((3, 1, NQ, NP), jnp.bfloat16),
        compiler_params=pltpu.CompilerParams(vmem_limit_bytes=VMEM),
        cost_estimate=pl.CostEstimate(flops=150000, bytes_accessed=900000, transcendentals=0),
        name="finish",
    )(core, own, far_own, near, far_near)


def exchange(values, axis):
    return lax.all_to_all(values, axis, split_axis=0, concat_axis=0, tiled=True)


def swap_cores(values):
    return lax.ppermute(values, "core", [(0, 1), (1, 0)])


def move_z(values, step, flip):
    def position(z, core):
        return (z % 8) * 4 + (z // 8) * 2 + core

    perm = []
    for z in range(16):
        for core in range(2):
            target = (z + (step if core == 0 else -step)) % 16
            perm.append((position(z, core), position(target, core ^ flip)))
    return lax.ppermute(values, ("z_lo", "z_hi", "core"), perm)


def per_device(wall, kernel):
    core = lax.axis_index("core")
    gz = (lax.axis_index("z_hi") * 2 + core).reshape(1).astype(jnp.int32)

    rows, z_table = pack_call(wall, jnp.asarray(forward_z_table()))
    rows = exchange(rows, ("z_lo", "z_hi"))
    other = swap_cores(rows)
    z_spectra = forward_z_call(gz, other, z_table, forward_z_call(gz, rows, z_table, None))
    z_spectra = exchange(z_spectra, ("gx_pair", "gx_in", "y"))
    spec = exchange(forward_x_call(z_spectra, jnp.asarray(forward_x_table())), ("gx_in", "y"))

    modes = exchange(modes_call(kernel, spec.reshape(2, 4, 72, 512)), ("gx_pair", "gx_in"))
    planes = exchange(inverse_x_call(modes, jnp.asarray(inverse_x_table())), ("core", "gx_pair", "gx_in"))
    planes = planes.reshape(NZ, 384)
    z_table = jnp.asarray(inverse_z_table())
    (to_far,) = inverse_z_call(gz, planes, z_table, (2, 3), True)
    own, to_near = inverse_z_call(gz, planes, z_table, (0, 1))
    half = move_z(to_far, 4, 0)
    far_own = move_z(half[0], 4, 0)
    far_near = move_z(half[1], 4, 1)
    near = swap_cores(to_near)
    return finish_call(core.reshape(1).astype(jnp.int32), own, far_own, near, far_near)


def solution(mesh):
    fine = Mesh(
        mesh.devices.reshape(8, 4, 2, 2, 2, 2),
        ("z_lo", "y", "gx_pair", "gx_in", "z_hi", "core"),
    )
    gx, gz = ("gx_pair", "gx_in"), ("z_hi", "core")
    return jax.shard_map(
        per_device,
        mesh=fine,
        in_specs=(
            P(None, ("z_lo", "y") + gx, gz),
            P(None, None, None, ("z_lo", "y"), gz, gx),
        ),
        out_specs=P(None, ("z_lo", "y"), gz, gx),
        check_vma=False,
    )
```

```python
import functools
import math

import jax
import jax.numpy as jnp
import numpy as np
from jax import lax
from jax.experimental import pallas as pl
from jax.experimental.pallas import tpu as pltpu
from jax.sharding import Mesh, PartitionSpec as P

NX = 1024
NZ = 768
NQ = 192
NP = 256
VMEM = 40 * 1024 * 1024


def angle(left, right, length):
    phase = (left[:, None].astype(np.int64) * right[None, :].astype(np.int64)) % length
    return phase * (2.0 * math.pi / length)


def forward_z_table():
    q = np.arange(NQ)
    theta = angle(q, q, NZ)
    both = np.stack([np.cos(theta), np.sin(theta)])
    main, tail = both[..., :128], both[..., 128:]
    zero = np.zeros_like(tail)
    return np.concatenate([tail, zero, main, zero, tail], axis=-1).astype(jnp.bfloat16)


def forward_x_table():
    source, y, low, r = np.meshgrid(
        np.arange(4), np.arange(4), np.arange(8), np.arange(8), indexing="ij"
    )
    x = (8 * (4 * (low * 4 + y) + source) + r).reshape(-1)
    theta = angle(x, np.arange(NP), NX).reshape(16, 64, NP)
    cos, sin = np.cos(theta), np.sin(theta)
    from_real = np.concatenate([cos, -sin], axis=2)
    from_imag = np.concatenate([sin, cos], axis=2)
    both = np.concatenate([from_real, from_imag], axis=1)
    return both.reshape(8, 256, 512).astype(jnp.bfloat16)


def inverse_x_table():
    theta = angle(np.arange(NX), np.arange(NX), NX).reshape(NX, 8, 128)
    both = np.concatenate([np.cos(theta), np.sin(theta)], axis=2)
    return np.transpose(both, (1, 0, 2)).astype(jnp.bfloat16)


def inverse_z_table():
    q = (
        192 * np.arange(2)[:, None, None]
        + 48 * np.arange(4)[None, :, None]
        + np.arange(48)[None, None, :]
    ).reshape(-1)
    theta = angle(np.arange(NZ), q, NZ).reshape(NZ, 8, 48)
    both = np.stack([np.cos(theta), -np.sin(theta)], axis=2)
    return both.reshape(4, NQ, NZ).astype(jnp.bfloat16)


def pack_body(wall_hbm, table_hbm, out_ref, kept_ref, wall_ref, sems):
    wall_copy = pltpu.make_async_copy(wall_hbm, wall_ref, sems.at[0])
    table_copy = pltpu.make_async_copy(table_hbm, kept_ref, sems.at[1])
    wall_copy.start()
    table_copy.start()
    wall_copy.wait()
    rows = [wall_ref[c].astype(jnp.float32) for c in range(3)]
    tails = [row[:, 128:] for row in rows] + [jnp.zeros((8, 64), jnp.float32)]
    pieces = [row[:, :128] for row in rows]
    for c in range(0, 4, 2):
        pieces.append(jnp.concatenate(tails[c : c + 2], axis=1))
    packed = jnp.concatenate(pieces, axis=0).astype(jnp.bfloat16)
    for k in range(16):
        out_ref[k] = packed
    table_copy.wait()


def pack_call(wall, table):
    return pl.pallas_call(
        pack_body,
        in_specs=[pl.BlockSpec(memory_space=pltpu.HBM)] * 2,
        scratch_shapes=[pltpu.VMEM((3, 8, NQ), jnp.bfloat16), pltpu.SemaphoreType.DMA((2,))],
        out_shape=[
            jax.ShapeDtypeStruct((16, 40, 128), jnp.bfloat16),
            jax.ShapeDtypeStruct((2, NQ, 384), jnp.bfloat16),
        ],
        compiler_params=pltpu.CompilerParams(vmem_limit_bytes=VMEM),
        cost_estimate=pl.CostEstimate(flops=10000, bytes_accessed=180000, transcendentals=0),
        name="pack",
    )(
        pltpu.with_memory_space_constraint(wall, pltpu.HBM),
        pltpu.with_memory_space_constraint(table, pltpu.HBM),
    )


def turned_lanes(values, turn):
    lane = lax.broadcasted_iota(jnp.int32, values.shape, 1)
    keep = jnp.where(turn == 0, 1.0, jnp.where(turn == 2, -1.0, 0.0))
    swap = jnp.where(turn == 1, 1.0, jnp.where(turn == 3, -1.0, 0.0))
    swap = jnp.where(lane < 64, swap, -swap)
    return values * keep + pltpu.roll(values, 64, axis=1) * swap


def partial_z(me_ref, rows_ref, table_ref, step, c):
    me = me_ref[0]
    wanted = pl.ds(pl.multiple_of(me_ref[1] * 96, 96), 96)
    turn = (me * lax.broadcasted_iota(jnp.int32, (64, 256), 1)) % 4
    to_real = jnp.where(turn == 0, 1.0, jnp.where(turn == 2, -1.0, 0.0))
    to_imag = jnp.where(turn == 3, 1.0, jnp.where(turn == 1, -1.0, 0.0))
    row = lax.broadcasted_iota(jnp.int32, (96, 128), 0)
    core = me % 2
    result = None
    for high in range(2):
        position = high * 2 + (core if step == 0 else 1 - core)
        blocks = [rows_ref[low * 2 + high].astype(jnp.float32) for low in range(8)]
        main = jnp.concatenate([block[c * 8 : c * 8 + 8] for block in blocks], axis=0)
        start = 24 + (c // 2) * 8
        tail = jnp.concatenate([block[start : start + 8] for block in blocks], axis=0)
        both = [main, tail] if c == 1 else [tail, main]
        rows = jnp.concatenate(both, axis=1)
        real = rows * to_real
        imag = rows * to_imag
        by_cos = jnp.concatenate([real, imag], axis=0).astype(jnp.bfloat16)
        by_sin = jnp.concatenate([imag, -real], axis=0).astype(jnp.bfloat16)
        lanes = slice(128, 384) if c == 1 else slice(0, 256)
        total = jnp.zeros((96, 128), jnp.float32)
        for part, values in enumerate((by_cos, by_sin)):
            total = total + lax.dot_general(
                table_ref[part, wanted, lanes],
                values,
                (((1,), (1,)), ((), ())),
                preferred_element_type=jnp.float32,
            )
        total = turned_lanes(total, (position * row) % 4)
        result = total if result is None else result + total
    return result


def forward_z_own_body(me_ref, rows_ref, table_ref, out_ref):
    for c in range(3):
        out_ref[c] = partial_z(me_ref, rows_ref, table_ref, 0, c)


def forward_z_body(me_ref, rows_ref, table_ref, own_ref, out_ref):
    lane = lax.broadcasted_iota(jnp.int32, (96, 128), 1)
    totals = []
    for c in range(3):
        total = own_ref[c] + partial_z(me_ref, rows_ref, table_ref, 1, c)
        totals.append(total * (1.0 / math.sqrt(NZ)))
    for pair in range(2):
        if pair:
            totals = [jnp.where(lane % 2 == 1, -total, total) for total in totals]
        for y in range(4):
            for half in range(2):
                start = (y % 2) * 48 + half * 24
                pieces = [total[start : start + 24] for total in totals]
                block = jnp.concatenate(pieces, axis=0).astype(jnp.bfloat16)
                out_ref[pair * 8 + half * 4 + y] = block


def forward_z_call(me, rows, table, own):
    rows_spec = pl.BlockSpec((16, 40, 128), lambda j, s: (0, 0, 0))
    table_spec = pl.BlockSpec((2, NQ, 384), lambda j, s: (0, 0, 0))
    own_spec = pl.BlockSpec((3, 96, 128), lambda j, s: (0, 0, 0))
    out_spec = pl.BlockSpec((16, 72, 128), lambda j, s: (0, 0, 0))
    first = own is None
    return pl.pallas_call(
        forward_z_own_body if first else forward_z_body,
        grid_spec=pltpu.PrefetchScalarGridSpec(
            num_scalar_prefetch=1,
            grid=(1,),
            in_specs=[rows_spec, table_spec] + ([] if first else [own_spec]),
            out_specs=own_spec if first else out_spec,
        ),
        out_shape=jax.ShapeDtypeStruct((3, 96, 128), jnp.float32)
        if first
        else jax.ShapeDtypeStruct((16, 72, 128), jnp.bfloat16),
        compiler_params=pltpu.CompilerParams(vmem_limit_bytes=VMEM),
        cost_estimate=pl.CostEstimate(flops=76000000, bytes_accessed=1200000, transcendentals=0),
        name="forward_z_own" if first else "forward_z",
    )(me, rows, table, *([] if first else [own]))


def forward_x_body(values_ref, table_ref, out_ref):
    turn = lax.broadcasted_iota(jnp.int32, (72, 128), 1) % 4
    total = jnp.zeros((144, 512), jnp.float32)
    for k in range(8):
        first = [values_ref[2 * k + i].astype(jnp.float32) for i in range(2)]
        second = [turned_lanes(value, turn) for value in first]
        both = [jnp.concatenate(pieces, axis=1) for pieces in (first, second)]
        both = jnp.concatenate(both, axis=0).astype(jnp.bfloat16)
        total = total + jnp.dot(both, table_ref[k], preferred_element_type=jnp.float32)
    total = total * (1.0 / 32.0)
    for half in range(2):
        block = total[half * 72 : half * 72 + 72].astype(jnp.bfloat16)
        for i in range(4):
            out_ref[i * 2 + half] = block


def forward_x_call(values, table):
    return pl.pallas_call(
        forward_x_body,
        out_shape=jax.ShapeDtypeStruct((8, 72, 512), jnp.bfloat16),
        compiler_params=pltpu.CompilerParams(vmem_limit_bytes=VMEM),
        cost_estimate=pl.CostEstimate(flops=302000000, bytes_accessed=3000000, transcendentals=0),
        name="forward_x",
    )(values, table)


def modes_body(kernel_ref, spec_ref, out_ref):
    halves = [spec_ref[half].astype(jnp.float32) for half in range(2)]
    spec = []
    for c in range(3):
        pieces = [half[c * 24 : c * 24 + 24] for half in halves]
        spec.append(jnp.concatenate(pieces, axis=0))
    for o in range(3):
        real = None
        imag = None
        for c in range(3):
            kr = kernel_ref[0, o, c, 0].astype(jnp.float32)
            ki = kernel_ref[1, o, c, 0].astype(jnp.float32)
            sr = spec[c][:, :NP]
            si = spec[c][:, NP:]
            r = kr * sr - ki * si
            i = kr * si + ki * sr
            real = r if real is None else real + r
            imag = i if imag is None else imag + i
        out_ref[0, o * 48 : o * 48 + 48, :] = real.astype(jnp.bfloat16)
        out_ref[0, 144 + o * 48 : 192 + o * 48, :] = imag.astype(jnp.bfloat16)


def modes_call(kernel, spec):
    return pl.pallas_call(
        modes_body,
        grid=(4,),
        in_specs=[
            pl.BlockSpec((2, 3, 3, 1, 48, NP), lambda j: (0, 0, 0, 0, j, 0)),
            pl.BlockSpec((2, 72, 512), lambda j: (j, 0, 0)),
        ],
        out_specs=pl.BlockSpec((1, 288, NP), lambda j: (j, 0, 0)),
        out_shape=jax.ShapeDtypeStruct((4, 288, NP), jnp.bfloat16),
        compiler_params=pltpu.CompilerParams(vmem_limit_bytes=VMEM),
        cost_estimate=pl.CostEstimate(flops=3600000, bytes_accessed=2950000, transcendentals=0),
        name="modes",
    )(kernel, spec)


def inverse_x_body(values_ref, table_ref, out_ref):
    values = jnp.concatenate([values_ref[s] for s in range(4)], axis=1)

    def block(j, carry):
        total = jnp.dot(values, table_ref[j], preferred_element_type=jnp.float32)
        total = total * (1.0 / 32.0)
        real = (total[:144, :128] - total[144:, 128:]).astype(jnp.bfloat16)
        imag = (total[:144, 128:] + total[144:, :128]).astype(jnp.bfloat16)
        for o in range(3):
            out_ref[(j % 2) * 4 + j // 2, 0:48, o * 128 : (o + 1) * 128] = real[o * 48 : (o + 1) * 48]
            out_ref[(j % 2) * 4 + j // 2, 48:96, o * 128 : (o + 1) * 128] = imag[o * 48 : (o + 1) * 48]
        return carry

    lax.fori_loop(0, 8, block, 0, unroll=True)


def inverse_x_call(values, table):
    return pl.pallas_call(
        inverse_x_body,
        out_shape=jax.ShapeDtypeStruct((8, 96, 384), jnp.bfloat16),
        compiler_params=pltpu.CompilerParams(vmem_limit_bytes=VMEM),
        cost_estimate=pl.CostEstimate(flops=1208000000, bytes_accessed=5400000, transcendentals=0),
        name="inverse_x",
    )(values, table)


def inverse_z_body(steps, me_ref, values_ref, table_ref, *out_refs):
    me = me_ref[0]
    values = values_ref[...]
    odd = (lax.broadcasted_iota(jnp.int32, (NQ, 384), 0) * (me // 2)) % 2
    scale = jnp.where(odd == 1, -1.0, 1.0) * (1.0 / math.sqrt(NZ))
    for k, out_ref in zip(steps, out_refs):
        total = jnp.dot(table_ref[me ^ k], values, preferred_element_type=jnp.float32)
        out_ref[...] = (total * scale).astype(out_ref.dtype)


def inverse_z_call(me, values, table, steps):
    block = pl.BlockSpec((NQ, 384), lambda j, s: (0, 0))
    return pl.pallas_call(
        functools.partial(inverse_z_body, steps),
        grid_spec=pltpu.PrefetchScalarGridSpec(
            num_scalar_prefetch=1,
            grid=(1,),
            in_specs=[
                pl.BlockSpec((NZ, 384), lambda j, s: (0, 0)),
                pl.BlockSpec((4, NQ, NZ), lambda j, s: (0, 0, 0)),
            ],
            out_specs=[block] * len(steps),
        ),
        out_shape=[jax.ShapeDtypeStruct((NQ, 384), jnp.bfloat16) for _ in steps],
        compiler_params=pltpu.CompilerParams(vmem_limit_bytes=VMEM),
        cost_estimate=pl.CostEstimate(flops=227000000, bytes_accessed=2000000, transcendentals=0),
        name="inverse_z_far" if steps[0] else "inverse_z_near",
    )(me, values, table)


def finish_body(core_ref, own_ref, far_own_ref, near_ref, far_near_ref, out_ref):
    own = own_ref[...].astype(jnp.float32) + far_own_ref[...].astype(jnp.float32)
    near = near_ref[...].astype(jnp.float32) + far_near_ref[...].astype(jnp.float32)
    first = core_ref[0] == 0
    left = jnp.where(first, own, near).astype(jnp.bfloat16)
    right = jnp.where(first, near, own).astype(jnp.bfloat16)
    for o in range(3):
        out_ref[o, 0, :, 0:128] = left[:, o * 128 : (o + 1) * 128]
        out_ref[o, 0, :, 128:256] = right[:, o * 128 : (o + 1) * 128]


def finish_call(core, own, far_own, near, far_near):
    block = pl.BlockSpec((NQ, 384), lambda j, s: (0, 0))
    return pl.pallas_call(
        finish_body,
        grid_spec=pltpu.PrefetchScalarGridSpec(
            num_scalar_prefetch=1,
            grid=(1,),
            in_specs=[block] * 4,
            out_specs=pl.BlockSpec((3, 1, NQ, NP), lambda j, s: (0, 0, 0, 0)),
        ),
        out_shape=jax.ShapeDtypeStruct((3, 1, NQ, NP), jnp.bfloat16),
        compiler_params=pltpu.CompilerParams(vmem_limit_bytes=VMEM),
        cost_estimate=pl.CostEstimate(flops=150000, bytes_accessed=900000, transcendentals=0),
        name="finish",
    )(core, own, far_own, near, far_near)


def exchange(values, axis):
    return lax.all_to_all(values, axis, split_axis=0, concat_axis=0, tiled=True)


def swap_cores(values):
    return lax.ppermute(values, "core", [(0, 1), (1, 0)])


def move_z(values, step, flip):
    def position(z, core):
        return (z % 8) * 4 + (z // 8) * 2 + core

    perm = []
    for z in range(16):
        for core in range(2):
            target = (z + (step if core == 0 else -step)) % 16
            perm.append((position(z, core), position(target, core ^ flip)))
    return lax.ppermute(values, ("z_a", "z_b", "z_hi", "core"), perm)


def per_device(wall, kernel):
    core = lax.axis_index("core")
    gz = (lax.axis_index("z_hi") * 2 + core).reshape(1).astype(jnp.int32)

    rows, z_table = pack_call(wall, jnp.asarray(forward_z_table()))
    rows = exchange(rows, ("z_a", "z_b", "z_hi"))
    other = swap_cores(rows)
    place = jnp.concatenate([gz, lax.axis_index("z_b").reshape(1).astype(jnp.int32)])
    z_spectra = forward_z_call(
        place, other, z_table, forward_z_call(place, rows, z_table, None)
    )
    z_spectra = exchange(z_spectra, ("gx_pair", "gx_in", "y_pair", "y_in"))
    spec = exchange(
        forward_x_call(z_spectra, jnp.asarray(forward_x_table())), ("z_b", "y_in", "gx_in")
    )

    modes = exchange(modes_call(kernel, spec), ("gx_pair", "gx_in"))
    planes = exchange(inverse_x_call(modes, jnp.asarray(inverse_x_table())), ("core", "gx_pair", "gx_in"))
    planes = planes.reshape(NZ, 384)
    z_table = jnp.asarray(inverse_z_table())
    (to_far,) = inverse_z_call(gz, planes, z_table, (2,))
    (to_far_near,) = inverse_z_call(gz, planes, z_table, (3,))
    own, to_near = inverse_z_call(gz, planes, z_table, (0, 1))
    far_own = move_z(move_z(to_far, 4, 0), 4, 0)
    far_near = move_z(move_z(to_far_near, 4, 0), 4, 1)
    near = swap_cores(to_near)
    return finish_call(core.reshape(1).astype(jnp.int32), own, far_own, near, far_near)


def solution(mesh):
    names = ("z_a", "z_b", "y_pair", "y_in", "gx_pair", "gx_in", "z_hi", "core")
    fine = Mesh(mesh.devices.reshape(4, 2, 2, 2, 2, 2, 2, 2), names)
    gy, gx, gz = names[:4], names[4:6], names[6:]
    return jax.shard_map(
        per_device,
        mesh=fine,
        in_specs=(P(None, gy + gx, gz), P(None, None, None, gy, gz, gx)),
        out_specs=P(None, gy, gz, gx),
        check_vma=False,
    )
```

```python
import functools
import math

import jax
import jax.numpy as jnp
import numpy as np
from jax import lax
from jax.experimental import pallas as pl
from jax.experimental.pallas import tpu as pltpu
from jax.sharding import Mesh, PartitionSpec as P

NX = 1024
NZ = 768
NQ = 192
NP = 256
VMEM = 40 * 1024 * 1024


def angle(left, right, length):
    phase = (left[:, None].astype(np.int64) * right[None, :].astype(np.int64)) % length
    return phase * (2.0 * math.pi / length)


def forward_z_table():
    q = np.arange(NQ)
    theta = angle(q, q, NZ)
    both = np.stack([np.cos(theta), np.sin(theta)])
    main, tail = both[..., :128], both[..., 128:]
    zero = np.zeros_like(tail)
    both = np.concatenate([tail, zero, main, zero, tail], axis=-1)
    return np.transpose(both.reshape(2, 2, 96, 384), (1, 0, 2, 3)).astype(jnp.bfloat16)


def forward_x_table():
    source, y, low, r = np.meshgrid(
        np.arange(4), np.arange(4), np.arange(8), np.arange(8), indexing="ij"
    )
    x = (8 * (4 * (low * 4 + y) + source) + r).reshape(-1)
    theta = angle(x, np.arange(NP), NX).reshape(16, 64, NP)
    cos, sin = np.cos(theta), np.sin(theta)
    from_real = np.concatenate([cos, -sin], axis=2)
    from_imag = np.concatenate([sin, cos], axis=2)
    both = np.concatenate([from_real, from_imag], axis=1)
    return both.reshape(8, 256, 512).astype(jnp.bfloat16)


def inverse_x_table():
    theta = angle(np.arange(NX), np.arange(NX), NX).reshape(NX, 8, 128)
    both = np.concatenate([np.cos(theta), np.sin(theta)], axis=2)
    return np.transpose(both, (1, 0, 2)).astype(jnp.bfloat16)


def inverse_z_table():
    q = (
        192 * np.arange(2)[:, None, None]
        + 48 * np.arange(4)[None, :, None]
        + np.arange(48)[None, None, :]
    ).reshape(-1)
    theta = angle(np.arange(NZ), q, NZ).reshape(NZ, 8, 48)
    both = np.stack([np.cos(theta), -np.sin(theta)], axis=2)
    return both.reshape(4, NQ, NZ).astype(jnp.bfloat16)


def pack_body(wall_hbm, table_hbm, out_ref, kept_ref, wall_ref, sems):
    wall_copy = pltpu.make_async_copy(wall_hbm, wall_ref, sems.at[0])
    table_copy = pltpu.make_async_copy(table_hbm, kept_ref, sems.at[1])
    wall_copy.start()
    table_copy.start()
    wall_copy.wait()
    rows = [wall_ref[c].astype(jnp.float32) for c in range(3)]
    tails = [row[:, 128:] for row in rows] + [jnp.zeros((8, 64), jnp.float32)]
    pieces = [row[:, :128] for row in rows]
    for c in range(0, 4, 2):
        pieces.append(jnp.concatenate(tails[c : c + 2], axis=1))
    packed = jnp.concatenate(pieces, axis=0).astype(jnp.bfloat16)
    for k in range(16):
        out_ref[k] = packed
    table_copy.wait()


def pack_call(wall, table):
    return pl.pallas_call(
        pack_body,
        in_specs=[pl.BlockSpec(memory_space=pltpu.HBM)] * 2,
        scratch_shapes=[pltpu.VMEM((3, 8, NQ), jnp.bfloat16), pltpu.SemaphoreType.DMA((2,))],
        out_shape=[
            jax.ShapeDtypeStruct((16, 40, 128), jnp.bfloat16),
            jax.ShapeDtypeStruct((2, 2, 96, 384), jnp.bfloat16),
        ],
        compiler_params=pltpu.CompilerParams(vmem_limit_bytes=VMEM),
        cost_estimate=pl.CostEstimate(flops=10000, bytes_accessed=180000, transcendentals=0),
        name="pack",
    )(
        pltpu.with_memory_space_constraint(wall, pltpu.HBM),
        pltpu.with_memory_space_constraint(table, pltpu.HBM),
    )


def turned_lanes(values, turn):
    lane = lax.broadcasted_iota(jnp.int32, values.shape, 1)
    keep = jnp.where(turn == 0, 1.0, jnp.where(turn == 2, -1.0, 0.0))
    swap = jnp.where(turn == 1, 1.0, jnp.where(turn == 3, -1.0, 0.0))
    swap = jnp.where(lane < 64, swap, -swap)
    return values * keep + pltpu.roll(values, 64, axis=1) * swap


def partial_z(me_ref, rows_ref, table_ref, step, c):
    me = me_ref[0]
    wanted = me_ref[1]
    turn = (me * lax.broadcasted_iota(jnp.int32, (64, 256), 1)) % 4
    to_real = jnp.where(turn == 0, 1.0, jnp.where(turn == 2, -1.0, 0.0))
    to_imag = jnp.where(turn == 3, 1.0, jnp.where(turn == 1, -1.0, 0.0))
    row = lax.broadcasted_iota(jnp.int32, (96, 128), 0)
    core = me % 2
    result = None
    for high in range(2):
        position = high * 2 + (core if step == 0 else 1 - core)
        blocks = [rows_ref[low * 2 + high].astype(jnp.float32) for low in range(8)]
        main = jnp.concatenate([block[c * 8 : c * 8 + 8] for block in blocks], axis=0)
        start = 24 + (c // 2) * 8
        tail = jnp.concatenate([block[start : start + 8] for block in blocks], axis=0)
        both = [main, tail] if c == 1 else [tail, main]
        rows = jnp.concatenate(both, axis=1)
        real = rows * to_real
        imag = rows * to_imag
        by_cos = jnp.concatenate([real, imag], axis=0).astype(jnp.bfloat16)
        by_sin = jnp.concatenate([imag, -real], axis=0).astype(jnp.bfloat16)
        lanes = slice(128, 384) if c == 1 else slice(0, 256)
        total = jnp.zeros((96, 128), jnp.float32)
        for part, values in enumerate((by_cos, by_sin)):
            total = total + lax.dot_general(
                table_ref[wanted, part, :, lanes],
                values,
                (((1,), (1,)), ((), ())),
                preferred_element_type=jnp.float32,
            )
        total = turned_lanes(total, (position * row) % 4)
        result = total if result is None else result + total
    return result


def forward_z_own_body(me_ref, rows_ref, table_ref, out_ref):
    for c in range(3):
        out_ref[c] = partial_z(me_ref, rows_ref, table_ref, 0, c)


def forward_z_body(me_ref, rows_ref, table_ref, own_ref, out_ref):
    lane = lax.broadcasted_iota(jnp.int32, (96, 128), 1)
    totals = []
    for c in range(3):
        total = own_ref[c] + partial_z(me_ref, rows_ref, table_ref, 1, c)
        totals.append(total * (1.0 / math.sqrt(NZ)))
    for pair in range(2):
        if pair:
            totals = [jnp.where(lane % 2 == 1, -total, total) for total in totals]
        for y in range(4):
            for half in range(2):
                start = (y % 2) * 48 + half * 24
                pieces = [total[start : start + 24] for total in totals]
                block = jnp.concatenate(pieces, axis=0).astype(jnp.bfloat16)
                out_ref[pair * 8 + half * 4 + y] = block


def forward_z_call(me, rows, table, own):
    rows_spec = pl.BlockSpec((16, 40, 128), lambda j, s: (0, 0, 0))
    table_spec = pl.BlockSpec((2, 2, 96, 384), lambda j, s: (0, 0, 0, 0))
    own_spec = pl.BlockSpec((3, 96, 128), lambda j, s: (0, 0, 0))
    out_spec = pl.BlockSpec((16, 72, 128), lambda j, s: (0, 0, 0))
    first = own is None
    return pl.pallas_call(
        forward_z_own_body if first else forward_z_body,
        grid_spec=pltpu.PrefetchScalarGridSpec(
            num_scalar_prefetch=1,
            grid=(1,),
            in_specs=[rows_spec, table_spec] + ([] if first else [own_spec]),
            out_specs=own_spec if first else out_spec,
        ),
        out_shape=jax.ShapeDtypeStruct((3, 96, 128), jnp.float32)
        if first
        else jax.ShapeDtypeStruct((16, 72, 128), jnp.bfloat16),
        compiler_params=pltpu.CompilerParams(vmem_limit_bytes=VMEM),
        cost_estimate=pl.CostEstimate(flops=76000000, bytes_accessed=1200000, transcendentals=0),
        name="forward_z_own" if first else "forward_z",
    )(me, rows, table, *([] if first else [own]))


def forward_x_body(values_ref, table_ref, out_ref):
    turn = lax.broadcasted_iota(jnp.int32, (72, 128), 1) % 4
    total = jnp.zeros((144, 512), jnp.float32)
    for k in range(8):
        first = [values_ref[2 * k + i].astype(jnp.float32) for i in range(2)]
        second = [turned_lanes(value, turn) for value in first]
        both = [jnp.concatenate(pieces, axis=1) for pieces in (first, second)]
        both = jnp.concatenate(both, axis=0).astype(jnp.bfloat16)
        total = total + jnp.dot(both, table_ref[k], preferred_element_type=jnp.float32)
    total = total * (1.0 / 32.0)
    for half in range(2):
        block = total[half * 72 : half * 72 + 72].astype(jnp.bfloat16)
        for i in range(4):
            out_ref[i * 2 + half] = block


def forward_x_call(values, table):
    return pl.pallas_call(
        forward_x_body,
        out_shape=jax.ShapeDtypeStruct((8, 72, 512), jnp.bfloat16),
        compiler_params=pltpu.CompilerParams(vmem_limit_bytes=VMEM),
        cost_estimate=pl.CostEstimate(flops=302000000, bytes_accessed=3000000, transcendentals=0),
        name="forward_x",
    )(values, table)


def modes_body(kernel_ref, spec_ref, out_ref):
    halves = [spec_ref[half].astype(jnp.float32) for half in range(2)]
    spec = []
    for c in range(3):
        pieces = [half[c * 24 : c * 24 + 24] for half in halves]
        spec.append(jnp.concatenate(pieces, axis=0))
    for o in range(3):
        real = None
        imag = None
        for c in range(3):
            kr = kernel_ref[0, o, c, 0].astype(jnp.float32)
            ki = kernel_ref[1, o, c, 0].astype(jnp.float32)
            sr = spec[c][:, :NP]
            si = spec[c][:, NP:]
            r = kr * sr - ki * si
            i = kr * si + ki * sr
            real = r if real is None else real + r
            imag = i if imag is None else imag + i
        out_ref[0, o * 48 : o * 48 + 48, :] = real.astype(jnp.bfloat16)
        out_ref[0, 144 + o * 48 : 192 + o * 48, :] = imag.astype(jnp.bfloat16)


def modes_call(kernel, spec):
    return pl.pallas_call(
        modes_body,
        grid=(4,),
        in_specs=[
            pl.BlockSpec((2, 3, 3, 1, 48, NP), lambda j: (0, 0, 0, 0, j, 0)),
            pl.BlockSpec((2, 72, 512), lambda j: (j, 0, 0)),
        ],
        out_specs=pl.BlockSpec((1, 288, NP), lambda j: (j, 0, 0)),
        out_shape=jax.ShapeDtypeStruct((4, 288, NP), jnp.bfloat16),
        compiler_params=pltpu.CompilerParams(vmem_limit_bytes=VMEM),
        cost_estimate=pl.CostEstimate(flops=3600000, bytes_accessed=2950000, transcendentals=0),
        name="modes",
    )(kernel, spec)


def inverse_x_body(values_ref, table_ref, out_ref):
    values = jnp.concatenate([values_ref[s] for s in range(4)], axis=1)

    def block(j, carry):
        total = jnp.dot(values, table_ref[j], preferred_element_type=jnp.float32)
        total = total * (1.0 / 32.0)
        real = (total[:144, :128] - total[144:, 128:]).astype(jnp.bfloat16)
        imag = (total[:144, 128:] + total[144:, :128]).astype(jnp.bfloat16)
        for o in range(3):
            out_ref[(j % 2) * 4 + j // 2, 0:48, o * 128 : (o + 1) * 128] = real[o * 48 : (o + 1) * 48]
            out_ref[(j % 2) * 4 + j // 2, 48:96, o * 128 : (o + 1) * 128] = imag[o * 48 : (o + 1) * 48]
        return carry

    lax.fori_loop(0, 8, block, 0, unroll=True)


def inverse_x_call(values, table):
    return pl.pallas_call(
        inverse_x_body,
        out_shape=jax.ShapeDtypeStruct((8, 96, 384), jnp.bfloat16),
        compiler_params=pltpu.CompilerParams(vmem_limit_bytes=VMEM),
        cost_estimate=pl.CostEstimate(flops=1208000000, bytes_accessed=5400000, transcendentals=0),
        name="inverse_x",
    )(values, table)


def inverse_z_body(steps, me_ref, values_ref, table_ref, *out_refs):
    me = me_ref[0]
    values = values_ref[...]
    odd = (lax.broadcasted_iota(jnp.int32, (NQ, 384), 0) * (me // 2)) % 2
    scale = jnp.where(odd == 1, -1.0, 1.0) * (1.0 / math.sqrt(NZ))
    for k, out_ref in zip(steps, out_refs):
        total = jnp.dot(table_ref[me ^ k], values, preferred_element_type=jnp.float32)
        out_ref[...] = (total * scale).astype(out_ref.dtype)


def inverse_z_call(me, values, table, steps):
    block = pl.BlockSpec((NQ, 384), lambda j, s: (0, 0))
    return pl.pallas_call(
        functools.partial(inverse_z_body, steps),
        grid_spec=pltpu.PrefetchScalarGridSpec(
            num_scalar_prefetch=1,
            grid=(1,),
            in_specs=[
                pl.BlockSpec((NZ, 384), lambda j, s: (0, 0)),
                pl.BlockSpec((4, NQ, NZ), lambda j, s: (0, 0, 0)),
            ],
            out_specs=[block] * len(steps),
        ),
        out_shape=[jax.ShapeDtypeStruct((NQ, 384), jnp.bfloat16) for _ in steps],
        compiler_params=pltpu.CompilerParams(vmem_limit_bytes=VMEM),
        cost_estimate=pl.CostEstimate(flops=227000000, bytes_accessed=2000000, transcendentals=0),
        name="inverse_z_far" if steps[0] else "inverse_z_near",
    )(me, values, table)


def finish_body(core_ref, own_ref, far_own_ref, near_ref, far_near_ref, out_ref):
    own = own_ref[...].astype(jnp.float32) + far_own_ref[...].astype(jnp.float32)
    near = near_ref[...].astype(jnp.float32) + far_near_ref[...].astype(jnp.float32)
    first = core_ref[0] == 0
    left = jnp.where(first, own, near).astype(jnp.bfloat16)
    right = jnp.where(first, near, own).astype(jnp.bfloat16)
    for o in range(3):
        out_ref[o, 0, :, 0:128] = left[:, o * 128 : (o + 1) * 128]
        out_ref[o, 0, :, 128:256] = right[:, o * 128 : (o + 1) * 128]


def finish_call(core, own, far_own, near, far_near):
    block = pl.BlockSpec((NQ, 384), lambda j, s: (0, 0))
    return pl.pallas_call(
        finish_body,
        grid_spec=pltpu.PrefetchScalarGridSpec(
            num_scalar_prefetch=1,
            grid=(1,),
            in_specs=[block] * 4,
            out_specs=pl.BlockSpec((3, 1, NQ, NP), lambda j, s: (0, 0, 0, 0)),
        ),
        out_shape=jax.ShapeDtypeStruct((3, 1, NQ, NP), jnp.bfloat16),
        compiler_params=pltpu.CompilerParams(vmem_limit_bytes=VMEM),
        cost_estimate=pl.CostEstimate(flops=150000, bytes_accessed=900000, transcendentals=0),
        name="finish",
    )(core, own, far_own, near, far_near)


def exchange(values, axis):
    return lax.all_to_all(values, axis, split_axis=0, concat_axis=0, tiled=True)


def swap_cores(values):
    return lax.ppermute(values, "core", [(0, 1), (1, 0)])


def move_z(values, step, flip):
    def position(z, core):
        return (z % 8) * 4 + (z // 8) * 2 + core

    perm = []
    for z in range(16):
        for core in range(2):
            target = (z + (step if core == 0 else -step)) % 16
            perm.append((position(z, core), position(target, core ^ flip)))
    return lax.ppermute(values, ("z_a", "z_b", "z_hi", "core"), perm)


def per_device(wall, kernel):
    core = lax.axis_index("core")
    gz = (lax.axis_index("z_hi") * 2 + core).reshape(1).astype(jnp.int32)

    rows, z_table = pack_call(wall, jnp.asarray(forward_z_table()))
    rows = exchange(rows, ("z_a", "z_b", "z_hi"))
    other = swap_cores(rows)
    place = jnp.concatenate([gz, lax.axis_index("z_b").reshape(1).astype(jnp.int32)])
    z_spectra = forward_z_call(
        place, other, z_table, forward_z_call(place, rows, z_table, None)
    )
    z_spectra = exchange(z_spectra, ("gx_pair", "gx_in", "y_pair", "y_in"))
    spec = exchange(
        forward_x_call(z_spectra, jnp.asarray(forward_x_table())), ("z_b", "y_in", "gx_in")
    )

    modes = exchange(modes_call(kernel, spec), ("gx_pair", "gx_in"))
    planes = exchange(inverse_x_call(modes, jnp.asarray(inverse_x_table())), ("core", "gx_pair", "gx_in"))
    planes = planes.reshape(NZ, 384)
    z_table = jnp.asarray(inverse_z_table())
    (to_far,) = inverse_z_call(gz, planes, z_table, (2,))
    (to_far_near,) = inverse_z_call(gz, planes, z_table, (3,))
    own, to_near = inverse_z_call(gz, planes, z_table, (0, 1))
    far_own = move_z(move_z(to_far, 4, 0), 4, 0)
    far_near = move_z(move_z(to_far_near, 4, 0), 4, 1)
    near = swap_cores(to_near)
    return finish_call(core.reshape(1).astype(jnp.int32), own, far_own, near, far_near)


def solution(mesh):
    names = ("z_a", "z_b", "y_pair", "y_in", "gx_pair", "gx_in", "z_hi", "core")
    fine = Mesh(mesh.devices.reshape(4, 2, 2, 2, 2, 2, 2, 2), names)
    gy, gx, gz = names[:4], names[4:6], names[6:]
    return jax.shard_map(
        per_device,
        mesh=fine,
        in_specs=(P(None, gy + gx, gz), P(None, None, None, gy, gz, gx)),
        out_specs=P(None, gy, gz, gx),
        check_vma=False,
    )
```

```python
import functools
import math

import jax
import jax.numpy as jnp
import numpy as np
from jax import lax
from jax.experimental import pallas as pl
from jax.experimental.pallas import tpu as pltpu
from jax.sharding import Mesh, PartitionSpec as P

NX = 1024
NZ = 768
NQ = 192
NP = 256
VMEM = 40 * 1024 * 1024


def angle(left, right, length):
    phase = (left[:, None].astype(np.int64) * right[None, :].astype(np.int64)) % length
    return phase * (2.0 * math.pi / length)


def forward_z_table():
    q = np.arange(NQ)
    theta = angle(q, q, NZ)
    both = np.stack([np.cos(theta), np.sin(theta)])
    main, tail = both[..., :128], both[..., 128:]
    zero = np.zeros_like(tail)
    return np.concatenate([tail, zero, main, zero, tail], axis=-1).astype(jnp.bfloat16)


def forward_x_table():
    source, y, low, r = np.meshgrid(
        np.arange(4), np.arange(4), np.arange(8), np.arange(8), indexing="ij"
    )
    x = (8 * (4 * (low * 4 + y) + source) + r).reshape(-1)
    theta = angle(x, np.arange(NP), NX).reshape(16, 64, NP)
    cos, sin = np.cos(theta), np.sin(theta)
    from_real = np.concatenate([cos, -sin], axis=2)
    from_imag = np.concatenate([sin, cos], axis=2)
    both = np.concatenate([from_real, from_imag], axis=1)
    return both.reshape(8, 256, 512).astype(jnp.bfloat16)


def inverse_x_table():
    theta = angle(np.arange(NX), np.arange(NX), NX).reshape(NX, 8, 128)
    both = np.concatenate([np.cos(theta), np.sin(theta)], axis=2)
    return np.transpose(both, (1, 0, 2)).astype(jnp.bfloat16)


def inverse_z_table():
    q = (
        192 * np.arange(2)[:, None, None]
        + 48 * np.array([0, 2, 1, 3])[None, :, None]
        + np.arange(48)[None, None, :]
    ).reshape(-1)
    theta = angle(np.arange(NZ), q, NZ).reshape(NZ, 8, 48)
    both = np.stack([np.cos(theta), -np.sin(theta)], axis=2)
    return both.reshape(4, NQ, NZ).astype(jnp.bfloat16)


def pack_body(wall_hbm, table_hbm, out_ref, kept_ref, wall_ref, sems):
    wall_copy = pltpu.make_async_copy(wall_hbm, wall_ref, sems.at[0])
    table_copy = pltpu.make_async_copy(table_hbm, kept_ref, sems.at[1])
    wall_copy.start()
    table_copy.start()
    wall_copy.wait()
    rows = [wall_ref[c].astype(jnp.float32) for c in range(3)]
    tails = [row[:, 128:] for row in rows] + [jnp.zeros((8, 64), jnp.float32)]
    pieces = [row[:, :128] for row in rows]
    for c in range(0, 4, 2):
        pieces.append(jnp.concatenate(tails[c : c + 2], axis=1))
    packed = jnp.concatenate(pieces, axis=0).astype(jnp.bfloat16)
    for k in range(16):
        out_ref[k] = packed
    table_copy.wait()


def pack_call(wall, table):
    return pl.pallas_call(
        pack_body,
        in_specs=[pl.BlockSpec(memory_space=pltpu.HBM)] * 2,
        scratch_shapes=[pltpu.VMEM((3, 8, NQ), jnp.bfloat16), pltpu.SemaphoreType.DMA((2,))],
        out_shape=[
            jax.ShapeDtypeStruct((16, 40, 128), jnp.bfloat16),
            jax.ShapeDtypeStruct((2, NQ, 384), jnp.bfloat16),
        ],
        compiler_params=pltpu.CompilerParams(vmem_limit_bytes=VMEM),
        cost_estimate=pl.CostEstimate(flops=10000, bytes_accessed=180000, transcendentals=0),
        name="pack",
    )(
        pltpu.with_memory_space_constraint(wall, pltpu.HBM),
        pltpu.with_memory_space_constraint(table, pltpu.HBM),
    )


def turned_lanes(values, turn):
    lane = lax.broadcasted_iota(jnp.int32, values.shape, 1)
    keep = jnp.where(turn == 0, 1.0, jnp.where(turn == 2, -1.0, 0.0))
    swap = jnp.where(turn == 1, 1.0, jnp.where(turn == 3, -1.0, 0.0))
    swap = jnp.where(lane < 64, swap, -swap)
    return values * keep + pltpu.roll(values, 64, axis=1) * swap


def partial_z(me, rows_ref, table_ref, step, c):
    turn = (me * lax.broadcasted_iota(jnp.int32, (64, 256), 1)) % 4
    to_real = jnp.where(turn == 0, 1.0, jnp.where(turn == 2, -1.0, 0.0))
    to_imag = jnp.where(turn == 3, 1.0, jnp.where(turn == 1, -1.0, 0.0))
    row = lax.broadcasted_iota(jnp.int32, (NQ, 128), 0)
    core = me % 2
    result = None
    for high in range(2):
        position = high * 2 + (core if step == 0 else 1 - core)
        blocks = [rows_ref[low * 2 + high].astype(jnp.float32) for low in range(8)]
        main = jnp.concatenate([block[c * 8 : c * 8 + 8] for block in blocks], axis=0)
        start = 24 + (c // 2) * 8
        tail = jnp.concatenate([block[start : start + 8] for block in blocks], axis=0)
        both = [main, tail] if c == 1 else [tail, main]
        rows = jnp.concatenate(both, axis=1)
        real = rows * to_real
        imag = rows * to_imag
        by_cos = jnp.concatenate([real, imag], axis=0).astype(jnp.bfloat16)
        by_sin = jnp.concatenate([imag, -real], axis=0).astype(jnp.bfloat16)
        lanes = slice(128, 384) if c == 1 else slice(0, 256)
        total = jnp.zeros((NQ, 128), jnp.float32)
        for part, values in enumerate((by_cos, by_sin)):
            total = total + lax.dot_general(
                table_ref[part, :, lanes],
                values,
                (((1,), (1,)), ((), ())),
                preferred_element_type=jnp.float32,
            )
        total = turned_lanes(total, (position * row) % 4)
        result = total if result is None else result + total
    return result


def forward_z_own_body(me_ref, rows_ref, table_ref, out_ref):
    for c in range(3):
        out_ref[c] = partial_z(me_ref[0], rows_ref, table_ref, 0, c)


def forward_z_body(me_ref, rows_ref, table_ref, own_ref, out_ref):
    lane = lax.broadcasted_iota(jnp.int32, (NQ, 128), 1)
    totals = []
    for c in range(3):
        total = own_ref[c] + partial_z(me_ref[0], rows_ref, table_ref, 1, c)
        totals.append(total * (1.0 / math.sqrt(NZ)))
    for pair in range(2):
        if pair:
            totals = [jnp.where(lane % 2 == 1, -total, total) for total in totals]
        for y in range(4):
            for half in range(2):
                start = y * 48 + half * 24
                pieces = [total[start : start + 24] for total in totals]
                block = jnp.concatenate(pieces, axis=0).astype(jnp.bfloat16)
                out_ref[pair * 8 + half * 4 + y] = block


def forward_z_call(me, rows, table, own):
    rows_spec = pl.BlockSpec((16, 40, 128), lambda j, s: (0, 0, 0))
    table_spec = pl.BlockSpec((2, NQ, 384), lambda j, s: (0, 0, 0))
    own_spec = pl.BlockSpec((3, NQ, 128), lambda j, s: (0, 0, 0))
    out_spec = pl.BlockSpec((16, 72, 128), lambda j, s: (0, 0, 0))
    first = own is None
    return pl.pallas_call(
        forward_z_own_body if first else forward_z_body,
        grid_spec=pltpu.PrefetchScalarGridSpec(
            num_scalar_prefetch=1,
            grid=(1,),
            in_specs=[rows_spec, table_spec] + ([] if first else [own_spec]),
            out_specs=own_spec if first else out_spec,
        ),
        out_shape=jax.ShapeDtypeStruct((3, NQ, 128), jnp.float32)
        if first
        else jax.ShapeDtypeStruct((16, 72, 128), jnp.bfloat16),
        compiler_params=pltpu.CompilerParams(vmem_limit_bytes=VMEM),
        cost_estimate=pl.CostEstimate(flops=151000000, bytes_accessed=1700000, transcendentals=0),
        name="forward_z_own" if first else "forward_z",
    )(me, rows, table, *([] if first else [own]))


def forward_x_body(values_ref, table_ref, out_ref):
    turn = lax.broadcasted_iota(jnp.int32, (72, 128), 1) % 4
    total = jnp.zeros((144, 512), jnp.float32)
    for k in range(8):
        first = [values_ref[2 * k + i].astype(jnp.float32) for i in range(2)]
        second = [turned_lanes(value, turn) for value in first]
        both = [jnp.concatenate(pieces, axis=1) for pieces in (first, second)]
        both = jnp.concatenate(both, axis=0).astype(jnp.bfloat16)
        total = total + jnp.dot(both, table_ref[k], preferred_element_type=jnp.float32)
    total = total * (1.0 / 32.0)
    for half in range(2):
        block = total[half * 72 : half * 72 + 72].astype(jnp.bfloat16)
        for y in range(4):
            out_ref[half * 4 + y] = block


def forward_x_call(values, table):
    return pl.pallas_call(
        forward_x_body,
        out_shape=jax.ShapeDtypeStruct((8, 72, 512), jnp.bfloat16),
        compiler_params=pltpu.CompilerParams(vmem_limit_bytes=VMEM),
        cost_estimate=pl.CostEstimate(flops=302000000, bytes_accessed=3000000, transcendentals=0),
        name="forward_x",
    )(values, table)


def modes_body(kernel_ref, spec_ref, out_ref):
    halves = [spec_ref[half, 0].astype(jnp.float32) for half in range(2)]
    spec = []
    for c in range(3):
        pieces = [half[c * 24 : c * 24 + 24] for half in halves]
        spec.append(jnp.concatenate(pieces, axis=0))
    for o in range(3):
        real = None
        imag = None
        for c in range(3):
            kr = kernel_ref[0, o, c, 0].astype(jnp.float32)
            ki = kernel_ref[1, o, c, 0].astype(jnp.float32)
            sr = spec[c][:, :NP]
            si = spec[c][:, NP:]
            r = kr * sr - ki * si
            i = kr * si + ki * sr
            real = r if real is None else real + r
            imag = i if imag is None else imag + i
        out_ref[0, o * 48 : o * 48 + 48, :] = real.astype(jnp.bfloat16)
        out_ref[0, 144 + o * 48 : 192 + o * 48, :] = imag.astype(jnp.bfloat16)


def modes_call(kernel, spec):
    return pl.pallas_call(
        modes_body,
        grid=(4,),
        in_specs=[
            pl.BlockSpec((2, 3, 3, 1, 48, NP), lambda j: (0, 0, 0, 0, j, 0)),
            pl.BlockSpec((2, 1, 72, 512), lambda j: (0, j, 0, 0)),
        ],
        out_specs=pl.BlockSpec((1, 288, NP), lambda j: ((j % 2) * 2 + j // 2, 0, 0)),
        out_shape=jax.ShapeDtypeStruct((4, 288, NP), jnp.bfloat16),
        compiler_params=pltpu.CompilerParams(vmem_limit_bytes=VMEM),
        cost_estimate=pl.CostEstimate(flops=3600000, bytes_accessed=2950000, transcendentals=0),
        name="modes",
    )(kernel, spec)


def inverse_x_body(values_ref, table_ref, out_ref):
    values = jnp.concatenate([values_ref[s] for s in (0, 2, 1, 3)], axis=1)

    def block(j, carry):
        total = jnp.dot(values, table_ref[j], preferred_element_type=jnp.float32)
        total = total * (1.0 / 32.0)
        real = (total[:144, :128] - total[144:, 128:]).astype(jnp.bfloat16)
        imag = (total[:144, 128:] + total[144:, :128]).astype(jnp.bfloat16)
        gx = j // 2
        place = (j % 2) * 4 + (gx % 2) * 2 + gx // 2
        for o in range(3):
            out_ref[place, 0:48, o * 128 : (o + 1) * 128] = real[o * 48 : (o + 1) * 48]
            out_ref[place, 48:96, o * 128 : (o + 1) * 128] = imag[o * 48 : (o + 1) * 48]
        return carry

    lax.fori_loop(0, 8, block, 0, unroll=True)


def inverse_x_call(values, table):
    return pl.pallas_call(
        inverse_x_body,
        out_shape=jax.ShapeDtypeStruct((8, 96, 384), jnp.bfloat16),
        compiler_params=pltpu.CompilerParams(vmem_limit_bytes=VMEM),
        cost_estimate=pl.CostEstimate(flops=1208000000, bytes_accessed=5400000, transcendentals=0),
        name="inverse_x",
    )(values, table)


def inverse_z_body(steps, me_ref, values_ref, table_ref, *out_refs):
    me = me_ref[0]
    values = values_ref[...]
    odd = (lax.broadcasted_iota(jnp.int32, (NQ, 384), 0) * (me // 2)) % 2
    scale = jnp.where(odd == 1, -1.0, 1.0) * (1.0 / math.sqrt(NZ))
    for k, out_ref in zip(steps, out_refs):
        total = jnp.dot(table_ref[me ^ k], values, preferred_element_type=jnp.float32)
        out_ref[...] = (total * scale).astype(out_ref.dtype)


def inverse_z_call(me, values, table, steps):
    block = pl.BlockSpec((NQ, 384), lambda j, s: (0, 0))
    return pl.pallas_call(
        functools.partial(inverse_z_body, steps),
        grid_spec=pltpu.PrefetchScalarGridSpec(
            num_scalar_prefetch=1,
            grid=(1,),
            in_specs=[
                pl.BlockSpec((NZ, 384), lambda j, s: (0, 0)),
                pl.BlockSpec((4, NQ, NZ), lambda j, s: (0, 0, 0)),
            ],
            out_specs=[block] * len(steps),
        ),
        out_shape=[jax.ShapeDtypeStruct((NQ, 384), jnp.bfloat16) for _ in steps],
        compiler_params=pltpu.CompilerParams(vmem_limit_bytes=VMEM),
        cost_estimate=pl.CostEstimate(flops=227000000, bytes_accessed=2000000, transcendentals=0),
        name="inverse_z_far" if steps[0] else "inverse_z_near",
    )(me, values, table)


def finish_body(core_ref, own_ref, far_own_ref, near_ref, far_near_ref, out_ref):
    own = own_ref[...].astype(jnp.float32) + far_own_ref[...].astype(jnp.float32)
    near = near_ref[...].astype(jnp.float32) + far_near_ref[...].astype(jnp.float32)
    first = core_ref[0] == 0
    left = jnp.where(first, own, near).astype(jnp.bfloat16)
    right = jnp.where(first, near, own).astype(jnp.bfloat16)
    for o in range(3):
        out_ref[o, 0, :, 0:128] = left[:, o * 128 : (o + 1) * 128]
        out_ref[o, 0, :, 128:256] = right[:, o * 128 : (o + 1) * 128]


def finish_call(core, own, far_own, near, far_near):
    block = pl.BlockSpec((NQ, 384), lambda j, s: (0, 0))
    return pl.pallas_call(
        finish_body,
        grid_spec=pltpu.PrefetchScalarGridSpec(
            num_scalar_prefetch=1,
            grid=(1,),
            in_specs=[block] * 4,
            out_specs=pl.BlockSpec((3, 1, NQ, NP), lambda j, s: (0, 0, 0, 0)),
        ),
        out_shape=jax.ShapeDtypeStruct((3, 1, NQ, NP), jnp.bfloat16),
        compiler_params=pltpu.CompilerParams(vmem_limit_bytes=VMEM),
        cost_estimate=pl.CostEstimate(flops=150000, bytes_accessed=900000, transcendentals=0),
        name="finish",
    )(core, own, far_own, near, far_near)


def exchange(values, axis):
    return lax.all_to_all(values, axis, split_axis=0, concat_axis=0, tiled=True)


def swap_cores(values):
    return lax.ppermute(values, "core", [(0, 1), (1, 0)])


def move_z(values, step, flip):
    def position(z, core):
        return (z % 8) * 4 + (z // 8) * 2 + core

    perm = []
    for z in range(16):
        for core in range(2):
            target = (z + (step if core == 0 else -step)) % 16
            perm.append((position(z, core), position(target, core ^ flip)))
    return lax.ppermute(values, ("z_lo", "z_hi", "core"), perm)


def per_device(wall, kernel):
    core = lax.axis_index("core")
    gz = (lax.axis_index("z_hi") * 2 + core).reshape(1).astype(jnp.int32)

    rows, z_table = pack_call(wall, jnp.asarray(forward_z_table()))
    rows = exchange(rows, ("z_lo", "z_hi"))
    other = swap_cores(rows)
    z_spectra = forward_z_call(gz, other, z_table, forward_z_call(gz, rows, z_table, None))
    z_spectra = exchange(z_spectra, ("gx_pair", "gx_in", "y"))
    spec = exchange(forward_x_call(z_spectra, jnp.asarray(forward_x_table())), ("gx_in", "y"))

    modes = exchange(modes_call(kernel, spec.reshape(2, 4, 72, 512)), ("gx_in", "gx_pair"))
    planes = exchange(inverse_x_call(modes, jnp.asarray(inverse_x_table())), ("core", "gx_in", "gx_pair"))
    planes = planes.reshape(NZ, 384)
    z_table = jnp.asarray(inverse_z_table())
    (to_far,) = inverse_z_call(gz, planes, z_table, (2,))
    (to_far_near,) = inverse_z_call(gz, planes, z_table, (3,))
    own, to_near = inverse_z_call(gz, planes, z_table, (0, 1))
    far_own = move_z(move_z(to_far, 4, 0), 4, 0)
    far_near = move_z(move_z(to_far_near, 4, 0), 4, 1)
    near = swap_cores(to_near)
    return finish_call(core.reshape(1).astype(jnp.int32), own, far_own, near, far_near)


def solution(mesh):
    fine = Mesh(
        mesh.devices.reshape(8, 4, 2, 2, 2, 2),
        ("z_lo", "y", "gx_pair", "gx_in", "z_hi", "core"),
    )
    gx, gz = ("gx_pair", "gx_in"), ("z_hi", "core")
    return jax.shard_map(
        per_device,
        mesh=fine,
        in_specs=(
            P(None, ("z_lo", "y") + gx, gz),
            P(None, None, None, ("z_lo", "y"), gz, gx),
        ),
        out_specs=P(None, ("z_lo", "y"), gz, gx),
        check_vma=False,
    )
```

```python
import functools
import math

import jax
import jax.numpy as jnp
import numpy as np
from jax import lax
from jax.experimental import pallas as pl
from jax.experimental.pallas import tpu as pltpu
from jax.sharding import Mesh, PartitionSpec as P

NX = 1024
NZ = 768
NQ = 192
NP = 256
VMEM = 40 * 1024 * 1024


def angle(left, right, length):
    phase = (left[:, None].astype(np.int64) * right[None, :].astype(np.int64)) % length
    return phase * (2.0 * math.pi / length)


def forward_z_table():
    q = np.arange(NQ)
    theta = angle(q, q, NZ)
    both = np.stack([np.cos(theta), np.sin(theta)])
    main, tail = both[..., :128], both[..., 128:]
    zero = np.zeros_like(tail)
    return np.concatenate([tail, zero, main, zero, tail], axis=-1).astype(jnp.bfloat16)


def forward_x_table():
    source, y, low, r = np.meshgrid(
        np.arange(4), np.arange(4), np.arange(8), np.arange(8), indexing="ij"
    )
    x = (8 * (4 * (low * 4 + y) + source) + r).reshape(-1)
    theta = angle(x, np.arange(NP), NX).reshape(16, 64, NP)
    cos, sin = np.cos(theta), np.sin(theta)
    from_real = np.concatenate([cos, -sin], axis=2)
    from_imag = np.concatenate([sin, cos], axis=2)
    both = np.concatenate([from_real, from_imag], axis=1)
    return both.reshape(8, 256, 512).astype(jnp.bfloat16)


def inverse_x_table():
    theta = angle(np.arange(NX), np.arange(NX), NX).reshape(NX, 8, 128)
    both = np.concatenate([np.cos(theta), np.sin(theta)], axis=2)
    return np.transpose(both, (1, 0, 2)).astype(jnp.bfloat16)


def inverse_z_table():
    q = (
        192 * np.arange(2)[:, None, None]
        + 48 * np.array([0, 2, 1, 3])[None, :, None]
        + np.arange(48)[None, None, :]
    ).reshape(-1)
    theta = angle(np.arange(NZ), q, NZ).reshape(NZ, 8, 48)
    both = np.stack([np.cos(theta), -np.sin(theta)], axis=2)
    return both.reshape(4, NQ, NZ).astype(jnp.bfloat16)


def pack_body(wall_hbm, table_hbm, out_ref, kept_ref, wall_ref, sems):
    wall_copy = pltpu.make_async_copy(wall_hbm, wall_ref, sems.at[0])
    table_copy = pltpu.make_async_copy(table_hbm, kept_ref, sems.at[1])
    wall_copy.start()
    table_copy.start()
    wall_copy.wait()
    rows = [wall_ref[c].astype(jnp.float32) for c in range(3)]
    tails = [row[:, 128:] for row in rows] + [jnp.zeros((8, 64), jnp.float32)]
    pieces = [row[:, :128] for row in rows]
    for c in range(0, 4, 2):
        pieces.append(jnp.concatenate(tails[c : c + 2], axis=1))
    packed = jnp.concatenate(pieces, axis=0).astype(jnp.bfloat16)
    for k in range(16):
        out_ref[k] = packed
    table_copy.wait()


def pack_call(wall, table):
    return pl.pallas_call(
        pack_body,
        in_specs=[pl.BlockSpec(memory_space=pltpu.HBM)] * 2,
        scratch_shapes=[pltpu.VMEM((3, 8, NQ), jnp.bfloat16), pltpu.SemaphoreType.DMA((2,))],
        out_shape=[
            jax.ShapeDtypeStruct((16, 40, 128), jnp.bfloat16),
            jax.ShapeDtypeStruct((2, NQ, 384), jnp.bfloat16),
        ],
        compiler_params=pltpu.CompilerParams(vmem_limit_bytes=VMEM),
        cost_estimate=pl.CostEstimate(flops=10000, bytes_accessed=180000, transcendentals=0),
        name="pack",
    )(
        pltpu.with_memory_space_constraint(wall, pltpu.HBM),
        pltpu.with_memory_space_constraint(table, pltpu.HBM),
    )


def turned_lanes(values, turn):
    lane = lax.broadcasted_iota(jnp.int32, values.shape, 1)
    keep = jnp.where(turn == 0, 1.0, jnp.where(turn == 2, -1.0, 0.0))
    swap = jnp.where(turn == 1, 1.0, jnp.where(turn == 3, -1.0, 0.0))
    swap = jnp.where(lane < 64, swap, -swap)
    return values * keep + pltpu.roll(values, 64, axis=1) * swap


def partial_z(me, rows_ref, table_ref, step, c):
    turn = (me * lax.broadcasted_iota(jnp.int32, (64, 256), 1)) % 4
    to_real = jnp.where(turn == 0, 1.0, jnp.where(turn == 2, -1.0, 0.0))
    to_imag = jnp.where(turn == 3, 1.0, jnp.where(turn == 1, -1.0, 0.0))
    row = lax.broadcasted_iota(jnp.int32, (NQ, 128), 0)
    core = me % 2
    result = None
    for high in range(2):
        position = high * 2 + (core if step == 0 else 1 - core)
        blocks = [rows_ref[low * 2 + high].astype(jnp.float32) for low in range(8)]
        main = jnp.concatenate([block[c * 8 : c * 8 + 8] for block in blocks], axis=0)
        start = 24 + (c // 2) * 8
        tail = jnp.concatenate([block[start : start + 8] for block in blocks], axis=0)
        both = [main, tail] if c == 1 else [tail, main]
        rows = jnp.concatenate(both, axis=1)
        real = rows * to_real
        imag = rows * to_imag
        by_cos = jnp.concatenate([real, imag], axis=0).astype(jnp.bfloat16)
        by_sin = jnp.concatenate([imag, -real], axis=0).astype(jnp.bfloat16)
        lanes = slice(128, 384) if c == 1 else slice(0, 256)
        total = jnp.zeros((NQ, 128), jnp.float32)
        for part, values in enumerate((by_cos, by_sin)):
            total = total + lax.dot_general(
                table_ref[part, :, lanes],
                values,
                (((1,), (1,)), ((), ())),
                preferred_element_type=jnp.float32,
            )
        total = turned_lanes(total, (position * row) % 4)
        result = total if result is None else result + total
    return result


def forward_z_own_body(me_ref, rows_ref, table_ref, out_ref):
    for c in range(3):
        out_ref[c] = partial_z(me_ref[0], rows_ref, table_ref, 0, c)


def forward_z_body(me_ref, rows_ref, table_ref, own_ref, out_ref):
    lane = lax.broadcasted_iota(jnp.int32, (NQ, 128), 1)
    totals = []
    for c in range(3):
        total = own_ref[c] + partial_z(me_ref[0], rows_ref, table_ref, 1, c)
        totals.append(total * (1.0 / math.sqrt(NZ)))
    for pair in range(2):
        if pair:
            totals = [jnp.where(lane % 2 == 1, -total, total) for total in totals]
        for y in range(4):
            for half in range(2):
                start = y * 48 + half * 24
                pieces = [total[start : start + 24] for total in totals]
                block = jnp.concatenate(pieces, axis=0).astype(jnp.bfloat16)
                out_ref[pair * 8 + half * 4 + y] = block


def forward_z_call(me, rows, table, own):
    rows_spec = pl.BlockSpec((16, 40, 128), lambda j, s: (0, 0, 0))
    table_spec = pl.BlockSpec((2, NQ, 384), lambda j, s: (0, 0, 0))
    own_spec = pl.BlockSpec((3, NQ, 128), lambda j, s: (0, 0, 0))
    out_spec = pl.BlockSpec((16, 72, 128), lambda j, s: (0, 0, 0))
    first = own is None
    return pl.pallas_call(
        forward_z_own_body if first else forward_z_body,
        grid_spec=pltpu.PrefetchScalarGridSpec(
            num_scalar_prefetch=1,
            grid=(1,),
            in_specs=[rows_spec, table_spec] + ([] if first else [own_spec]),
            out_specs=own_spec if first else out_spec,
        ),
        out_shape=jax.ShapeDtypeStruct((3, NQ, 128), jnp.float32)
        if first
        else jax.ShapeDtypeStruct((16, 72, 128), jnp.bfloat16),
        compiler_params=pltpu.CompilerParams(vmem_limit_bytes=VMEM),
        cost_estimate=pl.CostEstimate(flops=151000000, bytes_accessed=1700000, transcendentals=0),
        name="forward_z_own" if first else "forward_z",
    )(me, rows, table, *([] if first else [own]))


def forward_x_body(values_ref, table_ref, out_ref):
    turn = lax.broadcasted_iota(jnp.int32, (72, 128), 1) % 4
    total = jnp.zeros((144, 512), jnp.float32)
    for k in range(8):
        first = [values_ref[2 * k + i].astype(jnp.float32) for i in range(2)]
        second = [turned_lanes(value, turn) for value in first]
        both = [jnp.concatenate(pieces, axis=1) for pieces in (first, second)]
        both = jnp.concatenate(both, axis=0).astype(jnp.bfloat16)
        total = total + jnp.dot(both, table_ref[k], preferred_element_type=jnp.float32)
    total = total * (1.0 / 32.0)
    for half in range(2):
        block = total[half * 72 : half * 72 + 72].astype(jnp.bfloat16)
        for y in range(4):
            out_ref[half * 4 + y] = block


def forward_x_call(values, table):
    return pl.pallas_call(
        forward_x_body,
        out_shape=jax.ShapeDtypeStruct((8, 72, 512), jnp.bfloat16),
        compiler_params=pltpu.CompilerParams(vmem_limit_bytes=VMEM),
        cost_estimate=pl.CostEstimate(flops=302000000, bytes_accessed=3000000, transcendentals=0),
        name="forward_x",
    )(values, table)


def modes_body(kernel_ref, spec_ref, out_ref):
    halves = [spec_ref[half, 0].astype(jnp.float32) for half in range(2)]
    spec = []
    for c in range(3):
        pieces = [half[c * 24 : c * 24 + 24] for half in halves]
        spec.append(jnp.concatenate(pieces, axis=0))
    for o in range(3):
        real = None
        imag = None
        for c in range(3):
            kr = kernel_ref[0, o, c, 0].astype(jnp.float32)
            ki = kernel_ref[1, o, c, 0].astype(jnp.float32)
            sr = spec[c][:, :NP]
            si = spec[c][:, NP:]
            r = kr * sr - ki * si
            i = kr * si + ki * sr
            real = r if real is None else real + r
            imag = i if imag is None else imag + i
        out_ref[0, o * 48 : o * 48 + 48, :] = real.astype(jnp.bfloat16)
        out_ref[0, 144 + o * 48 : 192 + o * 48, :] = imag.astype(jnp.bfloat16)


def modes_call(kernel, spec):
    return pl.pallas_call(
        modes_body,
        grid=(4,),
        in_specs=[
            pl.BlockSpec((2, 3, 3, 1, 48, NP), lambda j: (0, 0, 0, 0, j, 0)),
            pl.BlockSpec((2, 1, 72, 512), lambda j: (0, j, 0, 0)),
        ],
        out_specs=pl.BlockSpec((1, 288, NP), lambda j: ((j % 2) * 2 + j // 2, 0, 0)),
        out_shape=jax.ShapeDtypeStruct((4, 288, NP), jnp.bfloat16),
        compiler_params=pltpu.CompilerParams(vmem_limit_bytes=VMEM),
        cost_estimate=pl.CostEstimate(flops=3600000, bytes_accessed=2950000, transcendentals=0),
        name="modes",
    )(kernel, spec)


def inverse_x_body(values_ref, table_ref, out_ref):
    values = jnp.concatenate([values_ref[s] for s in (0, 2, 1, 3)], axis=1)

    def block(j, carry):
        total = jnp.dot(values, table_ref[j], preferred_element_type=jnp.float32)
        total = total * (1.0 / 32.0)
        real = (total[:144, :128] - total[144:, 128:]).astype(jnp.bfloat16)
        imag = (total[:144, 128:] + total[144:, :128]).astype(jnp.bfloat16)
        gx = j // 2
        place = (j % 2) * 4 + (gx % 2) * 2 + gx // 2
        for o in range(3):
            out_ref[place, 0:48, o * 128 : (o + 1) * 128] = real[o * 48 : (o + 1) * 48]
            out_ref[place, 48:96, o * 128 : (o + 1) * 128] = imag[o * 48 : (o + 1) * 48]
        return carry

    lax.fori_loop(0, 8, block, 0, unroll=True)


def inverse_x_call(values, table):
    return pl.pallas_call(
        inverse_x_body,
        out_shape=jax.ShapeDtypeStruct((8, 96, 384), jnp.bfloat16),
        compiler_params=pltpu.CompilerParams(vmem_limit_bytes=VMEM),
        cost_estimate=pl.CostEstimate(flops=1208000000, bytes_accessed=5400000, transcendentals=0),
        name="inverse_x",
    )(values, table)


def inverse_z_body(steps, me_ref, values_ref, table_ref, *out_refs):
    me = me_ref[0]
    values = values_ref[...]
    odd = (lax.broadcasted_iota(jnp.int32, (NQ, 384), 0) * (me // 2)) % 2
    scale = jnp.where(odd == 1, -1.0, 1.0) * (1.0 / math.sqrt(NZ))
    for k, out_ref in zip(steps, out_refs):
        total = jnp.dot(table_ref[me ^ k], values, preferred_element_type=jnp.float32)
        out_ref[...] = (total * scale).astype(out_ref.dtype)


def inverse_z_call(me, values, table, steps):
    block = pl.BlockSpec((NQ, 384), lambda j, s: (0, 0))
    return pl.pallas_call(
        functools.partial(inverse_z_body, steps),
        grid_spec=pltpu.PrefetchScalarGridSpec(
            num_scalar_prefetch=1,
            grid=(1,),
            in_specs=[
                pl.BlockSpec((NZ, 384), lambda j, s: (0, 0)),
                pl.BlockSpec((4, NQ, NZ), lambda j, s: (0, 0, 0)),
            ],
            out_specs=[block] * len(steps),
        ),
        out_shape=[jax.ShapeDtypeStruct((NQ, 384), jnp.bfloat16) for _ in steps],
        compiler_params=pltpu.CompilerParams(vmem_limit_bytes=VMEM),
        cost_estimate=pl.CostEstimate(flops=227000000, bytes_accessed=2000000, transcendentals=0),
        name="inverse_z_far" if steps[0] else "inverse_z_near",
    )(me, values, table)


def finish_body(core_ref, own_ref, far_own_ref, near_ref, far_near_ref, out_ref):
    own = own_ref[...].astype(jnp.float32) + far_own_ref[...].astype(jnp.float32)
    near = near_ref[...].astype(jnp.float32) + far_near_ref[...].astype(jnp.float32)
    first = core_ref[0] == 0
    left = jnp.where(first, own, near).astype(jnp.bfloat16)
    right = jnp.where(first, near, own).astype(jnp.bfloat16)
    for o in range(3):
        out_ref[o, 0, :, 0:128] = left[:, o * 128 : (o + 1) * 128]
        out_ref[o, 0, :, 128:256] = right[:, o * 128 : (o + 1) * 128]


def finish_call(core, own, far_own, near, far_near):
    block = pl.BlockSpec((NQ, 384), lambda j, s: (0, 0))
    return pl.pallas_call(
        finish_body,
        grid_spec=pltpu.PrefetchScalarGridSpec(
            num_scalar_prefetch=1,
            grid=(1,),
            in_specs=[block] * 4,
            out_specs=pl.BlockSpec((3, 1, NQ, NP), lambda j, s: (0, 0, 0, 0)),
        ),
        out_shape=jax.ShapeDtypeStruct((3, 1, NQ, NP), jnp.bfloat16),
        compiler_params=pltpu.CompilerParams(vmem_limit_bytes=VMEM),
        cost_estimate=pl.CostEstimate(flops=150000, bytes_accessed=900000, transcendentals=0),
        name="finish",
    )(core, own, far_own, near, far_near)


def exchange(values, axis):
    return lax.all_to_all(values, axis, split_axis=0, concat_axis=0, tiled=True)


def swap_cores(values):
    return lax.ppermute(values, "core", [(0, 1), (1, 0)])


def move_z(values, step, flip):
    def position(z, core):
        return (z % 8) * 4 + (z // 8) * 2 + core

    perm = []
    for z in range(16):
        for core in range(2):
            target = (z + (step if core == 1 else -step)) % 16
            perm.append((position(z, core), position(target, core ^ flip)))
    return lax.ppermute(values, ("z_lo", "z_hi", "core"), perm)


def per_device(wall, kernel):
    core = lax.axis_index("core")
    gz = (lax.axis_index("z_hi") * 2 + core).reshape(1).astype(jnp.int32)

    rows, z_table = pack_call(wall, jnp.asarray(forward_z_table()))
    rows = exchange(rows, ("z_lo", "z_hi"))
    other = swap_cores(rows)
    z_spectra = forward_z_call(gz, other, z_table, forward_z_call(gz, rows, z_table, None))
    z_spectra = exchange(z_spectra, ("gx_pair", "gx_in", "y"))
    spec = exchange(forward_x_call(z_spectra, jnp.asarray(forward_x_table())), ("gx_in", "y"))

    modes = exchange(modes_call(kernel, spec.reshape(2, 4, 72, 512)), ("gx_in", "gx_pair"))
    planes = exchange(inverse_x_call(modes, jnp.asarray(inverse_x_table())), ("core", "gx_in", "gx_pair"))
    planes = planes.reshape(NZ, 384)
    z_table = jnp.asarray(inverse_z_table())
    (to_far,) = inverse_z_call(gz, planes, z_table, (2,))
    (to_far_near,) = inverse_z_call(gz, planes, z_table, (3,))
    own, to_near = inverse_z_call(gz, planes, z_table, (0, 1))
    far_own = move_z(move_z(to_far, 4, 0), 4, 0)
    far_near = move_z(move_z(to_far_near, 4, 0), 4, 1)
    near = swap_cores(to_near)
    return finish_call(core.reshape(1).astype(jnp.int32), own, far_own, near, far_near)


def solution(mesh):
    fine = Mesh(
        mesh.devices.reshape(8, 4, 2, 2, 2, 2),
        ("z_lo", "y", "gx_pair", "gx_in", "z_hi", "core"),
    )
    gx, gz = ("gx_pair", "gx_in"), ("z_hi", "core")
    return jax.shard_map(
        per_device,
        mesh=fine,
        in_specs=(
            P(None, ("z_lo", "y") + gx, gz),
            P(None, None, None, ("z_lo", "y"), gz, gx),
        ),
        out_specs=P(None, ("z_lo", "y"), gz, gx),
        check_vma=False,
    )
```

```python
import functools
import math

import jax
import jax.numpy as jnp
import numpy as np
from jax import lax
from jax.experimental import pallas as pl
from jax.experimental.pallas import tpu as pltpu
from jax.sharding import Mesh, PartitionSpec as P

NX = 1024
NZ = 768
NQ = 192
NP = 256
VMEM = 40 * 1024 * 1024


def angle(left, right, length):
    phase = (left[:, None].astype(np.int64) * right[None, :].astype(np.int64)) % length
    return phase * (2.0 * math.pi / length)


def forward_z_table():
    q = np.arange(NQ)
    theta = angle(q, q, NZ)
    both = np.stack([np.cos(theta), np.sin(theta)])
    main, tail = both[..., :128], both[..., 128:]
    zero = np.zeros_like(tail)
    return np.concatenate([tail, zero, main, zero, tail], axis=-1).astype(jnp.bfloat16)


def forward_x_table():
    source, y, low, r = np.meshgrid(
        np.arange(4), np.arange(4), np.arange(8), np.arange(8), indexing="ij"
    )
    x = (8 * (4 * (low * 4 + y) + source) + r).reshape(-1)
    theta = angle(x, np.arange(NP), NX).reshape(16, 64, NP)
    cos, sin = np.cos(theta), np.sin(theta)
    from_real = np.concatenate([cos, -sin], axis=2)
    from_imag = np.concatenate([sin, cos], axis=2)
    both = np.concatenate([from_real, from_imag], axis=1)
    return both.reshape(8, 256, 512).astype(jnp.bfloat16)


def inverse_x_table():
    theta = angle(np.arange(NX), np.arange(NX), NX).reshape(NX, 8, 128)
    both = np.concatenate([np.cos(theta), np.sin(theta)], axis=2)
    return np.transpose(both, (1, 0, 2)).astype(jnp.bfloat16)


def inverse_z_table():
    q = (
        192 * np.arange(2)[:, None, None]
        + 48 * np.array([0, 2, 1, 3])[None, :, None]
        + np.arange(48)[None, None, :]
    ).reshape(-1)
    theta = angle(np.arange(NZ), q, NZ).reshape(NZ, 8, 48)
    both = np.stack([np.cos(theta), -np.sin(theta)], axis=2)
    return both.reshape(4, NQ, NZ).astype(jnp.bfloat16)


def pack_body(wall_hbm, table_hbm, out_ref, kept_ref, wall_ref, sems):
    wall_copy = pltpu.make_async_copy(wall_hbm, wall_ref, sems.at[0])
    table_copy = pltpu.make_async_copy(table_hbm, kept_ref, sems.at[1])
    wall_copy.start()
    table_copy.start()
    wall_copy.wait()
    rows = [wall_ref[c].astype(jnp.float32) for c in range(3)]
    tails = [row[:, 128:] for row in rows] + [jnp.zeros((8, 64), jnp.float32)]
    pieces = [row[:, :128] for row in rows]
    for c in range(0, 4, 2):
        pieces.append(jnp.concatenate(tails[c : c + 2], axis=1))
    packed = jnp.concatenate(pieces, axis=0).astype(jnp.bfloat16)
    for k in range(16):
        out_ref[k] = packed
    table_copy.wait()


def pack_call(wall, table):
    return pl.pallas_call(
        pack_body,
        in_specs=[pl.BlockSpec(memory_space=pltpu.HBM)] * 2,
        scratch_shapes=[pltpu.VMEM((3, 8, NQ), jnp.bfloat16), pltpu.SemaphoreType.DMA((2,))],
        out_shape=[
            jax.ShapeDtypeStruct((16, 40, 128), jnp.bfloat16),
            jax.ShapeDtypeStruct((2, NQ, 384), jnp.bfloat16),
        ],
        compiler_params=pltpu.CompilerParams(vmem_limit_bytes=VMEM),
        cost_estimate=pl.CostEstimate(flops=10000, bytes_accessed=180000, transcendentals=0),
        name="pack",
    )(
        pltpu.with_memory_space_constraint(wall, pltpu.HBM),
        pltpu.with_memory_space_constraint(table, pltpu.HBM),
    )


def turned_lanes(values, turn):
    lane = lax.broadcasted_iota(jnp.int32, values.shape, 1)
    keep = jnp.where(turn == 0, 1.0, jnp.where(turn == 2, -1.0, 0.0))
    swap = jnp.where(turn == 1, 1.0, jnp.where(turn == 3, -1.0, 0.0))
    swap = jnp.where(lane < 64, swap, -swap)
    return values * keep + pltpu.roll(values, 64, axis=1) * swap


def partial_z(me, rows_ref, table_ref, step, c):
    turn = (me * lax.broadcasted_iota(jnp.int32, (64, 256), 1)) % 4
    to_real = jnp.where(turn == 0, 1.0, jnp.where(turn == 2, -1.0, 0.0))
    to_imag = jnp.where(turn == 3, 1.0, jnp.where(turn == 1, -1.0, 0.0))
    row = lax.broadcasted_iota(jnp.int32, (NQ, 128), 0)
    core = me % 2
    result = None
    for high in range(2):
        position = high * 2 + (core if step == 0 else 1 - core)
        blocks = [rows_ref[low * 2 + high].astype(jnp.float32) for low in range(8)]
        main = jnp.concatenate([block[c * 8 : c * 8 + 8] for block in blocks], axis=0)
        start = 24 + (c // 2) * 8
        tail = jnp.concatenate([block[start : start + 8] for block in blocks], axis=0)
        both = [main, tail] if c == 1 else [tail, main]
        rows = jnp.concatenate(both, axis=1)
        real = rows * to_real
        imag = rows * to_imag
        by_cos = jnp.concatenate([real, imag], axis=0).astype(jnp.bfloat16)
        by_sin = jnp.concatenate([imag, -real], axis=0).astype(jnp.bfloat16)
        lanes = slice(128, 384) if c == 1 else slice(0, 256)
        total = jnp.zeros((NQ, 128), jnp.float32)
        for part, values in enumerate((by_cos, by_sin)):
            total = total + lax.dot_general(
                table_ref[part, :, lanes],
                values,
                (((1,), (1,)), ((), ())),
                preferred_element_type=jnp.float32,
            )
        total = turned_lanes(total, (position * row) % 4)
        result = total if result is None else result + total
    return result


def forward_z_own_body(me_ref, rows_ref, table_ref, out_ref):
    for c in range(3):
        out_ref[c] = partial_z(me_ref[0], rows_ref, table_ref, 0, c)


def forward_z_body(me_ref, rows_ref, table_ref, own_ref, out_ref):
    lane = lax.broadcasted_iota(jnp.int32, (NQ, 128), 1)
    totals = []
    for c in range(3):
        total = own_ref[c] + partial_z(me_ref[0], rows_ref, table_ref, 1, c)
        totals.append(total * (1.0 / math.sqrt(NZ)))
    for pair in range(2):
        if pair:
            totals = [jnp.where(lane % 2 == 1, -total, total) for total in totals]
        for y in range(4):
            for half in range(2):
                start = y * 48 + half * 24
                pieces = [total[start : start + 24] for total in totals]
                block = jnp.concatenate(pieces, axis=0).astype(jnp.bfloat16)
                out_ref[pair * 8 + half * 4 + y] = block


def forward_z_call(me, rows, table, own):
    rows_spec = pl.BlockSpec((16, 40, 128), lambda j, s: (0, 0, 0))
    table_spec = pl.BlockSpec((2, NQ, 384), lambda j, s: (0, 0, 0))
    own_spec = pl.BlockSpec((3, NQ, 128), lambda j, s: (0, 0, 0))
    out_spec = pl.BlockSpec((16, 72, 128), lambda j, s: (0, 0, 0))
    first = own is None
    return pl.pallas_call(
        forward_z_own_body if first else forward_z_body,
        grid_spec=pltpu.PrefetchScalarGridSpec(
            num_scalar_prefetch=1,
            grid=(1,),
            in_specs=[rows_spec, table_spec] + ([] if first else [own_spec]),
            out_specs=own_spec if first else out_spec,
        ),
        out_shape=jax.ShapeDtypeStruct((3, NQ, 128), jnp.float32)
        if first
        else jax.ShapeDtypeStruct((16, 72, 128), jnp.bfloat16),
        compiler_params=pltpu.CompilerParams(vmem_limit_bytes=VMEM),
        cost_estimate=pl.CostEstimate(flops=151000000, bytes_accessed=1700000, transcendentals=0),
        name="forward_z_own" if first else "forward_z",
    )(me, rows, table, *([] if first else [own]))


def forward_x_body(values_ref, table_ref, out_ref):
    turn = lax.broadcasted_iota(jnp.int32, (72, 128), 1) % 4
    total = jnp.zeros((144, 512), jnp.float32)
    for k in range(8):
        first = [values_ref[2 * k + i].astype(jnp.float32) for i in range(2)]
        second = [turned_lanes(value, turn) for value in first]
        both = [jnp.concatenate(pieces, axis=1) for pieces in (first, second)]
        both = jnp.concatenate(both, axis=0).astype(jnp.bfloat16)
        total = total + jnp.dot(both, table_ref[k], preferred_element_type=jnp.float32)
    total = total * (1.0 / 32.0)
    for half in range(2):
        block = total[half * 72 : half * 72 + 72].astype(jnp.bfloat16)
        for y in range(4):
            out_ref[half * 4 + y] = block


def forward_x_call(values, table):
    return pl.pallas_call(
        forward_x_body,
        out_shape=jax.ShapeDtypeStruct((8, 72, 512), jnp.bfloat16),
        compiler_params=pltpu.CompilerParams(vmem_limit_bytes=VMEM),
        cost_estimate=pl.CostEstimate(flops=302000000, bytes_accessed=3000000, transcendentals=0),
        name="forward_x",
    )(values, table)


def modes_body(kernel_ref, spec_ref, out_ref):
    halves = [spec_ref[half, 0].astype(jnp.float32) for half in range(2)]
    spec = []
    for c in range(3):
        pieces = [half[c * 24 : c * 24 + 24] for half in halves]
        spec.append(jnp.concatenate(pieces, axis=0))
    for o in range(3):
        real = None
        imag = None
        for c in range(3):
            kr = kernel_ref[0, o, c, 0].astype(jnp.float32)
            ki = kernel_ref[1, o, c, 0].astype(jnp.float32)
            sr = spec[c][:, :NP]
            si = spec[c][:, NP:]
            r = kr * sr - ki * si
            i = kr * si + ki * sr
            real = r if real is None else real + r
            imag = i if imag is None else imag + i
        out_ref[0, o * 48 : o * 48 + 48, :] = real.astype(jnp.bfloat16)
        out_ref[0, 144 + o * 48 : 192 + o * 48, :] = imag.astype(jnp.bfloat16)


def modes_call(kernel, spec):
    return pl.pallas_call(
        modes_body,
        grid=(4,),
        in_specs=[
            pl.BlockSpec((2, 3, 3, 1, 48, NP), lambda j: (0, 0, 0, 0, j, 0)),
            pl.BlockSpec((2, 1, 72, 512), lambda j: (0, j, 0, 0)),
        ],
        out_specs=pl.BlockSpec((1, 288, NP), lambda j: ((j % 2) * 2 + j // 2, 0, 0)),
        out_shape=jax.ShapeDtypeStruct((4, 288, NP), jnp.bfloat16),
        compiler_params=pltpu.CompilerParams(vmem_limit_bytes=VMEM),
        cost_estimate=pl.CostEstimate(flops=3600000, bytes_accessed=2950000, transcendentals=0),
        name="modes",
    )(kernel, spec)


def inverse_x_body(values_ref, table_ref, out_ref):
    values = jnp.concatenate([values_ref[s] for s in (0, 2, 1, 3)], axis=1)

    def block(j, carry):
        total = jnp.dot(values, table_ref[j], preferred_element_type=jnp.float32)
        total = total * (1.0 / 32.0)
        real = (total[:144, :128] - total[144:, 128:]).astype(jnp.bfloat16)
        imag = (total[:144, 128:] + total[144:, :128]).astype(jnp.bfloat16)
        gx = j // 2
        place = (j % 2) * 4 + (gx % 2) * 2 + gx // 2
        for o in range(3):
            out_ref[place, 0:48, o * 128 : (o + 1) * 128] = real[o * 48 : (o + 1) * 48]
            out_ref[place, 48:96, o * 128 : (o + 1) * 128] = imag[o * 48 : (o + 1) * 48]
        return carry

    lax.fori_loop(0, 8, block, 0, unroll=True)


def inverse_x_call(values, table):
    return pl.pallas_call(
        inverse_x_body,
        out_shape=jax.ShapeDtypeStruct((8, 96, 384), jnp.bfloat16),
        compiler_params=pltpu.CompilerParams(vmem_limit_bytes=VMEM),
        cost_estimate=pl.CostEstimate(flops=1208000000, bytes_accessed=5400000, transcendentals=0),
        name="inverse_x",
    )(values, table)


def inverse_z_body(steps, me_ref, values_ref, table_ref, *out_refs):
    me = me_ref[0]
    values = values_ref[...]
    odd = (lax.broadcasted_iota(jnp.int32, (NQ, 384), 0) * (me // 2)) % 2
    scale = jnp.where(odd == 1, -1.0, 1.0) * (1.0 / math.sqrt(NZ))
    for k, out_ref in zip(steps, out_refs):
        total = jnp.dot(table_ref[me ^ k], values, preferred_element_type=jnp.float32)
        out_ref[...] = (total * scale).astype(out_ref.dtype)


def inverse_z_call(me, values, table, steps):
    block = pl.BlockSpec((NQ, 384), lambda j, s: (0, 0))
    return pl.pallas_call(
        functools.partial(inverse_z_body, steps),
        grid_spec=pltpu.PrefetchScalarGridSpec(
            num_scalar_prefetch=1,
            grid=(1,),
            in_specs=[
                pl.BlockSpec((NZ, 384), lambda j, s: (0, 0)),
                pl.BlockSpec((4, NQ, NZ), lambda j, s: (0, 0, 0)),
            ],
            out_specs=[block] * len(steps),
        ),
        out_shape=[jax.ShapeDtypeStruct((NQ, 384), jnp.bfloat16) for _ in steps],
        compiler_params=pltpu.CompilerParams(vmem_limit_bytes=VMEM),
        cost_estimate=pl.CostEstimate(flops=227000000, bytes_accessed=2000000, transcendentals=0),
        name="inverse_z_far" if steps[0] else "inverse_z_near",
    )(me, values, table)


def finish_body(core_ref, own_ref, far_own_ref, near_ref, far_near_ref, out_ref):
    own = own_ref[...].astype(jnp.float32) + far_own_ref[...].astype(jnp.float32)
    near = near_ref[...].astype(jnp.float32) + far_near_ref[...].astype(jnp.float32)
    first = core_ref[0] == 0
    left = jnp.where(first, own, near).astype(jnp.bfloat16)
    right = jnp.where(first, near, own).astype(jnp.bfloat16)
    for o in range(3):
        out_ref[o, 0, :, 0:128] = left[:, o * 128 : (o + 1) * 128]
        out_ref[o, 0, :, 128:256] = right[:, o * 128 : (o + 1) * 128]


def finish_call(core, own, far_own, near, far_near):
    block = pl.BlockSpec((NQ, 384), lambda j, s: (0, 0))
    return pl.pallas_call(
        finish_body,
        grid_spec=pltpu.PrefetchScalarGridSpec(
            num_scalar_prefetch=1,
            grid=(1,),
            in_specs=[block] * 4,
            out_specs=pl.BlockSpec((3, 1, NQ, NP), lambda j, s: (0, 0, 0, 0)),
        ),
        out_shape=jax.ShapeDtypeStruct((3, 1, NQ, NP), jnp.bfloat16),
        compiler_params=pltpu.CompilerParams(vmem_limit_bytes=VMEM),
        cost_estimate=pl.CostEstimate(flops=150000, bytes_accessed=900000, transcendentals=0),
        name="finish",
    )(core, own, far_own, near, far_near)


def exchange(values, axis):
    return lax.all_to_all(values, axis, split_axis=0, concat_axis=0, tiled=True)


def swap_cores(values):
    return lax.ppermute(values, "core", [(0, 1), (1, 0)])


def move_z(values, step, flip):
    def position(z, core):
        return (z % 8) * 4 + (z // 8) * 2 + core

    perm = []
    for z in range(16):
        for core in range(2):
            target = (z + (step if core == 0 else -step)) % 16
            perm.append((position(z, core), position(target, core ^ flip)))
    return lax.ppermute(values, ("z_lo", "z_hi", "core"), perm)


def per_device(wall, kernel):
    core = lax.axis_index("core")
    gz = (lax.axis_index("z_hi") * 2 + core).reshape(1).astype(jnp.int32)

    rows, z_table = pack_call(wall, jnp.asarray(forward_z_table()))
    rows = exchange(rows, ("z_lo", "z_hi"))
    other = swap_cores(rows)
    z_spectra = forward_z_call(gz, other, z_table, forward_z_call(gz, rows, z_table, None))
    z_spectra = exchange(z_spectra, ("gx_pair", "gx_in", "y"))
    spec = exchange(forward_x_call(z_spectra, jnp.asarray(forward_x_table())), ("gx_in", "y"))

    modes = exchange(modes_call(kernel, spec.reshape(2, 4, 72, 512)), ("gx_in", "gx_pair"))
    planes = exchange(inverse_x_call(modes, jnp.asarray(inverse_x_table())), ("core", "gx_in", "gx_pair"))
    planes = planes.reshape(NZ, 384)
    z_table = jnp.asarray(inverse_z_table())
    (to_far,) = inverse_z_call(gz, planes, z_table, (2,))
    (to_far_near,) = inverse_z_call(gz, planes, z_table, (3,))
    own, to_near = inverse_z_call(gz, planes, z_table, (0, 1))
    far_own = move_z(move_z(to_far, 4, 0), 4, 0)
    far_near = move_z(move_z(to_far_near, -4, 0), -4, 1)
    near = swap_cores(to_near)
    return finish_call(core.reshape(1).astype(jnp.int32), own, far_own, near, far_near)


def solution(mesh):
    fine = Mesh(
        mesh.devices.reshape(8, 4, 2, 2, 2, 2),
        ("z_lo", "y", "gx_pair", "gx_in", "z_hi", "core"),
    )
    gx, gz = ("gx_pair", "gx_in"), ("z_hi", "core")
    return jax.shard_map(
        per_device,
        mesh=fine,
        in_specs=(
            P(None, ("z_lo", "y") + gx, gz),
            P(None, None, None, ("z_lo", "y"), gz, gx),
        ),
        out_specs=P(None, ("z_lo", "y"), gz, gx),
        check_vma=False,
    )
```
